256 devices in a mesh: row: 32 (over z, x_lo, core), col: 8 (over y, x_hi).
Axes of the slice: x: 4 (x_hi: 2, x_lo: 2; x = x_hi * 2 + x_lo), y: 4, z: 8, core: 2. Of those that a mesh axis runs over, the one named last changes fastest.
Arguments:
- x_feat: bfloat16 [16384, 256], P('row', 'col')
- y_feat: bfloat16 [24576, 256], P('col', 'row')
- a_logits: float32 [16384], P('row')
- b_logits: float32 [24576], P('col')
Outputs:
- f_potential: float32 [16384], P('row')
- g_potential: float32 [24576], P('col')
- loss: float32 [], replicated
All inputs are finite; a program needn't handle non-finite values.
Results may differ from the reference program's by a relative error of at most 0.0003.
Values may be sent and summed in bfloat16 or wider, within the bound.
A program may use at most 64 MiB of HBM per device.

```python
import math
import jax
import jax.numpy as jnp
from jax import lax

F = 256
ITERS = 4
NS = 16384
NT = 24576


def feature_rows(key, count, width, spread):
    base = jnp.clip(jax.random.normal(key, (count, width), jnp.float32), -6.0, 6.0)
    factor = jnp.exp(jax.random.uniform(jax.random.fold_in(key, 1), (count, 1), jnp.float32) * math.log(spread))
    return (base * factor).astype(jnp.bfloat16)


def mass_logits(key, count, noise):
    ramp = math.log(3.0) * jnp.arange(count, dtype=jnp.float32) / max(count - 1, 1)
    return jax.random.normal(key, (count,), jnp.float32) * noise + ramp


def draw_x_feat(key, part):
    key = jax.random.fold_in(key, 11)
    return feature_rows(key, NS, F, 1.25)


def draw_y_feat(key, part):
    key = jax.random.fold_in(key, 23)
    return feature_rows(key, NT, F, 1.25)


def draw_a_logits(key, part):
    key = jax.random.fold_in(key, 37)
    return mass_logits(key, NS, 0.5)


def draw_b_logits(key, part):
    key = jax.random.fold_in(key, 41)
    return mass_logits(key, NT, 0.5)


def setup_inputs(seed: int = 0) -> dict:
    keys = jax.random.split(jax.random.key(seed), 5)
    return {
        "x_feat": draw_x_feat(jax.random.fold_in(keys[4], 71), 0),
        "y_feat": draw_y_feat(jax.random.fold_in(keys[4], 71), 0),
        "a_logits": draw_a_logits(jax.random.fold_in(keys[4], 71), 0),
        "b_logits": draw_b_logits(jax.random.fold_in(keys[4], 71), 0),
    }


epsilon = 0.05


def block_size(count):
    return 512 if count % 512 == 0 else count


def log_total(values):
    peak = jnp.max(values)
    return peak + jnp.log(jnp.sum(jnp.exp(values - peak)))


def tile_cost(x_part, x_sq, y_part, y_sq):
    inner = jnp.dot(x_part, y_part.T, precision=lax.Precision.HIGHEST)
    return (x_sq[:, None] + y_sq[None, :] - 2.0 * inner) / F


def reference(x_feat, y_feat, a_logits, b_logits):
    x_float = x_feat.astype(jnp.float32)
    y_float = y_feat.astype(jnp.float32)
    log_a = a_logits - log_total(a_logits)
    log_b = b_logits - log_total(b_logits)
    x_square = jnp.sum(x_float * x_float, axis=1)
    y_square = jnp.sum(y_float * y_float, axis=1)
    rows_block = block_size(NS)
    cols_block = block_size(NT)
    x_blocks = x_float.reshape(NS // rows_block, rows_block, F)
    xs_blocks = x_square.reshape(NS // rows_block, rows_block)
    y_blocks = y_float.reshape(NT // cols_block, cols_block, F)
    ys_blocks = y_square.reshape(NT // cols_block, cols_block)
    potential_g = jnp.zeros((NT,), jnp.float32)
    potential_f = jnp.zeros((NS,), jnp.float32)
    for step in range(ITERS):
        def row_update(pair):
            scores = log_b[None, :] + (potential_g[None, :] - tile_cost(pair[0], pair[1], y_float, y_square)) / epsilon
            peak = jnp.max(scores, axis=1)
            return -epsilon * (peak + jnp.log(jnp.sum(jnp.exp(scores - peak[:, None]), axis=1)))

        potential_f = lax.map(row_update, (x_blocks, xs_blocks)).reshape(NS)

        def col_update(pair):
            scores = log_a[:, None] + (potential_f[:, None] - tile_cost(x_float, x_square, pair[0], pair[1])) / epsilon
            peak = jnp.max(scores, axis=0)
            return -epsilon * (peak + jnp.log(jnp.sum(jnp.exp(scores - peak[None, :]), axis=0)))

        potential_g = lax.map(col_update, (y_blocks, ys_blocks)).reshape(NT)
    loss = jnp.sum(jnp.exp(log_a) * potential_f) + jnp.sum(jnp.exp(log_b) * potential_g)
    return potential_f, potential_g, loss
```

```python
import functools
import math

import jax
import jax.numpy as jnp
from jax import lax
from jax.experimental import pallas as pl
from jax.experimental.pallas import tpu as pltpu
from jax.sharding import PartitionSpec as P

ITERS = 4
EPS = 0.05
LN2 = math.log(2.0)
LOG2E = 1.0 / LN2
F = 256
SIZE = {"z": 8, "xl": 2, "c": 2, "y": 4, "xh": 2}
MESH = pl.DeviceIdType.MESH
ROWS, COLS = 1024, 1536
KT = COLS // 128


def coords():
    r = lax.axis_index("row")
    k = lax.axis_index("col")
    return {"z": r // 4, "xl": lax.rem(r // 2, 2), "c": lax.rem(r, 2), "y": k // 2, "xh": lax.rem(k, 2)}


def device(o):
    return ((o["z"] * 2 + o["xl"]) * 2 + o["c"], o["y"] * 2 + o["xh"])


def hops(o):
    z, y = o.get("z", 0), o.get("y", 0)
    return min(z, 8 - z) + min(y, 4 - y) + 2 * o.get("xh", 0) + o.get("xl", 0)


def offsets(names):
    out = [{}]
    for n in names:
        out = [{**o, n: d} for o in out for d in range(SIZE[n])]
    return sorted([o for o in out if any(o.values())], key=lambda o: -hops(o))


def at_offset(co, o):
    return {n: (lax.rem(co[n] + o[n], SIZE[n]) if o.get(n, 0) else co[n]) for n in co}


def send(src, dst, ssem, rsem, target):
    pltpu.make_async_remote_copy(
        src_ref=src, dst_ref=dst, send_sem=ssem, recv_sem=rsem, device_id=device(target), device_id_type=MESH
    ).start()


def drain(ref, sem):
    pltpu.make_async_copy(ref, ref, sem).wait()


def lse(x):
    peak = jnp.max(x, axis=0)
    return peak + jnp.log2(jnp.sum(jnp.exp2(x - peak[None]), axis=0))


def full_lse(x):
    peak = jnp.max(x, axis=(0, 1), keepdims=True)
    return peak + jnp.log2(jnp.sum(jnp.exp2(x - peak), axis=(0, 1), keepdims=True))


def kernel(
    xt, yt, a, b, f_out, g_out, loss_out,
    XT, Y8, YM, S, VB, UB, ALL_A, ALL_B, LA, LB, XSQ, YSQ, GM, GS, FX, GX, FL, GL, GH,
    ysem, xsem, asem, bsem, csem, local, fs, fr, gs, gr, ends,
):
    co = coords()
    row, col = device(co)
    zx = co["z"] * 2 + co["xl"]
    xy = (co["xh"] * 2 + co["xl"]) * 4 + co["y"]
    zc = co["z"] * 2 + co["c"]
    xy_peers = [at_offset(co, o) for o in offsets(["y", "xh", "xl"])]
    zc_peers = [at_offset(co, o) for o in offsets(["z", "c"])]
    zx_peers = [at_offset(co, o) for o in offsets(["z", "xl"])]
    row_peers = [at_offset(co, o) for o in offsets(["z", "xl", "c"])]
    col_peers = [at_offset(co, o) for o in offsets(["y", "xh"])]
    barrier_peers = row_peers + [at_offset(co, o) for o in offsets(["y", "xh", "xl"]) if o.get("y", 0) or o.get("xh", 0)]
    sibling = at_offset(co, {"c": 1})

    barrier = pltpu.get_barrier_semaphore()
    for t in barrier_peers:
        pl.semaphore_signal(barrier, inc=1, device_id=device(t), device_id_type=MESH)

    own_x = pltpu.make_async_copy(xt, XT.at[co["xl"] * 8 + col], local.at[0])
    own_x.start()
    half = pl.ds(pl.multiple_of(co["xl"] * COLS, 128), COLS)
    own_y = pltpu.make_async_copy(yt.at[:, half], Y8.at[co["c"], zx], local.at[1])
    own_y.start()
    ALL_A[row] = a[...]
    ALL_B[col] = b[...]
    pl.semaphore_wait(barrier, len(barrier_peers))

    for ty, tx in zip(zx_peers, xy_peers):
        part = pl.ds(pl.multiple_of(ty["xl"] * COLS, 128), COLS)
        send(yt.at[:, part], Y8.at[co["c"], zx], ysem.at[0], ysem.at[1], ty)
        send(xt, XT.at[co["xl"] * 8 + col], xsem.at[0], xsem.at[1], tx)
    for t in row_peers:
        send(ALL_A.at[row], ALL_A.at[row], asem.at[0], asem.at[1], t)
    for t in col_peers:
        send(ALL_B.at[col], ALL_B.at[col], bsem.at[0], bsem.at[1], t)

    own_x.wait()
    own_y.wait()
    drain(Y8.at[0, pl.ds(0, 15)], ysem.at[1])
    send(Y8.at[co["c"]], Y8.at[co["c"]], csem.at[0], csem.at[1], sibling)

    drain(ALL_A.at[pl.ds(0, 31)], asem.at[1])
    drain(ALL_B.at[pl.ds(0, 7)], bsem.at[1])
    whole_a = ALL_A[...].reshape(128, 128) * LOG2E
    log_a_norm = full_lse(whole_a)
    mine = jnp.concatenate([ALL_A[co["z"] * 4 + co["c"]], ALL_A[co["z"] * 4 + 2 + co["c"]]], axis=0)
    LA[...] = mine * LOG2E - log_a_norm
    whole_b = ALL_B[...].reshape(192, 128) * LOG2E
    log_b_norm = full_lse(whole_b)
    b_all = b[...]
    LB[...] = jnp.where(co["xl"] == 0, b_all[:KT], b_all[KT:]) * LOG2E - log_b_norm
    drain(XT.at[pl.ds(0, 15)], xsem.at[1])
    for p in range(8):
        x = XT[p // 4 * 8 : p // 4 * 8 + 8, :, pl.ds((p % 4) * 128, 128)].astype(jnp.float32).reshape(F, 128)
        XSQ[p : p + 1, :] = jnp.sum(x * x, axis=0, keepdims=True)
    drain(Y8.at[0], csem.at[1])

    def assemble(q, total):
        y = jnp.concatenate([Y8[0, q].astype(jnp.float32), Y8[1, q].astype(jnp.float32)], axis=0)
        YM[pl.ds(pl.multiple_of(q * 16, 16), 16), :] = y.astype(jnp.bfloat16)
        return total + y * y

    total = lax.fori_loop(0, 16, assemble, jnp.zeros((16, COLS), jnp.float32))
    total = jnp.sum(total, axis=0, keepdims=True)
    for k in range(KT):
        YSQ[k : k + 1, :] = total[:, k * 128 : (k + 1) * 128]

    scale = 2.0 / F / EPS * LOG2E
    for p in range(8):
        x = XT[p // 4 * 8 : p // 4 * 8 + 8, :, pl.ds((p % 4) * 128, 128)].reshape(F, 128)
        inner = lax.dot_general(x, YM[...], (((0,), (0,)), ((), ())), preferred_element_type=jnp.float32)
        S[pl.ds(p * 128, 128), :] = inner * scale

    def set_v(v):
        for k in range(KT):
            VB[:, k * 128 : (k + 1) * 128] = jnp.broadcast_to(v[k : k + 1, :], (8, 128))

    set_v(LB[...] - YSQ[...] * (LOG2E / F / EPS))

    def exchange(buf, me, peers, ssem, rsem):
        for t in peers:
            send(buf.at[me], buf.at[me], ssem, rsem, t)
        drain(buf.at[pl.ds(0, 15)], ssem)
        drain(buf.at[pl.ds(0, 15)], rsem)

    def iteration(t, _):
        def row_block(p, _):
            peaks, masses = [], []
            for r in range(16):
                at = pl.ds(pl.multiple_of(p * 128 + r * 8, 8), 8)
                tiles = [S[at, k * 128 : (k + 1) * 128] + VB[:, k * 128 : (k + 1) * 128] for k in range(KT)]
                peak = functools.reduce(jnp.maximum, tiles)
                peaks.append(peak)
                masses.append(functools.reduce(jnp.add, [jnp.exp2(s - peak) for s in tiles]))
            peak = jnp.concatenate(peaks, axis=0).T
            mass = jnp.concatenate(masses, axis=0).T
            top = jnp.max(peak, axis=0, keepdims=True)
            mass = jnp.sum(mass * jnp.exp2(peak - top), axis=0, keepdims=True)
            FX[t, xy, pl.ds(p, 1), :] = top + jnp.log2(mass)
            return 0

        lax.fori_loop(0, 8, row_block, 0)
        exchange(FX.at[t], xy, xy_peers, fs.at[t], fr.at[t])
        u = LA[...] - lse(FX[t])
        for p in range(8):
            UB[pl.ds(p * 128, 128), :] = jnp.broadcast_to(u[p : p + 1, :], (128, 128)).T

        def col_block(i, carry):
            peaks, masses = carry
            us = [UB[pl.ds(pl.multiple_of(i * 64 + r * 8, 8), 8), :] for r in range(8)]
            new_peaks, new_masses = [], []
            for k in range(KT):
                tiles = [
                    S[pl.ds(pl.multiple_of(i * 64 + r * 8, 8), 8), k * 128 : (k + 1) * 128] + us[r] for r in range(8)
                ]
                peak = functools.reduce(jnp.maximum, tiles + [peaks[k]])
                mass = functools.reduce(jnp.add, [jnp.exp2(s - peak) for s in tiles])
                new_masses.append(mass + masses[k] * jnp.exp2(peaks[k] - peak))
                new_peaks.append(peak)
            return new_peaks, new_masses

        start = [jnp.full((8, 128), -jnp.inf, jnp.float32)] * KT, [jnp.zeros((8, 128), jnp.float32)] * KT
        peaks, masses = lax.fori_loop(0, ROWS // 64, col_block, start)
        for k in range(KT):
            top = jnp.max(peaks[k], axis=0, keepdims=True)
            GM[k : k + 1, :] = top
            GS[k : k + 1, :] = jnp.sum(masses[k] * jnp.exp2(peaks[k] - top), axis=0, keepdims=True)
        GX[t, zc] = GM[...] + jnp.log2(GS[...])
        exchange(GX.at[t], zc, zc_peers, gs.at[t], gr.at[t])
        set_v(LB[...] - lse(GX[t]))
        return 0

    lax.fori_loop(0, ITERS, iteration, 0)
    last = ITERS - 1
    f = XSQ[...] * (1.0 / F) - lse(FX[last]) * (EPS * LN2)
    g = YSQ[...] * (1.0 / F) - lse(GX[last]) * (EPS * LN2)
    FL[zc] = jnp.exp2(LA[...]) * f
    GL[xy] = jnp.exp2(LB[...]) * g
    GH[co["xl"]] = g
    for t in xy_peers:
        send(GL.at[xy], GL.at[xy], ends.at[0], ends.at[1], t)
    send(GH.at[co["xl"]], GH.at[co["xl"]], ends.at[2], ends.at[3], at_offset(co, {"xl": 1}))
    for t in zc_peers:
        send(FL.at[zc], FL.at[zc], ends.at[4], ends.at[5], t)
    f_out[...] = jnp.where(co["xl"] == 0, f[:4], f[4:])
    drain(GH.at[0], ends.at[3])
    g_out[:KT] = GH[0]
    g_out[KT:] = GH[1]
    drain(GL.at[pl.ds(0, 15)], ends.at[1])
    drain(FL.at[pl.ds(0, 15)], ends.at[5])
    loss_out[...] = jnp.sum(jnp.sum(FL[...], axis=0), axis=(0, 1), keepdims=True) + jnp.sum(
        jnp.sum(GL[...], axis=0), axis=(0, 1), keepdims=True
    )
    drain(GL.at[pl.ds(0, 15)], ends.at[0])
    drain(GH.at[0], ends.at[2])
    drain(FL.at[pl.ds(0, 15)], ends.at[4])
    drain(Y8.at[0, pl.ds(0, 15)], ysem.at[0])
    drain(XT.at[pl.ds(0, 15)], xsem.at[0])
    drain(ALL_A.at[pl.ds(0, 31)], asem.at[0])
    drain(ALL_B.at[pl.ds(0, 7)], bsem.at[0])
    drain(Y8.at[0], csem.at[0])


def body(x_feat, y_feat, a_logits, b_logits):
    f32, bf16 = jnp.float32, jnp.bfloat16
    vmem = pl.BlockSpec(memory_space=pltpu.VMEM)
    hbm = pl.BlockSpec(memory_space=pl.ANY)
    dma = pltpu.SemaphoreType.DMA
    f, g, loss = pl.pallas_call(
        kernel,
        out_shape=(
            jax.ShapeDtypeStruct((4, 128), f32),
            jax.ShapeDtypeStruct((24, 128), f32),
            jax.ShapeDtypeStruct((1, 1), f32),
        ),
        in_specs=[hbm, hbm, vmem, vmem],
        out_specs=(vmem, vmem, vmem),
        scratch_shapes=[
            pltpu.VMEM((16, 32, 512), bf16),
            pltpu.VMEM((2, 16, 8, COLS), bf16),
            pltpu.VMEM((F, COLS), bf16),
            pltpu.VMEM((ROWS, COLS), f32),
            pltpu.VMEM((8, COLS), f32),
            pltpu.VMEM((ROWS, 128), f32),
            pltpu.VMEM((32, 4, 128), f32),
            pltpu.VMEM((8, 24, 128), f32),
            pltpu.VMEM((8, 128), f32),
            pltpu.VMEM((KT, 128), f32),
            pltpu.VMEM((8, 128), f32),
            pltpu.VMEM((KT, 128), f32),
            pltpu.VMEM((KT, 128), f32),
            pltpu.VMEM((KT, 128), f32),
            pltpu.VMEM((ITERS, 16, 8, 128), f32),
            pltpu.VMEM((ITERS, 16, KT, 128), f32),
            pltpu.VMEM((16, 8, 128), f32),
            pltpu.VMEM((16, KT, 128), f32),
            pltpu.VMEM((2, KT, 128), f32),
            dma((2,)),
            dma((2,)),
            dma((2,)),
            dma((2,)),
            dma((2,)),
            dma((2,)),
            dma((ITERS,)),
            dma((ITERS,)),
            dma((ITERS,)),
            dma((ITERS,)),
            dma((6,)),
        ],
        compiler_params=pltpu.CompilerParams(
            collective_id=0, has_side_effects=True, vmem_limit_bytes=40 * 1024 * 1024
        ),
        name="sinkhorn",
    )(x_feat.T, y_feat.T, a_logits.reshape(4, 128), b_logits.reshape(24, 128))
    return f.reshape(512), g.reshape(3072), loss.reshape(())


def solution(mesh):
    in_specs = (P("row", "col"), P("col", "row"), P("row"), P("col"))
    out_specs = (P("row"), P("col"), P())
    return jax.shard_map(body, mesh=mesh, in_specs=in_specs, out_specs=out_specs, check_vma=False)
```

```python
import functools
import math

import jax
import jax.numpy as jnp
from jax import lax
from jax.experimental import pallas as pl
from jax.experimental.pallas import tpu as pltpu
from jax.sharding import PartitionSpec as P

ITERS = 4
EPS = 0.05
LN2 = math.log(2.0)
LOG2E = 1.0 / LN2
F = 256
SIZE = {"z": 8, "xl": 2, "c": 2, "y": 4, "xh": 2}
MESH = pl.DeviceIdType.MESH
ROWS, COLS = 1024, 1536
KT = COLS // 128
CHUNKS = 2
CHUNK = COLS // CHUNKS


def coords():
    r = lax.axis_index("row")
    k = lax.axis_index("col")
    return {"z": r // 4, "xl": lax.rem(r // 2, 2), "c": lax.rem(r, 2), "y": k // 2, "xh": lax.rem(k, 2)}


def device(o):
    return ((o["z"] * 2 + o["xl"]) * 2 + o["c"], o["y"] * 2 + o["xh"])


def hops(o):
    z, y = o.get("z", 0), o.get("y", 0)
    return min(z, 8 - z) + min(y, 4 - y) + 2 * o.get("xh", 0) + o.get("xl", 0)


def offsets(names):
    out = [{}]
    for n in names:
        out = [{**o, n: d} for o in out for d in range(SIZE[n])]
    return sorted([o for o in out if any(o.values())], key=lambda o: -hops(o))


def at_offset(co, o):
    return {n: (lax.rem(co[n] + o[n], SIZE[n]) if o.get(n, 0) else co[n]) for n in co}


def send(src, dst, ssem, rsem, target):
    pltpu.make_async_remote_copy(
        src_ref=src, dst_ref=dst, send_sem=ssem, recv_sem=rsem, device_id=device(target), device_id_type=MESH
    ).start()


def drain(ref, sem):
    pltpu.make_async_copy(ref, ref, sem).wait()


def lse(x):
    peak = jnp.max(x, axis=0)
    return peak + jnp.log2(jnp.sum(jnp.exp2(x - peak[None]), axis=0))


def full_lse(x):
    peak = jnp.max(x, axis=(0, 1), keepdims=True)
    return peak + jnp.log2(jnp.sum(jnp.exp2(x - peak), axis=(0, 1), keepdims=True))


def kernel(
    xt, yt, a, b, f_out, g_out, loss_out,
    XT, XR, Y8, YM, S, VB, UB, ALL_A, ALL_B, LA, LB, XSQ, YSQ, GM, GS, FX, GX, FL, GL, GH,
    hsem, ysem, xsem, asem, bsem, csem, local, fs, fr, gs, gr, ends,
):
    co = coords()
    row, col = device(co)
    zx = co["z"] * 2 + co["xl"]
    xy = (co["xh"] * 2 + co["xl"]) * 4 + co["y"]
    zc = co["z"] * 2 + co["c"]
    xy_peers = [at_offset(co, o) for o in offsets(["y", "xh", "xl"])]
    zc_peers = [at_offset(co, o) for o in offsets(["z", "c"])]
    z_peers = [at_offset(co, o) for o in offsets(["z"])]
    across = at_offset(co, {"xl": 1})
    row_peers = [at_offset(co, o) for o in offsets(["z", "xl", "c"])]
    col_peers = [at_offset(co, o) for o in offsets(["y", "xh"])]
    barrier_peers = row_peers + [at_offset(co, o) for o in offsets(["y", "xh", "xl"]) if o.get("y", 0) or o.get("xh", 0)]
    sibling = at_offset(co, {"c": 1})

    barrier = pltpu.get_barrier_semaphore()
    for t in barrier_peers:
        pl.semaphore_signal(barrier, inc=1, device_id=device(t), device_id_type=MESH)

    def cut(xl, n):
        return yt.at[:, pl.ds(pl.multiple_of(xl * COLS + n * CHUNK, 128), CHUNK)]

    own = [
        pltpu.make_async_copy(a, ALL_A.at[row], local.at[0]),
        pltpu.make_async_copy(b, ALL_B.at[col], local.at[1]),
        pltpu.make_async_copy(xt, XT.at[co["xl"] * 8 + col], local.at[2]),
    ] + [pltpu.make_async_copy(cut(co["xl"], n), Y8.at[n, co["c"], zx], local.at[3 + n]) for n in range(CHUNKS)]
    for copy in own:
        copy.start()
    pl.semaphore_wait(barrier, len(barrier_peers))

    for n in range(CHUNKS):
        here = Y8.at[n, co["c"], zx]
        send(cut(across["xl"], n), here, hsem.at[0], hsem.at[1 + n], across)
    for n in range(CHUNKS):
        for t in z_peers:
            send(cut(co["xl"], n), Y8.at[n, co["c"], zx], ysem.at[0], ysem.at[1 + n], t)
    for t in xy_peers:
        send(xt, XT.at[co["xl"] * 8 + col], xsem.at[0], xsem.at[1], t)
    for copy in own:
        copy.wait()
    for t in row_peers:
        send(ALL_A.at[row], ALL_A.at[row], asem.at[0], asem.at[1], t)
    for t in col_peers:
        send(ALL_B.at[col], ALL_B.at[col], bsem.at[0], bsem.at[1], t)

    for n in range(CHUNKS):
        landed = Y8.at[n, co["c"], co["z"] * 2 + across["xl"]]
        drain(landed, hsem.at[1 + n])
        for t in z_peers:
            send(landed, landed, ysem.at[0], ysem.at[1 + n], t)

    drain(ALL_A.at[pl.ds(0, 31)], asem.at[1])
    drain(ALL_B.at[pl.ds(0, 7)], bsem.at[1])
    whole_a = ALL_A[...].reshape(128, 128) * LOG2E
    log_a_norm = full_lse(whole_a)
    mine = jnp.concatenate([ALL_A[co["z"] * 4 + co["c"]], ALL_A[co["z"] * 4 + 2 + co["c"]]], axis=0)
    LA[...] = mine * LOG2E - log_a_norm
    whole_b = ALL_B[...].reshape(192, 128) * LOG2E
    log_b_norm = full_lse(whole_b)
    b_all = ALL_B[col]
    LB[...] = jnp.where(co["xl"] == 0, b_all[:KT], b_all[KT:]) * LOG2E - log_b_norm
    drain(XT.at[pl.ds(0, 15)], xsem.at[1])
    for p in range(8):
        x = XT[p // 4 * 8 : p // 4 * 8 + 8, :, pl.ds((p % 4) * 128, 128)].reshape(F, 128)
        XR[p * 128 : (p + 1) * 128, :] = x.T
        x = x.astype(jnp.float32)
        XSQ[p : p + 1, :] = jnp.sum(x * x, axis=0, keepdims=True)

    scale = 2.0 / F / EPS * LOG2E

    def multiply(n):
        drain(Y8.at[n, 0], csem.at[1 + n])
        total = jnp.zeros((16, CHUNK), jnp.float32)
        for q in range(16):
            y = jnp.concatenate([Y8[n, 0, q].astype(jnp.float32), Y8[n, 1, q].astype(jnp.float32)], axis=0)
            YM[q * 16 : (q + 1) * 16, n * CHUNK : (n + 1) * CHUNK] = y.astype(jnp.bfloat16)
            total = total + y * y
        total = jnp.sum(total, axis=0, keepdims=True)
        for k in range(CHUNK // 128):
            at = n * (CHUNK // 128) + k
            YSQ[at : at + 1, :] = total[:, k * 128 : (k + 1) * 128]
        for p in range(8):
            inner = jnp.dot(
                XR[p * 128 : (p + 1) * 128, :],
                YM[:, n * CHUNK : (n + 1) * CHUNK],
                preferred_element_type=jnp.float32,
            )
            S[p * 128 : (p + 1) * 128, n * CHUNK : (n + 1) * CHUNK] = inner * scale

    for n in range(CHUNKS):
        drain(Y8.at[n, 0, pl.ds(0, 14)], ysem.at[1 + n])
        send(Y8.at[n, co["c"]], Y8.at[n, co["c"]], csem.at[0], csem.at[1 + n], sibling)
        if n:
            multiply(n - 1)
    multiply(CHUNKS - 1)

    def set_v(v):
        for k in range(KT):
            VB[:, k * 128 : (k + 1) * 128] = jnp.broadcast_to(v[k : k + 1, :], (8, 128))

    set_v(LB[...] - YSQ[...] * (LOG2E / F / EPS))

    def exchange(buf, me, peers, ssem, rsem):
        for t in peers:
            send(buf.at[me], buf.at[me], ssem, rsem, t)
        drain(buf.at[pl.ds(0, 15)], ssem)
        drain(buf.at[pl.ds(0, 15)], rsem)

    def iteration(t, _):
        def row_block(p, _):
            peaks, masses = [], []
            for r in range(16):
                at = pl.ds(pl.multiple_of(p * 128 + r * 8, 8), 8)
                tiles = [S[at, k * 128 : (k + 1) * 128] + VB[:, k * 128 : (k + 1) * 128] for k in range(KT)]
                peak = functools.reduce(jnp.maximum, tiles)
                peaks.append(peak)
                masses.append(functools.reduce(jnp.add, [jnp.exp2(s - peak) for s in tiles]))
            peak = jnp.concatenate(peaks, axis=0).T
            mass = jnp.concatenate(masses, axis=0).T
            top = jnp.max(peak, axis=0, keepdims=True)
            mass = jnp.sum(mass * jnp.exp2(peak - top), axis=0, keepdims=True)
            FX[t, xy, pl.ds(p, 1), :] = top + jnp.log2(mass)
            return 0

        lax.fori_loop(0, 8, row_block, 0, unroll=8)
        exchange(FX.at[t], xy, xy_peers, fs.at[t], fr.at[t])
        u = LA[...] - lse(FX[t])
        for p in range(8):
            UB[pl.ds(p * 128, 128), :] = jnp.broadcast_to(u[p : p + 1, :], (128, 128)).T

        def col_block(i, carry):
            peaks, masses = carry
            us = [UB[pl.ds(pl.multiple_of(i * 128 + r * 8, 8), 8), :] for r in range(16)]
            new_peaks, new_masses = [], []
            for k in range(KT):
                tiles = [
                    S[pl.ds(pl.multiple_of(i * 128 + r * 8, 8), 8), k * 128 : (k + 1) * 128] + us[r] for r in range(16)
                ]
                peak = functools.reduce(jnp.maximum, tiles + [peaks[k]])
                mass = functools.reduce(jnp.add, [jnp.exp2(s - peak) for s in tiles])
                new_masses.append(mass + masses[k] * jnp.exp2(peaks[k] - peak))
                new_peaks.append(peak)
            return new_peaks, new_masses

        start = [jnp.full((8, 128), -jnp.inf, jnp.float32)] * KT, [jnp.zeros((8, 128), jnp.float32)] * KT
        peaks, masses = lax.fori_loop(0, ROWS // 128, col_block, start, unroll=8)
        for k in range(KT):
            top = jnp.max(peaks[k], axis=0, keepdims=True)
            GM[k : k + 1, :] = top
            GS[k : k + 1, :] = jnp.sum(masses[k] * jnp.exp2(peaks[k] - top), axis=0, keepdims=True)
        GX[t, zc] = GM[...] + jnp.log2(GS[...])
        exchange(GX.at[t], zc, zc_peers, gs.at[t], gr.at[t])
        set_v(LB[...] - lse(GX[t]))
        return 0

    lax.fori_loop(0, ITERS, iteration, 0)
    last = ITERS - 1
    f = XSQ[...] * (1.0 / F) - lse(FX[last]) * (EPS * LN2)
    g = YSQ[...] * (1.0 / F) - lse(GX[last]) * (EPS * LN2)
    FL[zc] = jnp.exp2(LA[...]) * f
    GL[xy] = jnp.exp2(LB[...]) * g
    GH[co["xl"]] = g
    for t in xy_peers:
        send(GL.at[xy], GL.at[xy], ends.at[0], ends.at[1], t)
    send(GH.at[co["xl"]], GH.at[co["xl"]], ends.at[2], ends.at[3], across)
    for t in zc_peers:
        send(FL.at[zc], FL.at[zc], ends.at[4], ends.at[5], t)
    f_out[...] = jnp.where(co["xl"] == 0, f[:4], f[4:])
    drain(GH.at[0], ends.at[3])
    g_out[:KT] = GH[0]
    g_out[KT:] = GH[1]
    drain(GL.at[pl.ds(0, 15)], ends.at[1])
    drain(FL.at[pl.ds(0, 15)], ends.at[5])
    loss_out[...] = jnp.sum(jnp.sum(FL[...], axis=0), axis=(0, 1), keepdims=True) + jnp.sum(
        jnp.sum(GL[...], axis=0), axis=(0, 1), keepdims=True
    )
    drain(GL.at[pl.ds(0, 15)], ends.at[0])
    drain(GH.at[0], ends.at[2])
    drain(FL.at[pl.ds(0, 15)], ends.at[4])
    drain(Y8.at[:, 0, 0], hsem.at[0])
    drain(Y8.at[:, 0, pl.ds(0, 14)], ysem.at[0])
    drain(XT.at[pl.ds(0, 15)], xsem.at[0])
    drain(ALL_A.at[pl.ds(0, 31)], asem.at[0])
    drain(ALL_B.at[pl.ds(0, 7)], bsem.at[0])
    drain(Y8.at[:, 0], csem.at[0])


def body(x_feat, y_feat, a_logits, b_logits):
    f32, bf16 = jnp.float32, jnp.bfloat16
    vmem = pl.BlockSpec(memory_space=pltpu.VMEM)
    hbm = pl.BlockSpec(memory_space=pltpu.HBM)
    dma = pltpu.SemaphoreType.DMA
    f, g, loss = pl.pallas_call(
        kernel,
        out_shape=(
            jax.ShapeDtypeStruct((4, 128), f32),
            jax.ShapeDtypeStruct((24, 128), f32),
            jax.ShapeDtypeStruct((1, 1), f32),
        ),
        in_specs=[hbm, hbm, hbm, hbm],
        out_specs=(vmem, vmem, vmem),
        scratch_shapes=[
            pltpu.VMEM((16, 32, 512), bf16),
            pltpu.VMEM((ROWS, F), bf16),
            pltpu.VMEM((CHUNKS, 2, 16, 8, CHUNK), bf16),
            pltpu.VMEM((F, COLS), bf16),
            pltpu.VMEM((ROWS, COLS), f32),
            pltpu.VMEM((8, COLS), f32),
            pltpu.VMEM((ROWS, 128), f32),
            pltpu.VMEM((32, 4, 128), f32),
            pltpu.VMEM((8, 24, 128), f32),
            pltpu.VMEM((8, 128), f32),
            pltpu.VMEM((KT, 128), f32),
            pltpu.VMEM((8, 128), f32),
            pltpu.VMEM((KT, 128), f32),
            pltpu.VMEM((KT, 128), f32),
            pltpu.VMEM((KT, 128), f32),
            pltpu.VMEM((ITERS, 16, 8, 128), f32),
            pltpu.VMEM((ITERS, 16, KT, 128), f32),
            pltpu.VMEM((16, 8, 128), f32),
            pltpu.VMEM((16, KT, 128), f32),
            pltpu.VMEM((2, KT, 128), f32),
            dma((1 + CHUNKS,)),
            dma((1 + CHUNKS,)),
            dma((2,)),
            dma((2,)),
            dma((2,)),
            dma((1 + CHUNKS,)),
            dma((3 + CHUNKS,)),
            dma((ITERS,)),
            dma((ITERS,)),
            dma((ITERS,)),
            dma((ITERS,)),
            dma((6,)),
        ],
        compiler_params=pltpu.CompilerParams(
            collective_id=0, has_side_effects=True, vmem_limit_bytes=63 * 1024 * 1024
        ),
        name="sinkhorn",
    )(x_feat.T, y_feat.T, a_logits.reshape(4, 128), b_logits.reshape(24, 128))
    return f.reshape(512), g.reshape(3072), loss.reshape(())


def solution(mesh):
    in_specs = (P("row", "col"), P("col", "row"), P("row"), P("col"))
    out_specs = (P("row"), P("col"), P())
    return jax.shard_map(body, mesh=mesh, in_specs=in_specs, out_specs=out_specs, check_vma=False)
```

```python
import functools
import math

import jax
import jax.numpy as jnp
from jax import lax
from jax.experimental import pallas as pl
from jax.experimental.pallas import tpu as pltpu
from jax.sharding import PartitionSpec as P

ITERS = 4
EPS = 0.05
LN2 = math.log(2.0)
LOG2E = 1.0 / LN2
F = 256
SIZE = {"z": 8, "xl": 2, "c": 2, "y": 4, "xh": 2}
MESH = pl.DeviceIdType.MESH
ROWS, COLS = 2048, 1536
PARTS = 4
KT = COLS // 128
CHUNKS = 3
CHUNK = COLS // CHUNKS
GROUP = 4


def coords():
    r = lax.axis_index("row")
    k = lax.axis_index("col")
    return {"z": r // 4, "xl": lax.rem(r // 2, 2), "c": lax.rem(r, 2), "y": k // 2, "xh": lax.rem(k, 2)}


def device(o):
    return ((o["z"] * 2 + o["xl"]) * 2 + o["c"], o["y"] * 2 + o["xh"])


def hops(o):
    z, y = o.get("z", 0), o.get("y", 0)
    return min(z, 8 - z) + min(y, 4 - y) + 2 * o.get("xh", 0) + o.get("xl", 0)


def offsets(names):
    out = [{}]
    for n in names:
        out = [{**o, n: d} for o in out for d in range(SIZE[n])]
    return sorted([o for o in out if any(o.values())], key=lambda o: -hops(o))


def at_offset(co, o, c):
    return {n: (lax.rem(co[n] + o[n], SIZE[n]) if o.get(n, 0) else co[n]) for n in co} | {"c": c}


def send(src, dst, ssem, rsem, target):
    pltpu.make_async_remote_copy(
        src_ref=src, dst_ref=dst, send_sem=ssem, recv_sem=rsem, device_id=device(target), device_id_type=MESH
    ).start()


def drain(ref, sem):
    pltpu.make_async_copy(ref, ref, sem).wait()


def lse(x):
    peak = jnp.max(x, axis=0)
    return peak + jnp.log2(jnp.sum(jnp.exp2(x - peak[None]), axis=0))


def full_lse(x):
    peak = jnp.max(x, axis=(0, 1), keepdims=True)
    return peak + jnp.log2(jnp.sum(jnp.exp2(x - peak), axis=(0, 1), keepdims=True))


def kernel(
    xt, yt, a, b, f_out, g_out, loss_out,
    XT, XR, Y8, YM, S, VB, UB, AA, OWN_B, NA, NB, LA, LB, LBN, XSQ, YSQ, GM, GS, FX, GX, FL, GL, GH, FO, LO,
    hsem, ysem, xsem, asem, nsem, local, fs, fr, gs, gr, ends,
):
    co = coords()
    row, col = device(co)
    c = co["c"]
    xy = (co["xh"] * 2 + co["xl"]) * 4 + co["y"]
    zed = co["z"]
    xy_offsets = offsets(["y", "xh", "xl"])
    z_offsets = offsets(["z"])
    xy_peers = [at_offset(co, o, 1) for o in xy_offsets]
    z_peers = [at_offset(co, o, 1) for o in z_offsets]
    across = at_offset(co, {"xl": 1}, 1)
    sibling = at_offset(co, {}, 1 - c)
    worker = c == 1
    helper = c == 0

    barrier = pltpu.get_barrier_semaphore()

    def greet(t):
        pl.semaphore_signal(barrier, inc=1, device_id=device(t), device_id_type=MESH)

    @pl.when(worker)
    def _():
        for o in xy_offsets + z_offsets:
            greet(at_offset(co, o, 0))
            greet(at_offset(co, o, 1))
        greet(sibling)

    @pl.when(helper)
    def _():
        greet(sibling)

    def cut(xl, n):
        return yt.at[:, pl.ds(pl.multiple_of(xl * COLS + n * CHUNK, 128), CHUNK)]

    own = [
        pltpu.make_async_copy(xt, XT.at[row % 4 * 8 + col], local.at[0]),
        pltpu.make_async_copy(a, AA.at[row % 4], local.at[1]),
        pltpu.make_async_copy(b, OWN_B, local.at[2]),
    ] + [pltpu.make_async_copy(cut(co["xl"], n), Y8.at[n, row], local.at[3 + n]) for n in range(CHUNKS)]

    @pl.when(worker)
    def _():
        for copy in own:
            copy.start()

    pl.semaphore_wait(barrier, len(xy_offsets) + len(z_offsets) + 1)

    for n in range(CHUNKS):
        send(cut(across["xl"], n), Y8.at[n, row], hsem.at[0], hsem.at[1 + n], across)
    for n in range(CHUNKS):
        for t in z_peers:
            send(cut(co["xl"], n), Y8.at[n, row], ysem.at[0], ysem.at[1 + n], t)
    for t in xy_peers:
        send(xt, XT.at[row % 4 * 8 + col], xsem.at[0], xsem.at[1], t)
    send(a, AA.at[row % 4], asem.at[0], asem.at[1], across)

    @pl.when(helper)
    def _():
        for n in range(CHUNKS):
            send(cut(co["xl"], n), Y8.at[n, row], ysem.at[0], ysem.at[1 + n], sibling)
        send(xt, XT.at[row % 4 * 8 + col], xsem.at[0], xsem.at[1], sibling)
        send(a, AA.at[row % 4], asem.at[0], asem.at[1], sibling)
        drain(Y8.at[0, pl.ds(0, CHUNKS)], hsem.at[0])
        drain(Y8.at[0, pl.ds(0, CHUNKS * 8)], ysem.at[0])
        drain(XT.at[pl.ds(0, 16)], xsem.at[0])
        drain(AA.at[pl.ds(0, 2)], asem.at[0])
        drain(FO, ends.at[5])
        drain(GH, ends.at[7])
        drain(LO, ends.at[9])
        f_out[...] = FO[...]
        g_out[:KT] = GH[0]
        g_out[KT:] = GH[1]
        loss_out[...] = LO[0:1, 0:1]

    @pl.when(worker)
    def _():
        work(
            co, row, col, xy, zed, xy_peers, z_peers, across, sibling, own, f_out, g_out, loss_out,
            XT, XR, Y8, YM, S, VB, UB, AA, OWN_B, NA, NB, LA, LB, LBN, XSQ, YSQ, GM, GS, FX, GX, FL, GL, GH, FO, LO,
            hsem, ysem, xsem, asem, nsem, fs, fr, gs, gr, ends,
        )


def work(
    co, row, col, xy, zed, xy_peers, z_peers, across, sibling, own, f_out, g_out, loss_out,
    XT, XR, Y8, YM, S, VB, UB, AA, OWN_B, NA, NB, LA, LB, LBN, XSQ, YSQ, GM, GS, FX, GX, FL, GL, GH, FO, LO,
    hsem, ysem, xsem, asem, nsem, fs, fr, gs, gr, ends,
):
    other = co["z"] * 4 + across["xl"] * 2
    for n in range(CHUNKS):
        landed = Y8.at[n, pl.ds(other, 2)]
        drain(landed, hsem.at[1 + n])
        for t in z_peers:
            send(landed, landed, ysem.at[0], ysem.at[1 + n], t)

    for copy in own:
        copy.wait()
    own_b = jnp.where(co["xl"] == 0, OWN_B[:KT], OWN_B[KT:]) * LOG2E
    LB[...] = own_b
    NB[xy] = jnp.broadcast_to(full_lse(own_b), (1, 128))
    for t in xy_peers:
        send(NB.at[xy], NB.at[xy], nsem.at[0], nsem.at[1], t)
    drain(AA.at[pl.ds(0, 3)], asem.at[1])
    whole_a = AA[...].reshape(16, 128) * LOG2E
    LA[...] = whole_a
    NA[zed] = jnp.broadcast_to(full_lse(whole_a), (1, 128))
    for t in z_peers:
        send(NA.at[zed], NA.at[zed], nsem.at[2], nsem.at[3], t)

    drain(XT.at[pl.ds(0, 31)], xsem.at[1])
    for p in range(16):
        x = XT[p // 4 * 8 : p // 4 * 8 + 8, :, pl.ds((p % 4) * 128, 128)].reshape(F, 128)
        XR[p * 128 : (p + 1) * 128, :] = x.T
        x = x.astype(jnp.float32)
        XSQ[p : p + 1, :] = jnp.sum(x * x, axis=0, keepdims=True)

    def set_v(v, first, count):
        for k in range(count):
            at = first + k
            VB[:, at * 128 : (at + 1) * 128] = jnp.broadcast_to(v[k : k + 1, :], (8, 128))

    scale = 2.0 / F / EPS * LOG2E
    tiles_in = CHUNK // 128
    for n in range(CHUNKS):
        drain(Y8.at[n, pl.ds(0, 29)], ysem.at[1 + n])
        span = slice(n * CHUNK, (n + 1) * CHUNK)
        total = jnp.zeros((16, CHUNK), jnp.float32)
        for q in range(16):
            y = jnp.concatenate(
                [Y8[n, 2 * q].astype(jnp.float32), Y8[n, 2 * q + 1].astype(jnp.float32)], axis=0
            )
            YM[q * 16 : (q + 1) * 16, span] = y.astype(jnp.bfloat16)
            total = total + y * y
        total = jnp.sum(total, axis=0, keepdims=True)
        for k in range(tiles_in):
            at = n * tiles_in + k
            YSQ[at : at + 1, :] = total[:, k * 128 : (k + 1) * 128]
        mine = slice(n * tiles_in, (n + 1) * tiles_in)
        set_v(LB[mine] - YSQ[mine] * (LOG2E / F / EPS), n * tiles_in, tiles_in)

        def multiply(p, _):
            at = pl.ds(pl.multiple_of(p * 128, 128), 128)
            inner = jnp.dot(XR[at, :], YM[:, span], preferred_element_type=jnp.float32)
            S[at, span] = inner * scale
            return 0

        lax.fori_loop(0, 16, multiply, 0, unroll=4)

    def f_pass(t):
        def part(h, _):
            for q in range(4):
                peaks, masses = [], []
                for r in range(16):
                    at = pl.ds(pl.multiple_of(h * 512 + q * 128 + r * 8, 8), 8)
                    tiles = [S[at, k * 128 : (k + 1) * 128] + VB[:, k * 128 : (k + 1) * 128] for k in range(KT)]
                    peak = functools.reduce(jnp.maximum, tiles)
                    peaks.append(peak)
                    masses.append(functools.reduce(jnp.add, [jnp.exp2(s - peak) for s in tiles]))
                peak = jnp.concatenate(peaks, axis=0).T
                mass = jnp.concatenate(masses, axis=0).T
                top = jnp.max(peak, axis=0, keepdims=True)
                mass = jnp.sum(mass * jnp.exp2(peak - top), axis=0, keepdims=True)
                FX[t, h, xy, q : q + 1, :] = top + jnp.log2(mass)
            for peer in xy_peers:
                send(FX.at[t, h, xy], FX.at[t, h, xy], fs.at[t], fr.at[t, h], peer)
            return 0

        lax.fori_loop(0, PARTS, part, 0)

    def g_pass(t):
        def part(h, _):
            drain(FX.at[t, h, pl.ds(0, 15)], fr.at[t, h])
            rows = pl.ds(pl.multiple_of(h * 4, 4), 4)
            u = LA[rows, :] - (lse(FX[t, h]) - jnp.where(t == 0, LBN[...], 0.0))
            for q in range(4):
                UB[q * 128 : (q + 1) * 128, :] = jnp.broadcast_to(u[q : q + 1, :], (128, 128)).T
            for k0 in range(0, KT, GROUP):
                span = slice(k0 * 128, (k0 + GROUP) * 128)
                peaks = [GM[:, k * 128 : (k + 1) * 128] for k in range(k0, k0 + GROUP)]
                masses = [GS[:, k * 128 : (k + 1) * 128] for k in range(k0, k0 + GROUP)]
                for q in range(4):
                    us = [UB[q * 128 + r * 8 : q * 128 + r * 8 + 8, :] for r in range(16)]
                    for k in range(GROUP):
                        lanes = slice((k0 + k) * 128, (k0 + k + 1) * 128)
                        tiles = [
                            S[pl.ds(pl.multiple_of(h * 512 + q * 128 + r * 8, 8), 8), lanes] + us[r]
                            for r in range(16)
                        ]
                        peak = functools.reduce(jnp.maximum, tiles + [peaks[k]])
                        mass = functools.reduce(jnp.add, [jnp.exp2(s - peak) for s in tiles])
                        masses[k] = mass + masses[k] * jnp.exp2(peaks[k] - peak)
                        peaks[k] = peak
                for k in range(GROUP):
                    lanes = slice((k0 + k) * 128, (k0 + k + 1) * 128)
                    GM[:, lanes] = peaks[k]
                    GS[:, lanes] = masses[k]
            return 0

        GM[...] = jnp.full(GM.shape, -jnp.inf, jnp.float32)
        GS[...] = jnp.zeros(GS.shape, jnp.float32)
        lax.fori_loop(0, PARTS, part, 0)
        for k in range(KT):
            lanes = slice(k * 128, (k + 1) * 128)
            peak = GM[:, lanes]
            top = jnp.max(peak, axis=0, keepdims=True)
            mass = jnp.sum(GS[:, lanes] * jnp.exp2(peak - top), axis=0, keepdims=True)
            GX[t, zed, k : k + 1, :] = top + jnp.log2(mass)
        for peer in z_peers:
            send(GX.at[t, zed], GX.at[t, zed], gs.at[t], gr.at[t], peer)
        drain(GX.at[t, pl.ds(0, 7)], gr.at[t])

    f_pass(0)
    drain(NB.at[pl.ds(0, 15)], nsem.at[1])
    drain(NA.at[pl.ds(0, 7)], nsem.at[3])
    log_b_norm = lse(NB[...])
    log_a_norm = lse(NA[...])
    LB[...] = LB[...] - log_b_norm
    LA[...] = LA[...] - log_a_norm
    LBN[...] = log_b_norm

    def iteration(t, _):
        g_pass(t)

        @pl.when(t < ITERS - 1)
        def _():
            set_v(LB[...] - lse(GX[t]), 0, KT)
            f_pass(t + 1)

        return 0

    lax.fori_loop(0, ITERS, iteration, 0)
    last = ITERS - 1
    g = YSQ[...] * (1.0 / F) - lse(GX[last]) * (EPS * LN2)
    GL[xy] = jnp.sum(jnp.exp2(LB[...]) * g, axis=0, keepdims=True)
    GH[co["xl"]] = g
    for t in xy_peers:
        send(GL.at[xy], GL.at[xy], ends.at[0], ends.at[1], t)
    send(GH.at[co["xl"]], GH.at[co["xl"]], ends.at[2], ends.at[3], across)
    lam = jnp.concatenate([lse(FX[last, h]) for h in range(PARTS)], axis=0)
    f = XSQ[...] * (1.0 / F) - lam * (EPS * LN2)
    FL[zed] = jnp.sum(jnp.exp2(LA[...]) * f, axis=0, keepdims=True)
    for t in z_peers:
        send(FL.at[zed], FL.at[zed], ends.at[10], ends.at[11], t)
    FO[...] = jnp.where(co["xl"] == 0, f[0:4], f[8:12])
    send(FO, FO, ends.at[4], ends.at[5], sibling)
    f_out[...] = jnp.where(co["xl"] == 0, f[4:8], f[12:16])
    drain(GH.at[0], ends.at[3])
    send(GH, GH, ends.at[6], ends.at[7], sibling)
    g_out[:KT] = GH[0]
    g_out[KT:] = GH[1]
    drain(FL.at[pl.ds(0, 7)], ends.at[11])
    drain(GL.at[pl.ds(0, 15)], ends.at[1])
    loss = jnp.sum(jnp.sum(FL[...], axis=0), axis=(0, 1), keepdims=True) + jnp.sum(
        jnp.sum(GL[...], axis=0), axis=(0, 1), keepdims=True
    )
    LO[...] = jnp.broadcast_to(loss, (1, 128))
    send(LO, LO, ends.at[8], ends.at[9], sibling)
    loss_out[...] = loss

    drain(GL.at[pl.ds(0, 15)], ends.at[0])
    drain(GH.at[0], ends.at[2])
    drain(FO, ends.at[4])
    drain(GH, ends.at[6])
    drain(LO, ends.at[8])
    drain(FL.at[pl.ds(0, 7)], ends.at[10])
    for t in range(ITERS):
        drain(FX.at[t, :, pl.ds(0, 15)], fs.at[t])
        drain(GX.at[t, pl.ds(0, 7)], gs.at[t])
    drain(NB.at[pl.ds(0, 15)], nsem.at[0])
    drain(NA.at[pl.ds(0, 7)], nsem.at[2])
    drain(Y8.at[0, pl.ds(0, CHUNKS)], hsem.at[0])
    drain(Y8.at[:, pl.ds(0, 21)], ysem.at[0])
    drain(XT.at[pl.ds(0, 15)], xsem.at[0])
    drain(AA.at[0], asem.at[0])


def body(x_feat, y_feat, a_logits, b_logits):
    f32, bf16 = jnp.float32, jnp.bfloat16
    vmem = pl.BlockSpec(memory_space=pltpu.VMEM)
    hbm = pl.BlockSpec(memory_space=pltpu.HBM)
    dma = pltpu.SemaphoreType.DMA
    f, g, loss = pl.pallas_call(
        kernel,
        out_shape=(
            jax.ShapeDtypeStruct((4, 128), f32),
            jax.ShapeDtypeStruct((24, 128), f32),
            jax.ShapeDtypeStruct((1, 1), f32),
        ),
        in_specs=[hbm, hbm, hbm, hbm],
        out_specs=(vmem, vmem, vmem),
        scratch_shapes=[
            pltpu.VMEM((32, 32, 512), bf16),
            pltpu.VMEM((ROWS, F), bf16),
            pltpu.VMEM((CHUNKS, 32, 8, CHUNK), bf16),
            pltpu.VMEM((F, COLS), bf16),
            pltpu.VMEM((ROWS, COLS), f32),
            pltpu.VMEM((8, COLS), f32),
            pltpu.VMEM((512, 128), f32),
            pltpu.VMEM((4, 4, 128), f32),
            pltpu.VMEM((24, 128), f32),
            pltpu.VMEM((8, 1, 128), f32),
            pltpu.VMEM((16, 1, 128), f32),
            pltpu.VMEM((16, 128), f32),
            pltpu.VMEM((KT, 128), f32),
            pltpu.VMEM((1, 128), f32),
            pltpu.VMEM((16, 128), f32),
            pltpu.VMEM((KT, 128), f32),
            pltpu.VMEM((8, COLS), f32),
            pltpu.VMEM((8, COLS), f32),
            pltpu.VMEM((ITERS, PARTS, 16, 4, 128), f32),
            pltpu.VMEM((ITERS, 8, KT, 128), f32),
            pltpu.VMEM((8, 1, 128), f32),
            pltpu.VMEM((16, 1, 128), f32),
            pltpu.VMEM((2, KT, 128), f32),
            pltpu.VMEM((4, 128), f32),
            pltpu.VMEM((1, 128), f32),
            dma((1 + CHUNKS,)),
            dma((1 + CHUNKS,)),
            dma((2,)),
            dma((2,)),
            dma((4,)),
            dma((3 + CHUNKS,)),
            dma((ITERS,)),
            dma((ITERS, PARTS)),
            dma((ITERS,)),
            dma((ITERS,)),
            dma((12,)),
        ],
        compiler_params=pltpu.CompilerParams(
            collective_id=0, has_side_effects=True, vmem_limit_bytes=63 * 1024 * 1024
        ),
        name="sinkhorn",
    )(x_feat.T, y_feat.T, a_logits.reshape(4, 128), b_logits.reshape(24, 128))
    return f.reshape(512), g.reshape(3072), loss.reshape(())


def solution(mesh):
    in_specs = (P("row", "col"), P("col", "row"), P("row"), P("col"))
    out_specs = (P("row"), P("col"), P())
    return jax.shard_map(body, mesh=mesh, in_specs=in_specs, out_specs=out_specs, check_vma=False)
```

```python
import functools
import math

import jax
import jax.numpy as jnp
from jax import lax
from jax.experimental import pallas as pl
from jax.experimental.pallas import tpu as pltpu
from jax.sharding import PartitionSpec as P

ITERS = 4
EPS = 0.05
LN2 = math.log(2.0)
LOG2E = 1.0 / LN2
F = 256
SIZE = {"z": 8, "xl": 2, "c": 2, "y": 4, "xh": 2}
MESH = pl.DeviceIdType.MESH
ROWS, COLS = 2048, 1536
PARTS = 4
KT = COLS // 128
CHUNKS = 3
CHUNK = COLS // CHUNKS
GROUP = 4


def coords():
    r = lax.axis_index("row")
    k = lax.axis_index("col")
    return {"z": r // 4, "xl": lax.rem(r // 2, 2), "c": lax.rem(r, 2), "y": k // 2, "xh": lax.rem(k, 2)}


def device(o):
    return ((o["z"] * 2 + o["xl"]) * 2 + o["c"], o["y"] * 2 + o["xh"])


def hops(o):
    z, y = o.get("z", 0), o.get("y", 0)
    return min(z, 8 - z) + min(y, 4 - y) + 2 * o.get("xh", 0) + o.get("xl", 0)


def offsets(names):
    out = [{}]
    for n in names:
        out = [{**o, n: d} for o in out for d in range(SIZE[n])]
    return sorted([o for o in out if any(o.values())], key=lambda o: -hops(o))


def at_offset(co, o, c):
    return {n: (lax.rem(co[n] + o[n], SIZE[n]) if o.get(n, 0) else co[n]) for n in co} | {"c": c}


def send(src, dst, ssem, rsem, target):
    pltpu.make_async_remote_copy(
        src_ref=src, dst_ref=dst, send_sem=ssem, recv_sem=rsem, device_id=device(target), device_id_type=MESH
    ).start()


def drain(ref, sem):
    pltpu.make_async_copy(ref, ref, sem).wait()


def lse(x):
    peak = jnp.max(x, axis=0)
    return peak + jnp.log2(jnp.sum(jnp.exp2(x - peak[None]), axis=0))


def tree(op, xs):
    while len(xs) > 1:
        xs = [op(xs[i], xs[i + 1]) if i + 1 < len(xs) else xs[i] for i in range(0, len(xs), 2)]
    return xs[0]


def full_lse(x):
    peak = jnp.max(x, axis=(0, 1), keepdims=True)
    return peak + jnp.log2(jnp.sum(jnp.exp2(x - peak), axis=(0, 1), keepdims=True))


def kernel(
    fast, xt, yt, a, b, f_out, g_out, loss_out,
    XT, XR, Y8, YM, S, VB, UB, ZB, AA, OWN_B, NA, NB, LA, LB, LBN, XSQ, YSQ, GM, GS, FX, GX, FL, GL, GH, FO, LO, FP, FM, LAM, BADR, BADC,
    hsem, ysem, xsem, asem, nsem, local, fs, fr, gs, gr, ends,
):
    co = coords()
    row, col = device(co)
    c = co["c"]
    xy = (co["xh"] * 2 + co["xl"]) * 4 + co["y"]
    zed = co["z"]
    xy_offsets = offsets(["y", "xh", "xl"])
    z_offsets = offsets(["z"])
    xy_peers = [at_offset(co, o, 1) for o in xy_offsets]
    z_peers = [at_offset(co, o, 1) for o in z_offsets]
    across = at_offset(co, {"xl": 1}, 1)
    sibling = at_offset(co, {}, 1 - c)
    worker = c == 1
    helper = c == 0

    barrier = pltpu.get_barrier_semaphore()

    def greet(t):
        pl.semaphore_signal(barrier, inc=1, device_id=device(t), device_id_type=MESH)

    @pl.when(worker)
    def _():
        for o in xy_offsets + z_offsets:
            greet(at_offset(co, o, 0))
            greet(at_offset(co, o, 1))
        greet(sibling)

    @pl.when(helper)
    def _():
        greet(sibling)

    def cut(xl, n):
        return yt.at[:, pl.ds(pl.multiple_of(xl * COLS + n * CHUNK, 128), CHUNK)]

    own = [
        pltpu.make_async_copy(xt, XT.at[row % 4 * 8 + col], local.at[0]),
        pltpu.make_async_copy(a, AA.at[row % 4], local.at[1]),
        pltpu.make_async_copy(b, OWN_B, local.at[2]),
    ] + [pltpu.make_async_copy(cut(co["xl"], n), Y8.at[n, row], local.at[3 + n]) for n in range(CHUNKS)]

    @pl.when(worker)
    def _():
        for copy in own:
            copy.start()

    pl.semaphore_wait(barrier, len(xy_offsets) + len(z_offsets) + 1)

    for n in range(CHUNKS):
        send(cut(across["xl"], n), Y8.at[n, row], hsem.at[0], hsem.at[1 + n], across)
    for n in range(CHUNKS):
        for t in z_peers:
            send(cut(co["xl"], n), Y8.at[n, row], ysem.at[0], ysem.at[1 + n], t)
    for t in xy_peers:
        send(xt, XT.at[row % 4 * 8 + col], xsem.at[0], xsem.at[1], t)
    send(a, AA.at[row % 4], asem.at[0], asem.at[1], across)

    @pl.when(helper)
    def _():
        for n in range(CHUNKS):
            send(cut(co["xl"], n), Y8.at[n, row], ysem.at[0], ysem.at[1 + n], sibling)
        send(xt, XT.at[row % 4 * 8 + col], xsem.at[0], xsem.at[1], sibling)
        send(a, AA.at[row % 4], asem.at[0], asem.at[1], sibling)
        drain(Y8.at[0, pl.ds(0, CHUNKS)], hsem.at[0])
        drain(Y8.at[0, pl.ds(0, CHUNKS * 8)], ysem.at[0])
        drain(XT.at[pl.ds(0, 16)], xsem.at[0])
        drain(AA.at[pl.ds(0, 2)], asem.at[0])
        drain(FO, ends.at[5])
        drain(GH, ends.at[7])
        drain(LO, ends.at[9])
        f_out[...] = FO[...]
        g_out[:KT] = GH[0]
        g_out[KT:] = GH[1]
        loss_out[...] = LO[0:1, 0:1]

    @pl.when(worker)
    def _():
        work(
            fast, co, row, col, xy, zed, xy_peers, z_peers, across, sibling, own, f_out, g_out, loss_out,
            XT, XR, Y8, YM, S, VB, UB, ZB, AA, OWN_B, NA, NB, LA, LB, LBN, XSQ, YSQ, GM, GS, FX, GX, FL, GL, GH, FO, LO, FP, FM, LAM, BADR, BADC,
            hsem, ysem, xsem, asem, nsem, fs, fr, gs, gr, ends,
        )


def work(
    fast, co, row, col, xy, zed, xy_peers, z_peers, across, sibling, own, f_out, g_out, loss_out,
    XT, XR, Y8, YM, S, VB, UB, ZB, AA, OWN_B, NA, NB, LA, LB, LBN, XSQ, YSQ, GM, GS, FX, GX, FL, GL, GH, FO, LO, FP, FM, LAM, BADR, BADC,
    hsem, ysem, xsem, asem, nsem, fs, fr, gs, gr, ends,
):
    other = co["z"] * 4 + across["xl"] * 2
    for n in range(CHUNKS):
        landed = Y8.at[n, pl.ds(other, 2)]
        drain(landed, hsem.at[1 + n])
        for t in z_peers:
            send(landed, landed, ysem.at[0], ysem.at[1 + n], t)

    for copy in own:
        copy.wait()
    own_b = jnp.where(co["xl"] == 0, OWN_B[:KT], OWN_B[KT:]) * LOG2E
    LB[...] = own_b
    NB[xy] = jnp.broadcast_to(full_lse(own_b), (1, 128))
    for t in xy_peers:
        send(NB.at[xy], NB.at[xy], nsem.at[0], nsem.at[1], t)
    drain(AA.at[pl.ds(0, 3)], asem.at[1])
    whole_a = AA[...].reshape(16, 128) * LOG2E
    LA[...] = whole_a
    NA[zed] = jnp.broadcast_to(full_lse(whole_a), (1, 128))
    for t in z_peers:
        send(NA.at[zed], NA.at[zed], nsem.at[2], nsem.at[3], t)

    drain(XT.at[pl.ds(0, 31)], xsem.at[1])
    for p in range(16):
        x = XT[p // 4 * 8 : p // 4 * 8 + 8, :, pl.ds((p % 4) * 128, 128)].reshape(F, 128)
        XR[p * 128 : (p + 1) * 128, :] = x.T
        x = x.astype(jnp.float32)
        XSQ[p : p + 1, :] = jnp.sum(x * x, axis=0, keepdims=True)

    def set_v(v, first, count):
        for k in range(count):
            at = first + k
            VB[:, at * 128 : (at + 1) * 128] = jnp.broadcast_to(v[k : k + 1, :], (8, 128))

    def over_lanes(peaks, masses):
        peak = jnp.concatenate(peaks, axis=0).T
        mass = jnp.concatenate(masses, axis=0).T
        top = jnp.max(peak, axis=0, keepdims=True)
        return top + jnp.log2(jnp.sum(mass * jnp.exp2(peak - top), axis=0, keepdims=True))

    def send_rows(t, h):
        for peer in xy_peers:
            send(FX.at[t, h, xy], FX.at[t, h, xy], fs.at[t], fr.at[t, h], peer)

    scale = 2.0 / F / EPS * LOG2E
    tiles_in = CHUNK // 128
    for n in range(CHUNKS):
        drain(Y8.at[n, pl.ds(0, 29)], ysem.at[1 + n])
        span = slice(n * CHUNK, (n + 1) * CHUNK)
        total = jnp.zeros((16, CHUNK), jnp.float32)
        for q in range(16):
            y = jnp.concatenate(
                [Y8[n, 2 * q].astype(jnp.float32), Y8[n, 2 * q + 1].astype(jnp.float32)], axis=0
            )
            YM[q * 16 : (q + 1) * 16, span] = y.astype(jnp.bfloat16)
            total = total + y * y
        total = jnp.sum(total, axis=0, keepdims=True)
        for k in range(tiles_in):
            at = n * tiles_in + k
            YSQ[at : at + 1, :] = total[:, k * 128 : (k + 1) * 128]
        mine = slice(n * tiles_in, (n + 1) * tiles_in)
        set_v(LB[mine] - YSQ[mine] * (LOG2E / F / EPS), n * tiles_in, tiles_in)

        def multiply(p, _):
            at = pl.ds(pl.multiple_of(p * 128, 128), 128)
            inner = jnp.dot(XR[at, :], YM[:, span], preferred_element_type=jnp.float32)
            S[at, span] = inner * scale
            return 0

        lax.fori_loop(0, 16, multiply, 0, unroll=4)

        def first_rows(h, _):
            for q in range(4):
                peaks, masses = [], []
                for r in range(16):
                    at = pl.ds(pl.multiple_of(h * 512 + q * 128 + r * 8, 8), 8)
                    tiles = [
                        S[at, k * 128 : (k + 1) * 128] + VB[:, k * 128 : (k + 1) * 128]
                        for k in range(n * tiles_in, (n + 1) * tiles_in)
                    ]
                    if n:
                        before = FP[at, :]
                        peak = tree(jnp.maximum, tiles + [before])
                        mass = [jnp.exp2(s - peak) for s in tiles] + [FM[at, :] * jnp.exp2(before - peak)]
                    else:
                        peak = tree(jnp.maximum, tiles)
                        mass = [jnp.exp2(s - peak) for s in tiles]
                    mass = tree(jnp.add, mass)
                    if n < CHUNKS - 1:
                        FP[at, :] = peak
                        FM[at, :] = mass
                    peaks.append(peak)
                    masses.append(mass)
                if n == CHUNKS - 1:
                    FX[0, h, xy, q : q + 1, :] = over_lanes(peaks, masses)
            if n == CHUNKS - 1:
                send_rows(0, h)
            return 0

        lax.fori_loop(0, PARTS, first_rows, 0)

    def f_pass(t):
        def part(h, _):
            for q in range(4):
                peaks, masses = [], []
                for r in range(16):
                    at = pl.ds(pl.multiple_of(h * 512 + q * 128 + r * 8, 8), 8)
                    tiles = [S[at, k * 128 : (k + 1) * 128] + VB[:, k * 128 : (k + 1) * 128] for k in range(KT)]
                    peak = functools.reduce(jnp.maximum, tiles)
                    peaks.append(peak)
                    masses.append(functools.reduce(jnp.add, [jnp.exp2(s - peak) for s in tiles]))
                FX[t, h, xy, q : q + 1, :] = over_lanes(peaks, masses)
            send_rows(t, h)
            return 0

        lax.fori_loop(0, PARTS, part, 0)

    def swap_columns(t):
        for peer in z_peers:
            send(GX.at[t, zed], GX.at[t, zed], gs.at[t], gr.at[t], peer)
        drain(GX.at[t, pl.ds(0, 7)], gr.at[t])

    def g_pass(t):
        def part(h, _):
            drain(FX.at[t, h, pl.ds(0, 15)], fr.at[t, h])
            rows = pl.ds(pl.multiple_of(h * 4, 4), 4)
            u = LA[rows, :] - (lse(FX[t, h]) - jnp.where(t == 0, LBN[...], 0.0))
            for q in range(4):
                UB[q * 128 : (q + 1) * 128, :] = jnp.broadcast_to(u[q : q + 1, :], (128, 128)).T
            for k0 in range(0, KT, GROUP):
                span = slice(k0 * 128, (k0 + GROUP) * 128)
                peaks = [GM[:, k * 128 : (k + 1) * 128] for k in range(k0, k0 + GROUP)]
                masses = [GS[:, k * 128 : (k + 1) * 128] for k in range(k0, k0 + GROUP)]
                for q in range(4):
                    us = [UB[q * 128 + r * 8 : q * 128 + r * 8 + 8, :] for r in range(16)]
                    for k in range(GROUP):
                        lanes = slice((k0 + k) * 128, (k0 + k + 1) * 128)
                        tiles = [
                            S[pl.ds(pl.multiple_of(h * 512 + q * 128 + r * 8, 8), 8), lanes] + us[r]
                            for r in range(16)
                        ]
                        peak = functools.reduce(jnp.maximum, tiles + [peaks[k]])
                        mass = functools.reduce(jnp.add, [jnp.exp2(s - peak) for s in tiles])
                        masses[k] = mass + masses[k] * jnp.exp2(peaks[k] - peak)
                        peaks[k] = peak
                for k in range(GROUP):
                    lanes = slice((k0 + k) * 128, (k0 + k + 1) * 128)
                    GM[:, lanes] = peaks[k]
                    GS[:, lanes] = masses[k]
            return 0

        GM[...] = jnp.full(GM.shape, -jnp.inf, jnp.float32)
        GS[...] = jnp.zeros(GS.shape, jnp.float32)
        lax.fori_loop(0, PARTS, part, 0)
        for k in range(KT):
            lanes = slice(k * 128, (k + 1) * 128)
            peak = GM[:, lanes]
            top = jnp.max(peak, axis=0, keepdims=True)
            mass = jnp.sum(GS[:, lanes] * jnp.exp2(peak - top), axis=0, keepdims=True)
            GX[t, zed, k : k + 1, :] = top + jnp.log2(mass)
        swap_columns(t)

    def fast_rows(t):
        def part(h, _):
            for q in range(4):
                sums = []
                for r in range(16):
                    at = pl.ds(pl.multiple_of(h * 512 + q * 128 + r * 8, 8), 8)
                    sums.append(
                        tree(
                            jnp.add,
                            [S[at, k * 128 : (k + 1) * 128] * VB[:, k * 128 : (k + 1) * 128] for k in range(KT)],
                        )
                    )
                FX[t, h, xy, q : q + 1, :] = jnp.sum(jnp.concatenate(sums, axis=0).T, axis=0, keepdims=True)
            send_rows(t, h)
            return 0

        lax.fori_loop(0, PARTS, part, 0)

    def fast_columns(t, first):
        def part(h, _):
            drain(FX.at[t, h, pl.ds(0, 15)], fr.at[t, h])
            rows = pl.ds(pl.multiple_of(h * 4, 4), 4)
            mass_a = jnp.exp2(LA[rows, :])
            if first:
                lam = lse(FX[t, h])
                LAM[rows, :] = lam - LBN[...]
                zs = mass_a
                for q in range(4):
                    UB[q * 128 : (q + 1) * 128, :] = jnp.broadcast_to(lam[q : q + 1, :], (128, 128)).T
            else:
                total = jnp.sum(FX[t, h], axis=0)
                zs = mass_a / total
                good = jnp.logical_and(total >= 2.0**-35, zs <= 2.0**20)
                BADR[...] = jnp.maximum(BADR[...], jnp.where(good, 0.0, 1.0))
            for q in range(4):
                ZB[q * 128 : (q + 1) * 128, :] = jnp.broadcast_to(zs[q : q + 1, :], (128, 128)).T
            for k0 in range(0, KT, GROUP):
                sums = [GS[:, k * 128 : (k + 1) * 128] for k in range(k0, k0 + GROUP)]
                for q in range(4):
                    at = [q * 128 + r * 8 for r in range(16)]
                    z = [ZB[i : i + 8, :] for i in at]
                    for k in range(GROUP):
                        lanes = slice((k0 + k) * 128, (k0 + k + 1) * 128)
                        terms = []
                        for r in range(16):
                            here = pl.ds(pl.multiple_of(h * 512 + at[r], 8), 8)
                            p = S[here, lanes]
                            if first:
                                p = jnp.exp2(p + VB[:, lanes] - UB[at[r] : at[r] + 8, :])
                                S[here, lanes] = p
                            terms.append(p * z[r])
                        sums[k] = sums[k] + tree(jnp.add, terms)
                for k in range(GROUP):
                    GS[:, (k0 + k) * 128 : (k0 + k + 1) * 128] = sums[k]
            return 0

        GS[...] = jnp.zeros(GS.shape, jnp.float32)
        lax.fori_loop(0, PARTS, part, 0)
        for k in range(KT):
            GX[t, zed, k : k + 1, :] = jnp.sum(GS[:, k * 128 : (k + 1) * 128], axis=0, keepdims=True)
        swap_columns(t)
        total = jnp.sum(GX[t], axis=0)
        w = jnp.exp2(LB[...]) / total
        good = jnp.logical_and(total >= 2.0**-65, w <= 2.0**45)
        BADC[...] = jnp.maximum(BADC[...], jnp.where(good, 0.0, 1.0))
        return w

    drain(NB.at[pl.ds(0, 15)], nsem.at[1])
    drain(NA.at[pl.ds(0, 7)], nsem.at[3])
    log_b_norm = lse(NB[...])
    log_a_norm = lse(NA[...])
    LB[...] = LB[...] - log_b_norm
    LA[...] = LA[...] - log_a_norm
    LBN[...] = log_b_norm
    BADR[...] = jnp.zeros(BADR.shape, jnp.float32)
    BADC[...] = jnp.zeros(BADC.shape, jnp.float32)
    last = ITERS - 1

    if fast:
        set_v(fast_columns(0, True), 0, KT)
        fast_rows(1)

        def iteration(t, _):
            w = fast_columns(t, False)

            @pl.when(t < last)
            def _():
                set_v(w, 0, KT)
                fast_rows(t + 1)

            return 0

        lax.fori_loop(1, ITERS, iteration, 0)
        g = (LB[...] - jnp.log2(jnp.sum(GX[last], axis=0))) * (EPS * LN2)
        lam = jnp.concatenate([jnp.sum(FX[last, h], axis=0) for h in range(PARTS)], axis=0)
        lam = LAM[...] + jnp.log2(lam)
    else:

        def iteration(t, _):
            g_pass(t)

            @pl.when(t < last)
            def _():
                set_v(LB[...] - lse(GX[t]), 0, KT)
                f_pass(t + 1)

            return 0

        lax.fori_loop(0, ITERS, iteration, 0)
        g = YSQ[...] * (1.0 / F) - lse(GX[last]) * (EPS * LN2)
        lam = jnp.concatenate([lse(FX[last, h]) for h in range(PARTS)], axis=0)
    f = XSQ[...] * (1.0 / F) - lam * (EPS * LN2)

    bad = jnp.maximum(jnp.max(BADR[...], axis=0, keepdims=True), jnp.max(BADC[...], axis=0, keepdims=True)) > 0.0
    GL[xy] = jnp.where(bad, jnp.nan, jnp.sum(jnp.exp2(LB[...]) * g, axis=0, keepdims=True))
    GH[co["xl"]] = g
    for t in xy_peers:
        send(GL.at[xy], GL.at[xy], ends.at[0], ends.at[1], t)
    send(GH.at[co["xl"]], GH.at[co["xl"]], ends.at[2], ends.at[3], across)
    FL[zed] = jnp.where(bad, jnp.nan, jnp.sum(jnp.exp2(LA[...]) * f, axis=0, keepdims=True))
    for t in z_peers:
        send(FL.at[zed], FL.at[zed], ends.at[10], ends.at[11], t)
    FO[...] = jnp.where(co["xl"] == 0, f[0:4], f[8:12])
    send(FO, FO, ends.at[4], ends.at[5], sibling)
    f_out[...] = jnp.where(co["xl"] == 0, f[4:8], f[12:16])
    drain(GH.at[0], ends.at[3])
    send(GH, GH, ends.at[6], ends.at[7], sibling)
    g_out[:KT] = GH[0]
    g_out[KT:] = GH[1]
    drain(FL.at[pl.ds(0, 7)], ends.at[11])
    drain(GL.at[pl.ds(0, 15)], ends.at[1])
    loss = jnp.sum(jnp.sum(FL[...], axis=0), axis=(0, 1), keepdims=True) + jnp.sum(
        jnp.sum(GL[...], axis=0), axis=(0, 1), keepdims=True
    )
    LO[...] = jnp.broadcast_to(loss, (1, 128))
    send(LO, LO, ends.at[8], ends.at[9], sibling)
    loss_out[...] = loss

    drain(GL.at[pl.ds(0, 15)], ends.at[0])
    drain(GH.at[0], ends.at[2])
    drain(FO, ends.at[4])
    drain(GH, ends.at[6])
    drain(LO, ends.at[8])
    drain(FL.at[pl.ds(0, 7)], ends.at[10])
    for t in range(ITERS):
        drain(FX.at[t, :, pl.ds(0, 15)], fs.at[t])
        drain(GX.at[t, pl.ds(0, 7)], gs.at[t])
    drain(NB.at[pl.ds(0, 15)], nsem.at[0])
    drain(NA.at[pl.ds(0, 7)], nsem.at[2])
    drain(Y8.at[0, pl.ds(0, CHUNKS)], hsem.at[0])
    drain(Y8.at[:, pl.ds(0, 21)], ysem.at[0])
    drain(XT.at[pl.ds(0, 15)], xsem.at[0])
    drain(AA.at[0], asem.at[0])


def whole(fast, x_feat, y_feat, a_logits, b_logits):
    f32, bf16 = jnp.float32, jnp.bfloat16
    vmem = pl.BlockSpec(memory_space=pltpu.VMEM)
    hbm = pl.BlockSpec(memory_space=pltpu.HBM)
    dma = pltpu.SemaphoreType.DMA
    f, g, loss = pl.pallas_call(
        functools.partial(kernel, fast),
        out_shape=(
            jax.ShapeDtypeStruct((4, 128), f32),
            jax.ShapeDtypeStruct((24, 128), f32),
            jax.ShapeDtypeStruct((1, 1), f32),
        ),
        in_specs=[hbm, hbm, hbm, hbm],
        out_specs=(vmem, vmem, vmem),
        scratch_shapes=[
            pltpu.VMEM((32, 32, 512), bf16),
            pltpu.VMEM((ROWS, F), bf16),
            pltpu.VMEM((CHUNKS, 32, 8, CHUNK), bf16),
            pltpu.VMEM((F, COLS), bf16),
            pltpu.VMEM((ROWS, COLS), f32),
            pltpu.VMEM((8, COLS), f32),
            pltpu.VMEM((512, 128), f32),
            pltpu.VMEM((512, 128), f32),
            pltpu.VMEM((4, 4, 128), f32),
            pltpu.VMEM((24, 128), f32),
            pltpu.VMEM((8, 1, 128), f32),
            pltpu.VMEM((16, 1, 128), f32),
            pltpu.VMEM((16, 128), f32),
            pltpu.VMEM((KT, 128), f32),
            pltpu.VMEM((1, 128), f32),
            pltpu.VMEM((16, 128), f32),
            pltpu.VMEM((KT, 128), f32),
            pltpu.VMEM((8, COLS), f32),
            pltpu.VMEM((8, COLS), f32),
            pltpu.VMEM((ITERS, PARTS, 16, 4, 128), f32),
            pltpu.VMEM((ITERS, 8, KT, 128), f32),
            pltpu.VMEM((8, 1, 128), f32),
            pltpu.VMEM((16, 1, 128), f32),
            pltpu.VMEM((2, KT, 128), f32),
            pltpu.VMEM((4, 128), f32),
            pltpu.VMEM((1, 128), f32),
            pltpu.VMEM((ROWS, 128), f32),
            pltpu.VMEM((ROWS, 128), f32),
            pltpu.VMEM((16, 128), f32),
            pltpu.VMEM((4, 128), f32),
            pltpu.VMEM((KT, 128), f32),
            dma((1 + CHUNKS,)),
            dma((1 + CHUNKS,)),
            dma((2,)),
            dma((2,)),
            dma((4,)),
            dma((3 + CHUNKS,)),
            dma((ITERS,)),
            dma((ITERS, PARTS)),
            dma((ITERS,)),
            dma((ITERS,)),
            dma((12,)),
        ],
        compiler_params=pltpu.CompilerParams(
            collective_id=0 if fast else 1, has_side_effects=True, vmem_limit_bytes=63 * 1024 * 1024
        ),
        name="sinkhorn" if fast else "sinkhorn_log",
    )(x_feat.T, y_feat.T, a_logits.reshape(4, 128), b_logits.reshape(24, 128))
    return f.reshape(512), g.reshape(3072), loss.reshape(())


def body(x_feat, y_feat, a_logits, b_logits):
    args = x_feat, y_feat, a_logits, b_logits
    f, g, loss = whole(True, *args)
    return lax.cond(jnp.isfinite(loss), lambda *_: (f, g, loss), functools.partial(whole, False), *args)


def solution(mesh):
    in_specs = (P("row", "col"), P("col", "row"), P("row"), P("col"))
    out_specs = (P("row"), P("col"), P())
    return jax.shard_map(body, mesh=mesh, in_specs=in_specs, out_specs=out_specs, check_vma=False)
```

```python
import functools
import math

import jax
import jax.numpy as jnp
from jax import lax
from jax.experimental import pallas as pl
from jax.experimental.pallas import tpu as pltpu
from jax.sharding import PartitionSpec as P

ITERS = 4
EPS = 0.05
LN2 = math.log(2.0)
LOG2E = 1.0 / LN2
F = 256
SIZE = {"z": 8, "xl": 2, "c": 2, "y": 4, "xh": 2}
MESH = pl.DeviceIdType.MESH
ROWS, COLS = 2048, 1536
PARTS = 4
KT = COLS // 128
CHUNKS = 3
CHUNK = COLS // CHUNKS
GROUP = 4


def coords():
    r = lax.axis_index("row")
    k = lax.axis_index("col")
    return {"z": r // 4, "xl": lax.rem(r // 2, 2), "c": lax.rem(r, 2), "y": k // 2, "xh": lax.rem(k, 2)}


def device(o):
    return ((o["z"] * 2 + o["xl"]) * 2 + o["c"], o["y"] * 2 + o["xh"])


def hops(o):
    z, y = o.get("z", 0), o.get("y", 0)
    return min(z, 8 - z) + min(y, 4 - y) + 2 * o.get("xh", 0) + o.get("xl", 0)


def offsets(names):
    out = [{}]
    for n in names:
        out = [{**o, n: d} for o in out for d in range(SIZE[n])]
    return sorted([o for o in out if any(o.values())], key=lambda o: -hops(o))


def at_offset(co, o, c):
    return {n: (lax.rem(co[n] + o[n], SIZE[n]) if o.get(n, 0) else co[n]) for n in co} | {"c": c}


def send(src, dst, ssem, rsem, target):
    pltpu.make_async_remote_copy(
        src_ref=src, dst_ref=dst, send_sem=ssem, recv_sem=rsem, device_id=device(target), device_id_type=MESH
    ).start()


def drain(ref, sem):
    pltpu.make_async_copy(ref, ref, sem).wait()


def lse(x):
    peak = jnp.max(x, axis=0)
    return peak + jnp.log2(jnp.sum(jnp.exp2(x - peak[None]), axis=0))


def tree(op, xs):
    while len(xs) > 1:
        xs = [op(xs[i], xs[i + 1]) if i + 1 < len(xs) else xs[i] for i in range(0, len(xs), 2)]
    return xs[0]


def full_lse(x):
    peak = jnp.max(x, axis=(0, 1), keepdims=True)
    return peak + jnp.log2(jnp.sum(jnp.exp2(x - peak), axis=(0, 1), keepdims=True))


def kernel(
    fast, xt, yt, a, b, f_out, g_out, loss_out,
    XT, XR, Y8, YM, S, PB, VB, UB, ZB, AA, OWN_B, NA, NB, LA, LB, LBN, XSQ, YSQ, GM, GS, FX, GX, FL, GL, GH, FO, LO, FP, FM, LAM, BADR, BADC,
    hsem, ysem, xsem, asem, nsem, local, fs, fr, gs, gr, ends,
):
    co = coords()
    row, col = device(co)
    c = co["c"]
    xy = (co["xh"] * 2 + co["xl"]) * 4 + co["y"]
    zed = co["z"]
    xy_offsets = offsets(["y", "xh", "xl"])
    z_offsets = offsets(["z"])
    xy_peers = [at_offset(co, o, 1) for o in xy_offsets]
    z_peers = [at_offset(co, o, 1) for o in z_offsets]
    across = at_offset(co, {"xl": 1}, 1)
    sibling = at_offset(co, {}, 1 - c)
    worker = c == 1
    helper = c == 0

    barrier = pltpu.get_barrier_semaphore()

    def greet(t):
        pl.semaphore_signal(barrier, inc=1, device_id=device(t), device_id_type=MESH)

    @pl.when(worker)
    def _():
        for o in xy_offsets + z_offsets:
            greet(at_offset(co, o, 0))
            greet(at_offset(co, o, 1))
        greet(sibling)

    @pl.when(helper)
    def _():
        greet(sibling)

    def cut(xl, n):
        return yt.at[:, pl.ds(pl.multiple_of(xl * COLS + n * CHUNK, 128), CHUNK)]

    own = [
        pltpu.make_async_copy(xt, XT.at[row % 4 * 8 + col], local.at[0]),
        pltpu.make_async_copy(a, AA.at[row % 4], local.at[1]),
        pltpu.make_async_copy(b, OWN_B, local.at[2]),
    ] + [pltpu.make_async_copy(cut(co["xl"], n), Y8.at[n, row], local.at[3 + n]) for n in range(CHUNKS)]

    @pl.when(worker)
    def _():
        for copy in own:
            copy.start()

    pl.semaphore_wait(barrier, len(xy_offsets) + len(z_offsets) + 1)

    for n in range(CHUNKS):
        send(cut(across["xl"], n), Y8.at[n, row], hsem.at[0], hsem.at[1 + n], across)
    for n in range(CHUNKS):
        for t in z_peers:
            send(cut(co["xl"], n), Y8.at[n, row], ysem.at[0], ysem.at[1 + n], t)
    for t in xy_peers:
        send(xt, XT.at[row % 4 * 8 + col], xsem.at[0], xsem.at[1], t)
    send(a, AA.at[row % 4], asem.at[0], asem.at[1], across)

    @pl.when(helper)
    def _():
        for n in range(CHUNKS):
            send(cut(co["xl"], n), Y8.at[n, row], ysem.at[0], ysem.at[1 + n], sibling)
        send(xt, XT.at[row % 4 * 8 + col], xsem.at[0], xsem.at[1], sibling)
        send(a, AA.at[row % 4], asem.at[0], asem.at[1], sibling)
        drain(Y8.at[0, pl.ds(0, CHUNKS)], hsem.at[0])
        drain(Y8.at[0, pl.ds(0, CHUNKS * 8)], ysem.at[0])
        drain(XT.at[pl.ds(0, 16)], xsem.at[0])
        drain(AA.at[pl.ds(0, 2)], asem.at[0])
        drain(FO, ends.at[5])
        drain(GH, ends.at[7])
        drain(LO, ends.at[9])
        f_out[...] = FO[...]
        g_out[:KT] = GH[0]
        g_out[KT:] = GH[1]
        loss_out[...] = LO[0:1, 0:1]

    @pl.when(worker)
    def _():
        work(
            fast, co, row, col, xy, zed, xy_peers, z_peers, across, sibling, own, f_out, g_out, loss_out,
            XT, XR, Y8, YM, S, PB, VB, UB, ZB, AA, OWN_B, NA, NB, LA, LB, LBN, XSQ, YSQ, GM, GS, FX, GX, FL, GL, GH, FO, LO, FP, FM, LAM, BADR, BADC,
            hsem, ysem, xsem, asem, nsem, fs, fr, gs, gr, ends,
        )


def work(
    fast, co, row, col, xy, zed, xy_peers, z_peers, across, sibling, own, f_out, g_out, loss_out,
    XT, XR, Y8, YM, S, PB, VB, UB, ZB, AA, OWN_B, NA, NB, LA, LB, LBN, XSQ, YSQ, GM, GS, FX, GX, FL, GL, GH, FO, LO, FP, FM, LAM, BADR, BADC,
    hsem, ysem, xsem, asem, nsem, fs, fr, gs, gr, ends,
):
    other = co["z"] * 4 + across["xl"] * 2
    for n in range(CHUNKS):
        landed = Y8.at[n, pl.ds(other, 2)]
        drain(landed, hsem.at[1 + n])
        for t in z_peers:
            send(landed, landed, ysem.at[0], ysem.at[1 + n], t)

    for copy in own:
        copy.wait()
    own_b = jnp.where(co["xl"] == 0, OWN_B[:KT], OWN_B[KT:]) * LOG2E
    LB[...] = own_b
    NB[xy] = jnp.broadcast_to(full_lse(own_b), (1, 128))
    for t in xy_peers:
        send(NB.at[xy], NB.at[xy], nsem.at[0], nsem.at[1], t)
    drain(AA.at[pl.ds(0, 3)], asem.at[1])
    whole_a = AA[...].reshape(16, 128) * LOG2E
    LA[...] = whole_a
    NA[zed] = jnp.broadcast_to(full_lse(whole_a), (1, 128))
    for t in z_peers:
        send(NA.at[zed], NA.at[zed], nsem.at[2], nsem.at[3], t)

    drain(XT.at[pl.ds(0, 31)], xsem.at[1])
    for p in range(16):
        x = XT[p // 4 * 8 : p // 4 * 8 + 8, :, pl.ds((p % 4) * 128, 128)].reshape(F, 128)
        XR[p * 128 : (p + 1) * 128, :] = x.T
        x = x.astype(jnp.float32)
        XSQ[p : p + 1, :] = jnp.sum(x * x, axis=0, keepdims=True)

    def set_v(v, first, count):
        for k in range(count):
            at = first + k
            VB[:, at * 128 : (at + 1) * 128] = jnp.broadcast_to(v[k : k + 1, :], (8, 128))

    def over_lanes(peaks, masses):
        peak = jnp.concatenate(peaks, axis=0).T
        mass = jnp.concatenate(masses, axis=0).T
        top = jnp.max(peak, axis=0, keepdims=True)
        return top + jnp.log2(jnp.sum(mass * jnp.exp2(peak - top), axis=0, keepdims=True))

    def send_rows(t, h):
        for peer in xy_peers:
            send(FX.at[t, h, xy], FX.at[t, h, xy], fs.at[t], fr.at[t, h], peer)

    scale = 2.0 / F / EPS * LOG2E
    tiles_in = CHUNK // 128
    for n in range(CHUNKS):
        drain(Y8.at[n, pl.ds(0, 29)], ysem.at[1 + n])
        span = slice(n * CHUNK, (n + 1) * CHUNK)
        total = jnp.zeros((16, CHUNK), jnp.float32)
        for q in range(16):
            y = jnp.concatenate(
                [Y8[n, 2 * q].astype(jnp.float32), Y8[n, 2 * q + 1].astype(jnp.float32)], axis=0
            )
            YM[q * 16 : (q + 1) * 16, span] = y.astype(jnp.bfloat16)
            total = total + y * y
        total = jnp.sum(total, axis=0, keepdims=True)
        for k in range(tiles_in):
            at = n * tiles_in + k
            YSQ[at : at + 1, :] = total[:, k * 128 : (k + 1) * 128]
        mine = slice(n * tiles_in, (n + 1) * tiles_in)
        set_v(LB[mine] - YSQ[mine] * (LOG2E / F / EPS), n * tiles_in, tiles_in)

        def multiply(p, _):
            at = pl.ds(pl.multiple_of(p * 128, 128), 128)
            inner = jnp.dot(XR[at, :], YM[:, span], preferred_element_type=jnp.float32)
            S[at, span] = inner * scale
            return 0

        lax.fori_loop(0, 16, multiply, 0, unroll=4)

        def first_rows(h, _):
            for q in range(4):
                peaks, masses = [], []
                for r in range(16):
                    at = pl.ds(pl.multiple_of(h * 512 + q * 128 + r * 8, 8), 8)
                    tiles = [
                        S[at, k * 128 : (k + 1) * 128] + VB[:, k * 128 : (k + 1) * 128]
                        for k in range(n * tiles_in, (n + 1) * tiles_in)
                    ]
                    if n:
                        before = FP[at, :]
                        peak = tree(jnp.maximum, tiles + [before])
                        mass = [jnp.exp2(s - peak) for s in tiles] + [FM[at, :] * jnp.exp2(before - peak)]
                    else:
                        peak = tree(jnp.maximum, tiles)
                        mass = [jnp.exp2(s - peak) for s in tiles]
                    mass = tree(jnp.add, mass)
                    if n < CHUNKS - 1:
                        FP[at, :] = peak
                        FM[at, :] = mass
                    peaks.append(peak)
                    masses.append(mass)
                if n == CHUNKS - 1:
                    FX[0, h, xy, q : q + 1, :] = over_lanes(peaks, masses)
            if n == CHUNKS - 1:
                send_rows(0, h)
            return 0

        lax.fori_loop(0, PARTS, first_rows, 0)

    def f_pass(t):
        def part(h, _):
            for q in range(4):
                peaks, masses = [], []
                for r in range(16):
                    at = pl.ds(pl.multiple_of(h * 512 + q * 128 + r * 8, 8), 8)
                    tiles = [S[at, k * 128 : (k + 1) * 128] + VB[:, k * 128 : (k + 1) * 128] for k in range(KT)]
                    peak = functools.reduce(jnp.maximum, tiles)
                    peaks.append(peak)
                    masses.append(functools.reduce(jnp.add, [jnp.exp2(s - peak) for s in tiles]))
                FX[t, h, xy, q : q + 1, :] = over_lanes(peaks, masses)
            send_rows(t, h)
            return 0

        lax.fori_loop(0, PARTS, part, 0)

    def swap_columns(t):
        for peer in z_peers:
            send(GX.at[t, zed], GX.at[t, zed], gs.at[t], gr.at[t], peer)
        drain(GX.at[t, pl.ds(0, 7)], gr.at[t])

    def g_pass(t):
        def part(h, _):
            drain(FX.at[t, h, pl.ds(0, 15)], fr.at[t, h])
            rows = pl.ds(pl.multiple_of(h * 4, 4), 4)
            u = LA[rows, :] - (lse(FX[t, h]) - jnp.where(t == 0, LBN[...], 0.0))
            for q in range(4):
                UB[q * 128 : (q + 1) * 128, :] = jnp.broadcast_to(u[q : q + 1, :], (128, 128)).T
            for k0 in range(0, KT, GROUP):
                span = slice(k0 * 128, (k0 + GROUP) * 128)
                peaks = [GM[:, k * 128 : (k + 1) * 128] for k in range(k0, k0 + GROUP)]
                masses = [GS[:, k * 128 : (k + 1) * 128] for k in range(k0, k0 + GROUP)]
                for q in range(4):
                    us = [UB[q * 128 + r * 8 : q * 128 + r * 8 + 8, :] for r in range(16)]
                    for k in range(GROUP):
                        lanes = slice((k0 + k) * 128, (k0 + k + 1) * 128)
                        tiles = [
                            S[pl.ds(pl.multiple_of(h * 512 + q * 128 + r * 8, 8), 8), lanes] + us[r]
                            for r in range(16)
                        ]
                        peak = functools.reduce(jnp.maximum, tiles + [peaks[k]])
                        mass = functools.reduce(jnp.add, [jnp.exp2(s - peak) for s in tiles])
                        masses[k] = mass + masses[k] * jnp.exp2(peaks[k] - peak)
                        peaks[k] = peak
                for k in range(GROUP):
                    lanes = slice((k0 + k) * 128, (k0 + k + 1) * 128)
                    GM[:, lanes] = peaks[k]
                    GS[:, lanes] = masses[k]
            return 0

        GM[...] = jnp.full(GM.shape, -jnp.inf, jnp.float32)
        GS[...] = jnp.zeros(GS.shape, jnp.float32)
        lax.fori_loop(0, PARTS, part, 0)
        for k in range(KT):
            lanes = slice(k * 128, (k + 1) * 128)
            peak = GM[:, lanes]
            top = jnp.max(peak, axis=0, keepdims=True)
            mass = jnp.sum(GS[:, lanes] * jnp.exp2(peak - top), axis=0, keepdims=True)
            GX[t, zed, k : k + 1, :] = top + jnp.log2(mass)
        swap_columns(t)

    def fast_rows(t):
        def part(h, _):
            for q in range(4):
                sums = []
                for r in range(16):
                    at = pl.ds(pl.multiple_of(h * 512 + q * 128 + r * 8, 8), 8)
                    sums.append(
                        tree(
                            jnp.add,
                            [PB[at, k * 128 : (k + 1) * 128] * VB[:, k * 128 : (k + 1) * 128] for k in range(KT)],
                        )
                    )
                FX[t, h, xy, q : q + 1, :] = jnp.sum(jnp.concatenate(sums, axis=0).T, axis=0, keepdims=True)
            send_rows(t, h)
            return 0

        lax.fori_loop(0, PARTS, part, 0)

    def fast_columns(t, first):
        def part(h, _):
            drain(FX.at[t, h, pl.ds(0, 15)], fr.at[t, h])
            rows = pl.ds(pl.multiple_of(h * 4, 4), 4)
            mass_a = jnp.exp2(LA[rows, :])
            if first:
                lam = lse(FX[t, h])
                LAM[rows, :] = lam - LBN[...]
                zs = mass_a
                for q in range(4):
                    UB[q * 128 : (q + 1) * 128, :] = jnp.broadcast_to(lam[q : q + 1, :], (128, 128)).T
            else:
                total = jnp.sum(FX[t, h], axis=0)
                zs = mass_a / total
                good = jnp.logical_and(total >= 2.0**-35, zs <= 2.0**20)
                BADR[...] = jnp.maximum(BADR[...], jnp.where(good, 0.0, 1.0))
            for q in range(4):
                ZB[q * 128 : (q + 1) * 128, :] = jnp.broadcast_to(zs[q : q + 1, :], (128, 128)).T
            for k0 in range(0, KT, GROUP):
                sums = [GS[:, k * 128 : (k + 1) * 128] for k in range(k0, k0 + GROUP)]
                for q in range(4):
                    at = [q * 128 + r * 8 for r in range(16)]
                    z = [ZB[i : i + 8, :] for i in at]
                    for k in range(GROUP):
                        lanes = slice((k0 + k) * 128, (k0 + k + 1) * 128)
                        here = [pl.ds(pl.multiple_of(h * 512 + i, 8), 8) for i in at]
                        if first:
                            p = [S[here[r], lanes] + VB[:, lanes] for r in range(16)]
                            p = [jnp.exp2(p[r] - UB[at[r] : at[r] + 8, :]) for r in range(16)]
                            for r in range(16):
                                PB[here[r], lanes] = p[r]
                        else:
                            p = [PB[here[r], lanes] for r in range(16)]
                        sums[k] = sums[k] + tree(jnp.add, [p[r] * z[r] for r in range(16)])
                for k in range(GROUP):
                    GS[:, (k0 + k) * 128 : (k0 + k + 1) * 128] = sums[k]
            return 0

        GS[...] = jnp.zeros(GS.shape, jnp.float32)
        lax.fori_loop(0, PARTS, part, 0)
        for k in range(KT):
            GX[t, zed, k : k + 1, :] = jnp.sum(GS[:, k * 128 : (k + 1) * 128], axis=0, keepdims=True)
        swap_columns(t)
        total = jnp.sum(GX[t], axis=0)
        w = jnp.exp2(LB[...]) / total
        good = jnp.logical_and(total >= 2.0**-65, w <= 2.0**45)
        BADC[...] = jnp.maximum(BADC[...], jnp.where(good, 0.0, 1.0))
        return w

    drain(NB.at[pl.ds(0, 15)], nsem.at[1])
    drain(NA.at[pl.ds(0, 7)], nsem.at[3])
    log_b_norm = lse(NB[...])
    log_a_norm = lse(NA[...])
    LB[...] = LB[...] - log_b_norm
    LA[...] = LA[...] - log_a_norm
    LBN[...] = log_b_norm
    BADR[...] = jnp.zeros(BADR.shape, jnp.float32)
    BADC[...] = jnp.zeros(BADC.shape, jnp.float32)
    last = ITERS - 1

    if fast:
        set_v(fast_columns(0, True), 0, KT)
        fast_rows(1)

        def iteration(t, _):
            w = fast_columns(t, False)

            @pl.when(t < last)
            def _():
                set_v(w, 0, KT)
                fast_rows(t + 1)

            return 0

        lax.fori_loop(1, ITERS, iteration, 0)
        g = (LB[...] - jnp.log2(jnp.sum(GX[last], axis=0))) * (EPS * LN2)
        lam = jnp.concatenate([jnp.sum(FX[last, h], axis=0) for h in range(PARTS)], axis=0)
        lam = LAM[...] + jnp.log2(lam)
    else:

        def iteration(t, _):
            g_pass(t)

            @pl.when(t < last)
            def _():
                set_v(LB[...] - lse(GX[t]), 0, KT)
                f_pass(t + 1)

            return 0

        lax.fori_loop(0, ITERS, iteration, 0)
        g = YSQ[...] * (1.0 / F) - lse(GX[last]) * (EPS * LN2)
        lam = jnp.concatenate([lse(FX[last, h]) for h in range(PARTS)], axis=0)
    f = XSQ[...] * (1.0 / F) - lam * (EPS * LN2)

    bad = jnp.maximum(jnp.max(BADR[...], axis=0, keepdims=True), jnp.max(BADC[...], axis=0, keepdims=True)) > 0.0
    GL[xy] = jnp.where(bad, jnp.nan, jnp.sum(jnp.exp2(LB[...]) * g, axis=0, keepdims=True))
    GH[co["xl"]] = g
    for t in xy_peers:
        send(GL.at[xy], GL.at[xy], ends.at[0], ends.at[1], t)
    send(GH.at[co["xl"]], GH.at[co["xl"]], ends.at[2], ends.at[3], across)
    FL[zed] = jnp.where(bad, jnp.nan, jnp.sum(jnp.exp2(LA[...]) * f, axis=0, keepdims=True))
    for t in z_peers:
        send(FL.at[zed], FL.at[zed], ends.at[10], ends.at[11], t)
    FO[...] = jnp.where(co["xl"] == 0, f[0:4], f[8:12])
    send(FO, FO, ends.at[4], ends.at[5], sibling)
    f_out[...] = jnp.where(co["xl"] == 0, f[4:8], f[12:16])
    drain(GH.at[0], ends.at[3])
    send(GH, GH, ends.at[6], ends.at[7], sibling)
    g_out[:KT] = GH[0]
    g_out[KT:] = GH[1]
    drain(FL.at[pl.ds(0, 7)], ends.at[11])
    drain(GL.at[pl.ds(0, 15)], ends.at[1])
    loss = jnp.sum(jnp.sum(FL[...], axis=0), axis=(0, 1), keepdims=True) + jnp.sum(
        jnp.sum(GL[...], axis=0), axis=(0, 1), keepdims=True
    )
    LO[...] = jnp.broadcast_to(loss, (1, 128))
    send(LO, LO, ends.at[8], ends.at[9], sibling)
    loss_out[...] = loss

    drain(GL.at[pl.ds(0, 15)], ends.at[0])
    drain(GH.at[0], ends.at[2])
    drain(FO, ends.at[4])
    drain(GH, ends.at[6])
    drain(LO, ends.at[8])
    drain(FL.at[pl.ds(0, 7)], ends.at[10])
    for t in range(ITERS):
        drain(FX.at[t, :, pl.ds(0, 15)], fs.at[t])
        drain(GX.at[t, pl.ds(0, 7)], gs.at[t])
    drain(NB.at[pl.ds(0, 15)], nsem.at[0])
    drain(NA.at[pl.ds(0, 7)], nsem.at[2])
    drain(Y8.at[0, pl.ds(0, CHUNKS)], hsem.at[0])
    drain(Y8.at[:, pl.ds(0, 21)], ysem.at[0])
    drain(XT.at[pl.ds(0, 15)], xsem.at[0])
    drain(AA.at[0], asem.at[0])


def whole(fast, x_feat, y_feat, a_logits, b_logits):
    f32, bf16 = jnp.float32, jnp.bfloat16
    vmem = pl.BlockSpec(memory_space=pltpu.VMEM)
    hbm = pl.BlockSpec(memory_space=pltpu.HBM)
    dma = pltpu.SemaphoreType.DMA
    f, g, loss = pl.pallas_call(
        functools.partial(kernel, fast),
        out_shape=(
            jax.ShapeDtypeStruct((4, 128), f32),
            jax.ShapeDtypeStruct((24, 128), f32),
            jax.ShapeDtypeStruct((1, 1), f32),
        ),
        in_specs=[hbm, hbm, hbm, hbm],
        out_specs=(vmem, vmem, vmem),
        scratch_shapes=[
            pltpu.VMEM((32, 32, 512), bf16),
            pltpu.VMEM((ROWS, F), bf16),
            pltpu.VMEM((CHUNKS, 32, 8, CHUNK), bf16),
            pltpu.VMEM((F, COLS), bf16),
            pltpu.VMEM((ROWS, COLS), f32),
            pltpu.VMEM((ROWS, COLS) if fast else (8, 128), f32),
            pltpu.VMEM((8, COLS), f32),
            pltpu.VMEM((512, 128), f32),
            pltpu.VMEM((512, 128), f32),
            pltpu.VMEM((4, 4, 128), f32),
            pltpu.VMEM((24, 128), f32),
            pltpu.VMEM((8, 1, 128), f32),
            pltpu.VMEM((16, 1, 128), f32),
            pltpu.VMEM((16, 128), f32),
            pltpu.VMEM((KT, 128), f32),
            pltpu.VMEM((1, 128), f32),
            pltpu.VMEM((16, 128), f32),
            pltpu.VMEM((KT, 128), f32),
            pltpu.VMEM((8, COLS), f32),
            pltpu.VMEM((8, COLS), f32),
            pltpu.VMEM((ITERS, PARTS, 16, 4, 128), f32),
            pltpu.VMEM((ITERS, 8, KT, 128), f32),
            pltpu.VMEM((8, 1, 128), f32),
            pltpu.VMEM((16, 1, 128), f32),
            pltpu.VMEM((2, KT, 128), f32),
            pltpu.VMEM((4, 128), f32),
            pltpu.VMEM((1, 128), f32),
            pltpu.VMEM((ROWS, 128), f32),
            pltpu.VMEM((ROWS, 128), f32),
            pltpu.VMEM((16, 128), f32),
            pltpu.VMEM((4, 128), f32),
            pltpu.VMEM((KT, 128), f32),
            dma((1 + CHUNKS,)),
            dma((1 + CHUNKS,)),
            dma((2,)),
            dma((2,)),
            dma((4,)),
            dma((3 + CHUNKS,)),
            dma((ITERS,)),
            dma((ITERS, PARTS)),
            dma((ITERS,)),
            dma((ITERS,)),
            dma((12,)),
        ],
        compiler_params=pltpu.CompilerParams(
            collective_id=0 if fast else 1, has_side_effects=True, vmem_limit_bytes=63 * 1024 * 1024
        ),
        name="sinkhorn" if fast else "sinkhorn_log",
    )(x_feat.T, y_feat.T, a_logits.reshape(4, 128), b_logits.reshape(24, 128))
    return f.reshape(512), g.reshape(3072), loss.reshape(())


def body(x_feat, y_feat, a_logits, b_logits):
    args = x_feat, y_feat, a_logits, b_logits
    f, g, loss = whole(True, *args)
    return lax.cond(jnp.isfinite(loss), lambda *_: (f, g, loss), functools.partial(whole, False), *args)


def solution(mesh):
    in_specs = (P("row", "col"), P("col", "row"), P("row"), P("col"))
    out_specs = (P("row"), P("col"), P())
    return jax.shard_map(body, mesh=mesh, in_specs=in_specs, out_specs=out_specs, check_vma=False)
```

```python
import functools
import math

import jax
import jax.numpy as jnp
from jax import lax
from jax.experimental import pallas as pl
from jax.experimental.pallas import tpu as pltpu
from jax.sharding import PartitionSpec as P

ITERS = 4
EPS = 0.05
LN2 = math.log(2.0)
LOG2E = 1.0 / LN2
F = 256
SIZE = {"z": 8, "xl": 2, "c": 2, "y": 4, "xh": 2}
MESH = pl.DeviceIdType.MESH
ROWS, COLS = 2048, 1536
PARTS = 4
KT = COLS // 128
CHUNKS = 2
CHUNK = COLS // CHUNKS
GROUP = 4


def coords():
    r = lax.axis_index("row")
    k = lax.axis_index("col")
    return {"z": r // 4, "xl": lax.rem(r // 2, 2), "c": lax.rem(r, 2), "y": k // 2, "xh": lax.rem(k, 2)}


def device(o):
    return ((o["z"] * 2 + o["xl"]) * 2 + o["c"], o["y"] * 2 + o["xh"])


def hops(o):
    z, y = o.get("z", 0), o.get("y", 0)
    return min(z, 8 - z) + min(y, 4 - y) + 2 * o.get("xh", 0) + o.get("xl", 0)


def offsets(names):
    out = [{}]
    for n in names:
        out = [{**o, n: d} for o in out for d in range(SIZE[n])]
    return sorted([o for o in out if any(o.values())], key=lambda o: -hops(o))


def at_offset(co, o, c):
    return {n: (lax.rem(co[n] + o[n], SIZE[n]) if o.get(n, 0) else co[n]) for n in co} | {"c": c}


def send(src, dst, ssem, rsem, target):
    pltpu.make_async_remote_copy(
        src_ref=src, dst_ref=dst, send_sem=ssem, recv_sem=rsem, device_id=device(target), device_id_type=MESH
    ).start()


def drain(ref, sem):
    pltpu.make_async_copy(ref, ref, sem).wait()


def lse(x):
    peak = jnp.max(x, axis=0)
    return peak + jnp.log2(jnp.sum(jnp.exp2(x - peak[None]), axis=0))


def tree(op, xs):
    while len(xs) > 1:
        xs = [op(xs[i], xs[i + 1]) if i + 1 < len(xs) else xs[i] for i in range(0, len(xs), 2)]
    return xs[0]


def full_lse(x):
    peak = jnp.max(x, axis=(0, 1), keepdims=True)
    return peak + jnp.log2(jnp.sum(jnp.exp2(x - peak), axis=(0, 1), keepdims=True))


def kernel(
    fast, xt, yt, a, b, f_out, g_out, loss_out,
    XT, XR, Y8, YM, S, PB, VB, UB, ZB, AA, OWN_B, NA, NB, LA, LB, LBN, XSQ, YSQ, GM, GS, FX, GX, FL, GL, GH, FO, LO, FP, FM, LAM, BADR, BADC,
    hsem, ysem, xsem, asem, nsem, local, fs, fr, gs, gr, ends,
):
    co = coords()
    row, col = device(co)
    c = co["c"]
    xy = (co["xh"] * 2 + co["xl"]) * 4 + co["y"]
    zed = co["z"]
    xy_offsets = offsets(["y", "xh", "xl"])
    z_offsets = offsets(["z"])
    xy_peers = [at_offset(co, o, 1) for o in xy_offsets]
    z_peers = [at_offset(co, o, 1) for o in z_offsets]
    across = at_offset(co, {"xl": 1}, 1)
    sibling = at_offset(co, {}, 1 - c)
    worker = c == 1
    helper = c == 0

    barrier = pltpu.get_barrier_semaphore()

    def greet(t):
        pl.semaphore_signal(barrier, inc=1, device_id=device(t), device_id_type=MESH)

    @pl.when(worker)
    def _():
        for o in xy_offsets + z_offsets:
            greet(at_offset(co, o, 0))
            greet(at_offset(co, o, 1))
        greet(sibling)

    @pl.when(helper)
    def _():
        greet(sibling)

    def cut(xl, n):
        return yt.at[:, pl.ds(pl.multiple_of(xl * COLS + n * CHUNK, 128), CHUNK)]

    own = [
        pltpu.make_async_copy(xt, XT.at[row % 4 * 8 + col], local.at[0]),
        pltpu.make_async_copy(a, AA.at[row % 4], local.at[1]),
        pltpu.make_async_copy(b, OWN_B, local.at[2]),
    ] + [pltpu.make_async_copy(cut(co["xl"], n), Y8.at[n, row], local.at[3 + n]) for n in range(CHUNKS)]

    @pl.when(worker)
    def _():
        for copy in own:
            copy.start()

    pl.semaphore_wait(barrier, len(xy_offsets) + len(z_offsets) + 1)

    send(a, AA.at[row % 4], asem.at[0], asem.at[1], across)

    @pl.when(helper)
    def _():
        send(a, AA.at[row % 4], asem.at[0], asem.at[1], sibling)

    for n in range(CHUNKS):
        send(cut(across["xl"], n), Y8.at[n, row], hsem.at[0], hsem.at[1 + n], across)
    for n in range(CHUNKS):
        for t in z_peers:
            send(cut(co["xl"], n), Y8.at[n, row], ysem.at[0], ysem.at[1 + n], t)
    for t in xy_peers:
        send(xt, XT.at[row % 4 * 8 + col], xsem.at[0], xsem.at[1], t)

    @pl.when(helper)
    def _():
        for n in range(CHUNKS):
            send(cut(co["xl"], n), Y8.at[n, row], ysem.at[0], ysem.at[1 + n], sibling)
        send(xt, XT.at[row % 4 * 8 + col], xsem.at[0], xsem.at[1], sibling)
        drain(Y8.at[0, pl.ds(0, CHUNKS)], hsem.at[0])
        drain(Y8.at[0, pl.ds(0, CHUNKS * 8)], ysem.at[0])
        drain(XT.at[pl.ds(0, 16)], xsem.at[0])
        drain(AA.at[pl.ds(0, 2)], asem.at[0])
        drain(FO, ends.at[5])
        drain(GH, ends.at[7])
        drain(LO, ends.at[9])
        f_out[...] = FO[...]
        g_out[:KT] = GH[0]
        g_out[KT:] = GH[1]
        loss_out[...] = LO[0:1, 0:1]

    @pl.when(worker)
    def _():
        work(
            fast, co, row, col, xy, zed, xy_peers, z_peers, across, sibling, own, f_out, g_out, loss_out,
            XT, XR, Y8, YM, S, PB, VB, UB, ZB, AA, OWN_B, NA, NB, LA, LB, LBN, XSQ, YSQ, GM, GS, FX, GX, FL, GL, GH, FO, LO, FP, FM, LAM, BADR, BADC,
            hsem, ysem, xsem, asem, nsem, fs, fr, gs, gr, ends,
        )


def work(
    fast, co, row, col, xy, zed, xy_peers, z_peers, across, sibling, own, f_out, g_out, loss_out,
    XT, XR, Y8, YM, S, PB, VB, UB, ZB, AA, OWN_B, NA, NB, LA, LB, LBN, XSQ, YSQ, GM, GS, FX, GX, FL, GL, GH, FO, LO, FP, FM, LAM, BADR, BADC,
    hsem, ysem, xsem, asem, nsem, fs, fr, gs, gr, ends,
):
    other = co["z"] * 4 + across["xl"] * 2
    for n in range(CHUNKS):
        landed = Y8.at[n, pl.ds(other, 2)]
        drain(landed, hsem.at[1 + n])
        for t in z_peers:
            send(landed, landed, ysem.at[0], ysem.at[1 + n], t)

    for copy in own:
        copy.wait()
    own_b = jnp.where(co["xl"] == 0, OWN_B[:KT], OWN_B[KT:]) * LOG2E
    LB[...] = own_b
    NB[xy] = jnp.broadcast_to(full_lse(own_b), (1, 128))
    for t in xy_peers:
        send(NB.at[xy], NB.at[xy], nsem.at[0], nsem.at[1], t)
    drain(AA.at[pl.ds(0, 3)], asem.at[1])
    whole_a = AA[...].reshape(16, 128) * LOG2E
    LA[...] = whole_a
    NA[zed] = jnp.broadcast_to(full_lse(whole_a), (1, 128))
    for t in z_peers:
        send(NA.at[zed], NA.at[zed], nsem.at[2], nsem.at[3], t)

    drain(XT.at[pl.ds(0, 31)], xsem.at[1])
    for p in range(16):
        x = XT[p // 4 * 8 : p // 4 * 8 + 8, :, pl.ds((p % 4) * 128, 128)].reshape(F, 128)
        XR[p * 128 : (p + 1) * 128, :] = x.T

    def set_v(v, first, count):
        for k in range(count):
            at = first + k
            VB[:, at * 128 : (at + 1) * 128] = jnp.broadcast_to(v[k : k + 1, :], (8, 128))

    def over_lanes(peaks, masses):
        peak = jnp.concatenate(peaks, axis=0).T
        mass = jnp.concatenate(masses, axis=0).T
        top = jnp.max(peak, axis=0, keepdims=True)
        return top + jnp.log2(jnp.sum(mass * jnp.exp2(peak - top), axis=0, keepdims=True))

    def send_rows(t, h):
        for peer in xy_peers:
            send(FX.at[t, h, xy], FX.at[t, h, xy], fs.at[t], fr.at[t, h], peer)

    scale = 2.0 / F / EPS * LOG2E
    tiles_in = CHUNK // 128
    for n in range(CHUNKS):
        drain(Y8.at[n, pl.ds(0, 29)], ysem.at[1 + n])
        span = slice(n * CHUNK, (n + 1) * CHUNK)
        total = jnp.zeros((16, CHUNK), jnp.float32)
        for q in range(16):
            y = jnp.concatenate(
                [Y8[n, 2 * q].astype(jnp.float32), Y8[n, 2 * q + 1].astype(jnp.float32)], axis=0
            )
            YM[q * 16 : (q + 1) * 16, span] = y.astype(jnp.bfloat16)
            total = total + y * y
        total = jnp.sum(total, axis=0, keepdims=True)
        for k in range(tiles_in):
            at = n * tiles_in + k
            YSQ[at : at + 1, :] = total[:, k * 128 : (k + 1) * 128]
        mine = slice(n * tiles_in, (n + 1) * tiles_in)
        set_v(LB[mine] - YSQ[mine] * (LOG2E / F / EPS), n * tiles_in, tiles_in)

        def first_rows(h, _):
            for q in range(4):
                block = pl.ds(pl.multiple_of(h * 512 + q * 128, 128), 128)
                inner = jnp.dot(XR[block, :], YM[:, span], preferred_element_type=jnp.float32) * scale
                S[block, span] = inner
                peaks, masses = [], []
                for r in range(16):
                    at = pl.ds(pl.multiple_of(h * 512 + q * 128 + r * 8, 8), 8)
                    tiles = [
                        inner[r * 8 : (r + 1) * 8, k * 128 : (k + 1) * 128]
                        + VB[:, (n * tiles_in + k) * 128 : (n * tiles_in + k + 1) * 128]
                        for k in range(tiles_in)
                    ]
                    if n:
                        before = FP[at, :]
                        peak = tree(jnp.maximum, tiles + [before])
                        mass = [jnp.exp2(s - peak) for s in tiles] + [FM[at, :] * jnp.exp2(before - peak)]
                    else:
                        peak = tree(jnp.maximum, tiles)
                        mass = [jnp.exp2(s - peak) for s in tiles]
                    mass = tree(jnp.add, mass)
                    if n < CHUNKS - 1:
                        FP[at, :] = peak
                        FM[at, :] = mass
                    peaks.append(peak)
                    masses.append(mass)
                if n == CHUNKS - 1:
                    FX[0, h, xy, q : q + 1, :] = over_lanes(peaks, masses)
            if n == CHUNKS - 1:
                send_rows(0, h)
            return 0

        lax.fori_loop(0, PARTS, first_rows, 0)

    def f_pass(t):
        def part(h, _):
            for q in range(4):
                peaks, masses = [], []
                for r in range(16):
                    at = pl.ds(pl.multiple_of(h * 512 + q * 128 + r * 8, 8), 8)
                    tiles = [S[at, k * 128 : (k + 1) * 128] + VB[:, k * 128 : (k + 1) * 128] for k in range(KT)]
                    peak = functools.reduce(jnp.maximum, tiles)
                    peaks.append(peak)
                    masses.append(functools.reduce(jnp.add, [jnp.exp2(s - peak) for s in tiles]))
                FX[t, h, xy, q : q + 1, :] = over_lanes(peaks, masses)
            send_rows(t, h)
            return 0

        lax.fori_loop(0, PARTS, part, 0)

    def swap_columns(t):
        for peer in z_peers:
            send(GX.at[t, zed], GX.at[t, zed], gs.at[t], gr.at[t], peer)
        drain(GX.at[t, pl.ds(0, 7)], gr.at[t])

    def g_pass(t):
        def part(h, _):
            drain(FX.at[t, h, pl.ds(0, 15)], fr.at[t, h])
            rows = pl.ds(pl.multiple_of(h * 4, 4), 4)
            u = LA[rows, :] - (lse(FX[t, h]) - jnp.where(t == 0, LBN[...], 0.0))
            for q in range(4):
                UB[q * 128 : (q + 1) * 128, :] = jnp.broadcast_to(u[q : q + 1, :], (128, 128)).T
            for k0 in range(0, KT, GROUP):
                span = slice(k0 * 128, (k0 + GROUP) * 128)
                peaks = [GM[:, k * 128 : (k + 1) * 128] for k in range(k0, k0 + GROUP)]
                masses = [GS[:, k * 128 : (k + 1) * 128] for k in range(k0, k0 + GROUP)]
                for q in range(4):
                    us = [UB[q * 128 + r * 8 : q * 128 + r * 8 + 8, :] for r in range(16)]
                    for k in range(GROUP):
                        lanes = slice((k0 + k) * 128, (k0 + k + 1) * 128)
                        tiles = [
                            S[pl.ds(pl.multiple_of(h * 512 + q * 128 + r * 8, 8), 8), lanes] + us[r]
                            for r in range(16)
                        ]
                        peak = functools.reduce(jnp.maximum, tiles + [peaks[k]])
                        mass = functools.reduce(jnp.add, [jnp.exp2(s - peak) for s in tiles])
                        masses[k] = mass + masses[k] * jnp.exp2(peaks[k] - peak)
                        peaks[k] = peak
                for k in range(GROUP):
                    lanes = slice((k0 + k) * 128, (k0 + k + 1) * 128)
                    GM[:, lanes] = peaks[k]
                    GS[:, lanes] = masses[k]
            return 0

        GM[...] = jnp.full(GM.shape, -jnp.inf, jnp.float32)
        GS[...] = jnp.zeros(GS.shape, jnp.float32)
        lax.fori_loop(0, PARTS, part, 0)
        for k in range(KT):
            lanes = slice(k * 128, (k + 1) * 128)
            peak = GM[:, lanes]
            top = jnp.max(peak, axis=0, keepdims=True)
            mass = jnp.sum(GS[:, lanes] * jnp.exp2(peak - top), axis=0, keepdims=True)
            GX[t, zed, k : k + 1, :] = top + jnp.log2(mass)
        swap_columns(t)

    def fast_rows(t):
        def part(h, _):
            for q in range(4):
                sums = []
                for r in range(16):
                    at = pl.ds(pl.multiple_of(h * 512 + q * 128 + r * 8, 8), 8)
                    sums.append(
                        tree(
                            jnp.add,
                            [PB[at, k * 128 : (k + 1) * 128] * VB[:, k * 128 : (k + 1) * 128] for k in range(KT)],
                        )
                    )
                FX[t, h, xy, q : q + 1, :] = jnp.sum(jnp.concatenate(sums, axis=0).T, axis=0, keepdims=True)
            send_rows(t, h)
            return 0

        lax.fori_loop(0, PARTS, part, 0)

    def fast_columns(t, first):
        def part(h, _):
            drain(FX.at[t, h, pl.ds(0, 15)], fr.at[t, h])
            rows = pl.ds(pl.multiple_of(h * 4, 4), 4)
            mass_a = jnp.exp2(LA[rows, :])
            if first:
                lam = lse(FX[t, h])
                LAM[rows, :] = lam - LBN[...]
                zs = mass_a
                for q in range(4):
                    UB[q * 128 : (q + 1) * 128, :] = jnp.broadcast_to(lam[q : q + 1, :], (128, 128)).T
            else:
                total = jnp.sum(FX[t, h], axis=0)
                zs = mass_a / total
                good = jnp.logical_and(total >= 2.0**-35, zs <= 2.0**20)
                BADR[...] = jnp.maximum(BADR[...], jnp.where(good, 0.0, 1.0))
            for q in range(4):
                ZB[q * 128 : (q + 1) * 128, :] = jnp.broadcast_to(zs[q : q + 1, :], (128, 128)).T
            for k0 in range(0, KT, GROUP):
                sums = [GS[:, k * 128 : (k + 1) * 128] for k in range(k0, k0 + GROUP)]
                for q in range(4):
                    at = [q * 128 + r * 8 for r in range(16)]
                    z = [ZB[i : i + 8, :] for i in at]
                    for k in range(GROUP):
                        lanes = slice((k0 + k) * 128, (k0 + k + 1) * 128)
                        here = [pl.ds(pl.multiple_of(h * 512 + i, 8), 8) for i in at]
                        if first:
                            p = [S[here[r], lanes] + VB[:, lanes] for r in range(16)]
                            p = [jnp.exp2(p[r] - UB[at[r] : at[r] + 8, :]) for r in range(16)]
                            for r in range(16):
                                PB[here[r], lanes] = p[r]
                        else:
                            p = [PB[here[r], lanes] for r in range(16)]
                        sums[k] = sums[k] + tree(jnp.add, [p[r] * z[r] for r in range(16)])
                for k in range(GROUP):
                    GS[:, (k0 + k) * 128 : (k0 + k + 1) * 128] = sums[k]
            return 0

        GS[...] = jnp.zeros(GS.shape, jnp.float32)
        lax.fori_loop(0, PARTS, part, 0)
        for k in range(KT):
            GX[t, zed, k : k + 1, :] = jnp.sum(GS[:, k * 128 : (k + 1) * 128], axis=0, keepdims=True)
        swap_columns(t)
        total = jnp.sum(GX[t], axis=0)
        w = jnp.exp2(LB[...]) / total
        good = jnp.logical_and(total >= 2.0**-65, w <= 2.0**45)
        BADC[...] = jnp.maximum(BADC[...], jnp.where(good, 0.0, 1.0))
        return w

    for p in range(16):
        x = XT[p // 4 * 8 : p // 4 * 8 + 8, :, pl.ds((p % 4) * 128, 128)].reshape(F, 128).astype(jnp.float32)
        XSQ[p : p + 1, :] = jnp.sum(x * x, axis=0, keepdims=True)

    drain(NB.at[pl.ds(0, 15)], nsem.at[1])
    drain(NA.at[pl.ds(0, 7)], nsem.at[3])
    log_b_norm = lse(NB[...])
    log_a_norm = lse(NA[...])
    LB[...] = LB[...] - log_b_norm
    LA[...] = LA[...] - log_a_norm
    LBN[...] = log_b_norm
    BADR[...] = jnp.zeros(BADR.shape, jnp.float32)
    BADC[...] = jnp.zeros(BADC.shape, jnp.float32)
    last = ITERS - 1

    if fast:
        set_v(fast_columns(0, True), 0, KT)
        fast_rows(1)

        def iteration(t, _):
            w = fast_columns(t, False)

            @pl.when(t < last)
            def _():
                set_v(w, 0, KT)
                fast_rows(t + 1)

            return 0

        lax.fori_loop(1, ITERS, iteration, 0)
        g = (LB[...] - jnp.log2(jnp.sum(GX[last], axis=0))) * (EPS * LN2)
        lam = jnp.concatenate([jnp.sum(FX[last, h], axis=0) for h in range(PARTS)], axis=0)
        lam = LAM[...] + jnp.log2(lam)
    else:

        def iteration(t, _):
            g_pass(t)

            @pl.when(t < last)
            def _():
                set_v(LB[...] - lse(GX[t]), 0, KT)
                f_pass(t + 1)

            return 0

        lax.fori_loop(0, ITERS, iteration, 0)
        g = YSQ[...] * (1.0 / F) - lse(GX[last]) * (EPS * LN2)
        lam = jnp.concatenate([lse(FX[last, h]) for h in range(PARTS)], axis=0)
    f = XSQ[...] * (1.0 / F) - lam * (EPS * LN2)

    bad = jnp.maximum(jnp.max(BADR[...], axis=0, keepdims=True), jnp.max(BADC[...], axis=0, keepdims=True)) > 0.0
    GL[xy] = jnp.where(bad, jnp.nan, jnp.sum(jnp.exp2(LB[...]) * g, axis=0, keepdims=True))
    GH[co["xl"]] = g
    for t in xy_peers:
        send(GL.at[xy], GL.at[xy], ends.at[0], ends.at[1], t)
    send(GH.at[co["xl"]], GH.at[co["xl"]], ends.at[2], ends.at[3], across)
    FL[zed] = jnp.where(bad, jnp.nan, jnp.sum(jnp.exp2(LA[...]) * f, axis=0, keepdims=True))
    for t in z_peers:
        send(FL.at[zed], FL.at[zed], ends.at[10], ends.at[11], t)
    FO[...] = jnp.where(co["xl"] == 0, f[0:4], f[8:12])
    send(FO, FO, ends.at[4], ends.at[5], sibling)
    f_out[...] = jnp.where(co["xl"] == 0, f[4:8], f[12:16])
    drain(GH.at[0], ends.at[3])
    send(GH, GH, ends.at[6], ends.at[7], sibling)
    g_out[:KT] = GH[0]
    g_out[KT:] = GH[1]
    drain(FL.at[pl.ds(0, 7)], ends.at[11])
    drain(GL.at[pl.ds(0, 15)], ends.at[1])
    loss = jnp.sum(jnp.sum(FL[...], axis=0), axis=(0, 1), keepdims=True) + jnp.sum(
        jnp.sum(GL[...], axis=0), axis=(0, 1), keepdims=True
    )
    LO[...] = jnp.broadcast_to(loss, (1, 128))
    send(LO, LO, ends.at[8], ends.at[9], sibling)
    loss_out[...] = loss

    drain(GL.at[pl.ds(0, 15)], ends.at[0])
    drain(GH.at[0], ends.at[2])
    drain(FO, ends.at[4])
    drain(GH, ends.at[6])
    drain(LO, ends.at[8])
    drain(FL.at[pl.ds(0, 7)], ends.at[10])
    for t in range(ITERS):
        drain(FX.at[t, :, pl.ds(0, 15)], fs.at[t])
        drain(GX.at[t, pl.ds(0, 7)], gs.at[t])
    drain(NB.at[pl.ds(0, 15)], nsem.at[0])
    drain(NA.at[pl.ds(0, 7)], nsem.at[2])
    drain(Y8.at[0, pl.ds(0, CHUNKS)], hsem.at[0])
    drain(Y8.at[:, pl.ds(0, 21)], ysem.at[0])
    drain(XT.at[pl.ds(0, 15)], xsem.at[0])
    drain(AA.at[0], asem.at[0])


def whole(fast, x_feat, y_feat, a_logits, b_logits):
    f32, bf16 = jnp.float32, jnp.bfloat16
    vmem = pl.BlockSpec(memory_space=pltpu.VMEM)
    hbm = pl.BlockSpec(memory_space=pltpu.HBM)
    dma = pltpu.SemaphoreType.DMA
    f, g, loss = pl.pallas_call(
        functools.partial(kernel, fast),
        out_shape=(
            jax.ShapeDtypeStruct((4, 128), f32),
            jax.ShapeDtypeStruct((24, 128), f32),
            jax.ShapeDtypeStruct((1, 1), f32),
        ),
        in_specs=[hbm, hbm, hbm, hbm],
        out_specs=(vmem, vmem, vmem),
        scratch_shapes=[
            pltpu.VMEM((32, 32, 512), bf16),
            pltpu.VMEM((ROWS, F), bf16),
            pltpu.VMEM((CHUNKS, 32, 8, CHUNK), bf16),
            pltpu.VMEM((F, COLS), bf16),
            pltpu.VMEM((ROWS, COLS), f32),
            pltpu.VMEM((ROWS, COLS) if fast else (8, 128), f32),
            pltpu.VMEM((8, COLS), f32),
            pltpu.VMEM((512, 128), f32),
            pltpu.VMEM((512, 128), f32),
            pltpu.VMEM((4, 4, 128), f32),
            pltpu.VMEM((24, 128), f32),
            pltpu.VMEM((8, 1, 128), f32),
            pltpu.VMEM((16, 1, 128), f32),
            pltpu.VMEM((16, 128), f32),
            pltpu.VMEM((KT, 128), f32),
            pltpu.VMEM((1, 128), f32),
            pltpu.VMEM((16, 128), f32),
            pltpu.VMEM((KT, 128), f32),
            pltpu.VMEM((8, COLS), f32),
            pltpu.VMEM((8, COLS), f32),
            pltpu.VMEM((ITERS, PARTS, 16, 4, 128), f32),
            pltpu.VMEM((ITERS, 8, KT, 128), f32),
            pltpu.VMEM((8, 1, 128), f32),
            pltpu.VMEM((16, 1, 128), f32),
            pltpu.VMEM((2, KT, 128), f32),
            pltpu.VMEM((4, 128), f32),
            pltpu.VMEM((1, 128), f32),
            pltpu.VMEM((ROWS, 128), f32),
            pltpu.VMEM((ROWS, 128), f32),
            pltpu.VMEM((16, 128), f32),
            pltpu.VMEM((4, 128), f32),
            pltpu.VMEM((KT, 128), f32),
            dma((1 + CHUNKS,)),
            dma((1 + CHUNKS,)),
            dma((2,)),
            dma((2,)),
            dma((4,)),
            dma((3 + CHUNKS,)),
            dma((ITERS,)),
            dma((ITERS, PARTS)),
            dma((ITERS,)),
            dma((ITERS,)),
            dma((12,)),
        ],
        compiler_params=pltpu.CompilerParams(
            collective_id=0 if fast else 1, has_side_effects=True, vmem_limit_bytes=63 * 1024 * 1024
        ),
        name="sinkhorn" if fast else "sinkhorn_log",
    )(x_feat.T, y_feat.T, a_logits.reshape(4, 128), b_logits.reshape(24, 128))
    return f.reshape(512), g.reshape(3072), loss.reshape(())


def body(x_feat, y_feat, a_logits, b_logits):
    args = x_feat, y_feat, a_logits, b_logits
    f, g, loss = whole(True, *args)
    return lax.cond(jnp.isfinite(loss), lambda *_: (f, g, loss), functools.partial(whole, False), *args)


def solution(mesh):
    in_specs = (P("row", "col"), P("col", "row"), P("row"), P("col"))
    out_specs = (P("row"), P("col"), P())
    return jax.shard_map(body, mesh=mesh, in_specs=in_specs, out_specs=out_specs, check_vma=False)
```

```python
import functools
import math

import jax
import jax.numpy as jnp
from jax import lax
from jax.experimental import pallas as pl
from jax.experimental.pallas import tpu as pltpu
from jax.sharding import PartitionSpec as P

ITERS = 4
EPS = 0.05
LN2 = math.log(2.0)
LOG2E = 1.0 / LN2
F = 256
SIZE = {"z": 8, "xl": 2, "c": 2, "y": 4, "xh": 2}
MESH = pl.DeviceIdType.MESH
ROWS, COLS = 2048, 1536
PARTS = 4
KT = COLS // 128
CHUNKS = 2
CHUNK = COLS // CHUNKS
GROUP = 4


def coords():
    r = lax.axis_index("row")
    k = lax.axis_index("col")
    return {"z": r // 4, "xl": lax.rem(r // 2, 2), "c": lax.rem(r, 2), "y": k // 2, "xh": lax.rem(k, 2)}


def device(o):
    return ((o["z"] * 2 + o["xl"]) * 2 + o["c"], o["y"] * 2 + o["xh"])


def hops(o):
    z, y = o.get("z", 0), o.get("y", 0)
    return min(z, 8 - z) + min(y, 4 - y) + 2 * o.get("xh", 0) + o.get("xl", 0)


def offsets(names):
    out = [{}]
    for n in names:
        out = [{**o, n: d} for o in out for d in range(SIZE[n])]
    return sorted([o for o in out if any(o.values())], key=lambda o: -hops(o))


def at_offset(co, o, c):
    return {n: (lax.rem(co[n] + o[n], SIZE[n]) if o.get(n, 0) else co[n]) for n in co} | {"c": c}


def send(src, dst, ssem, rsem, target):
    pltpu.make_async_remote_copy(
        src_ref=src, dst_ref=dst, send_sem=ssem, recv_sem=rsem, device_id=device(target), device_id_type=MESH
    ).start()


def drain(ref, sem):
    pltpu.make_async_copy(ref, ref, sem).wait()


def lse(x):
    peak = jnp.max(x, axis=0)
    return peak + jnp.log2(jnp.sum(jnp.exp2(x - peak[None]), axis=0))


def tree(op, xs):
    while len(xs) > 1:
        xs = [op(xs[i], xs[i + 1]) if i + 1 < len(xs) else xs[i] for i in range(0, len(xs), 2)]
    return xs[0]


def full_lse(x):
    peak = jnp.max(x, axis=(0, 1), keepdims=True)
    return peak + jnp.log2(jnp.sum(jnp.exp2(x - peak), axis=(0, 1), keepdims=True))


def kernel(
    fast, xt, yt, a, b, f_out, g_out, loss_out,
    XT, XR, Y8, YM, S, PB, VB, UB, ZB, AA, OWN_B, NA, NB, LA, LB, LBN, XSQ, YSQ, GM, GS, FX, GX, FL, GL, GH, FO, LO, FP, FM, LAM, TOP, RHO, BADR, BADC,
    hsem, ysem, xsem, asem, nsem, local, fs, fr, gs, gr, ends,
):
    co = coords()
    row, col = device(co)
    c = co["c"]
    xy = (co["xh"] * 2 + co["xl"]) * 4 + co["y"]
    zed = co["z"]
    xy_offsets = offsets(["y", "xh", "xl"])
    z_offsets = offsets(["z"])
    xy_peers = [at_offset(co, o, 1) for o in xy_offsets]
    z_peers = [at_offset(co, o, 1) for o in z_offsets]
    across = at_offset(co, {"xl": 1}, 1)
    sibling = at_offset(co, {}, 1 - c)
    worker = c == 1
    helper = c == 0

    barrier = pltpu.get_barrier_semaphore()

    def greet(t):
        pl.semaphore_signal(barrier, inc=1, device_id=device(t), device_id_type=MESH)

    @pl.when(worker)
    def _():
        for o in sorted(xy_offsets + z_offsets, key=lambda o: -hops(o)):
            greet(at_offset(co, o, 0))
            greet(at_offset(co, o, 1))
        greet(sibling)

    @pl.when(helper)
    def _():
        greet(sibling)

    def cut(xl, n):
        return yt.at[:, pl.ds(pl.multiple_of(xl * COLS + n * CHUNK, 128), CHUNK)]

    own = [
        pltpu.make_async_copy(xt, XT.at[row % 4 * 8 + col], local.at[0]),
        pltpu.make_async_copy(a, AA.at[row % 4], local.at[1]),
        pltpu.make_async_copy(b, OWN_B, local.at[2]),
    ] + [pltpu.make_async_copy(cut(co["xl"], n), Y8.at[n, row], local.at[3 + n]) for n in range(CHUNKS)]

    @pl.when(worker)
    def _():
        for copy in own:
            copy.start()

    pl.semaphore_wait(barrier, len(xy_offsets) + len(z_offsets) + 1)

    send(a, AA.at[row % 4], asem.at[0], asem.at[1], across)

    @pl.when(helper)
    def _():
        send(a, AA.at[row % 4], asem.at[0], asem.at[1], sibling)

    for n in range(CHUNKS):
        send(cut(across["xl"], n), Y8.at[n, row], hsem.at[0], hsem.at[1 + n], across)
    for n in range(CHUNKS):
        for t in z_peers:
            send(cut(co["xl"], n), Y8.at[n, row], ysem.at[0], ysem.at[1 + n], t)
    for t in xy_peers:
        send(xt, XT.at[row % 4 * 8 + col], xsem.at[0], xsem.at[1], t)

    @pl.when(helper)
    def _():
        for n in range(CHUNKS):
            send(cut(co["xl"], n), Y8.at[n, row], ysem.at[0], ysem.at[1 + n], sibling)
        send(xt, XT.at[row % 4 * 8 + col], xsem.at[0], xsem.at[1], sibling)
        drain(Y8.at[0, pl.ds(0, CHUNKS)], hsem.at[0])
        drain(Y8.at[0, pl.ds(0, CHUNKS * 8)], ysem.at[0])
        drain(XT.at[pl.ds(0, 16)], xsem.at[0])
        drain(AA.at[pl.ds(0, 2)], asem.at[0])
        drain(FO, ends.at[5])
        drain(GH, ends.at[7])
        drain(LO, ends.at[9])
        f_out[...] = FO[...]
        g_out[:KT] = GH[0]
        g_out[KT:] = GH[1]
        loss_out[...] = LO[0:1, 0:1]

    @pl.when(worker)
    def _():
        work(
            fast, co, row, col, xy, zed, xy_peers, z_peers, across, sibling, own, f_out, g_out, loss_out,
            XT, XR, Y8, YM, S, PB, VB, UB, ZB, AA, OWN_B, NA, NB, LA, LB, LBN, XSQ, YSQ, GM, GS, FX, GX, FL, GL, GH, FO, LO, FP, FM, LAM, TOP, RHO, BADR, BADC,
            hsem, ysem, xsem, asem, nsem, fs, fr, gs, gr, ends,
        )


def work(
    fast, co, row, col, xy, zed, xy_peers, z_peers, across, sibling, own, f_out, g_out, loss_out,
    XT, XR, Y8, YM, S, PB, VB, UB, ZB, AA, OWN_B, NA, NB, LA, LB, LBN, XSQ, YSQ, GM, GS, FX, GX, FL, GL, GH, FO, LO, FP, FM, LAM, TOP, RHO, BADR, BADC,
    hsem, ysem, xsem, asem, nsem, fs, fr, gs, gr, ends,
):
    other = co["z"] * 4 + across["xl"] * 2
    for n in range(CHUNKS):
        landed = Y8.at[n, pl.ds(other, 2)]
        drain(landed, hsem.at[1 + n])
        for t in z_peers:
            send(landed, landed, ysem.at[0], ysem.at[1 + n], t)

    for copy in own:
        copy.wait()
    own_b = jnp.where(co["xl"] == 0, OWN_B[:KT], OWN_B[KT:]) * LOG2E
    LB[...] = own_b
    NB[xy] = jnp.broadcast_to(full_lse(own_b), (1, 128))
    for t in xy_peers:
        send(NB.at[xy], NB.at[xy], nsem.at[0], nsem.at[1], t)
    drain(AA.at[pl.ds(0, 3)], asem.at[1])
    whole_a = AA[...].reshape(16, 128) * LOG2E
    LA[...] = whole_a
    NA[zed] = jnp.broadcast_to(full_lse(whole_a), (1, 128))
    for t in z_peers:
        send(NA.at[zed], NA.at[zed], nsem.at[2], nsem.at[3], t)

    def set_v(v, first, count):
        for k in range(count):
            at = first + k
            VB[:, at * 128 : (at + 1) * 128] = jnp.broadcast_to(v[k : k + 1, :], (8, 128))

    def over_lanes(peaks, masses):
        peak = jnp.concatenate(peaks, axis=0).T
        mass = jnp.concatenate(masses, axis=0).T
        top = jnp.max(peak, axis=0, keepdims=True)
        return top, top + jnp.log2(jnp.sum(mass * jnp.exp2(peak - top), axis=0, keepdims=True))

    def send_rows(t, h):
        for peer in xy_peers:
            send(FX.at[t, h, xy], FX.at[t, h, xy], fs.at[t], fr.at[t, h], peer)

    scale = 2.0 / F / EPS * LOG2E
    tiles_in = CHUNK // 128
    for n in range(CHUNKS):
        drain(Y8.at[n, pl.ds(0, 29)], ysem.at[1 + n])
        span = slice(n * CHUNK, (n + 1) * CHUNK)
        total = jnp.zeros((16, CHUNK), jnp.float32)
        for q in range(16):
            y = jnp.concatenate(
                [Y8[n, 2 * q].astype(jnp.float32), Y8[n, 2 * q + 1].astype(jnp.float32)], axis=0
            )
            YM[q * 16 : (q + 1) * 16, span] = y.astype(jnp.bfloat16)
            total = total + y * y
        total = jnp.sum(total, axis=0, keepdims=True)
        for k in range(tiles_in):
            at = n * tiles_in + k
            YSQ[at : at + 1, :] = total[:, k * 128 : (k + 1) * 128]
        mine = slice(n * tiles_in, (n + 1) * tiles_in)
        set_v(LB[mine] - YSQ[mine] * (LOG2E / F / EPS), n * tiles_in, tiles_in)

        if n == 0:
            drain(XT.at[pl.ds(0, 31)], xsem.at[1])

        def first_rows(h, _):
            for q in range(4):
                block = pl.ds(pl.multiple_of(h * 512 + q * 128, 128), 128)
                if n:
                    x = XR[block, :]
                else:
                    x = XT[pl.ds(pl.multiple_of(h * 8, 8), 8), :, q * 128 : (q + 1) * 128].reshape(F, 128).T
                    XR[block, :] = x
                inner = jnp.dot(x, YM[:, span], preferred_element_type=jnp.float32) * scale
                S[block, span] = inner
                peaks, masses = [], []
                for r in range(16):
                    at = pl.ds(pl.multiple_of(h * 512 + q * 128 + r * 8, 8), 8)
                    tiles = [
                        inner[r * 8 : (r + 1) * 8, k * 128 : (k + 1) * 128]
                        + VB[:, (n * tiles_in + k) * 128 : (n * tiles_in + k + 1) * 128]
                        for k in range(tiles_in)
                    ]
                    if n:
                        before = FP[at, :]
                        peak = tree(jnp.maximum, tiles + [before])
                        mass = [jnp.exp2(s - peak) for s in tiles] + [FM[at, :] * jnp.exp2(before - peak)]
                    else:
                        peak = tree(jnp.maximum, tiles)
                        mass = [jnp.exp2(s - peak) for s in tiles]
                    mass = tree(jnp.add, mass)
                    if n < CHUNKS - 1:
                        FP[at, :] = peak
                        FM[at, :] = mass
                    peaks.append(peak)
                    masses.append(mass)
                if n == CHUNKS - 1:
                    top, FX[0, h, xy, q : q + 1, :] = over_lanes(peaks, masses)
                    TOP[pl.ds(h * 4 + q, 1), :] = top
            if n == CHUNKS - 1:
                send_rows(0, h)
            return 0

        lax.fori_loop(0, PARTS, first_rows, 0)

    def f_pass(t):
        def part(h, _):
            for q in range(4):
                peaks, masses = [], []
                for r in range(16):
                    at = pl.ds(pl.multiple_of(h * 512 + q * 128 + r * 8, 8), 8)
                    tiles = [S[at, k * 128 : (k + 1) * 128] + VB[:, k * 128 : (k + 1) * 128] for k in range(KT)]
                    peak = functools.reduce(jnp.maximum, tiles)
                    peaks.append(peak)
                    masses.append(functools.reduce(jnp.add, [jnp.exp2(s - peak) for s in tiles]))
                FX[t, h, xy, q : q + 1, :] = over_lanes(peaks, masses)[1]
            send_rows(t, h)
            return 0

        lax.fori_loop(0, PARTS, part, 0)

    def swap_columns(t):
        for peer in z_peers:
            send(GX.at[t, zed], GX.at[t, zed], gs.at[t], gr.at[t], peer)
        drain(GX.at[t, pl.ds(0, 7)], gr.at[t])

    def g_pass(t):
        def part(h, _):
            drain(FX.at[t, h, pl.ds(0, 15)], fr.at[t, h])
            rows = pl.ds(pl.multiple_of(h * 4, 4), 4)
            u = LA[rows, :] - (lse(FX[t, h]) - jnp.where(t == 0, LBN[...], 0.0))
            for q in range(4):
                UB[q * 128 : (q + 1) * 128, :] = jnp.broadcast_to(u[q : q + 1, :], (128, 128)).T
            for k0 in range(0, KT, GROUP):
                span = slice(k0 * 128, (k0 + GROUP) * 128)
                peaks = [GM[:, k * 128 : (k + 1) * 128] for k in range(k0, k0 + GROUP)]
                masses = [GS[:, k * 128 : (k + 1) * 128] for k in range(k0, k0 + GROUP)]
                for q in range(4):
                    us = [UB[q * 128 + r * 8 : q * 128 + r * 8 + 8, :] for r in range(16)]
                    for k in range(GROUP):
                        lanes = slice((k0 + k) * 128, (k0 + k + 1) * 128)
                        tiles = [
                            S[pl.ds(pl.multiple_of(h * 512 + q * 128 + r * 8, 8), 8), lanes] + us[r]
                            for r in range(16)
                        ]
                        peak = functools.reduce(jnp.maximum, tiles + [peaks[k]])
                        mass = functools.reduce(jnp.add, [jnp.exp2(s - peak) for s in tiles])
                        masses[k] = mass + masses[k] * jnp.exp2(peaks[k] - peak)
                        peaks[k] = peak
                for k in range(GROUP):
                    lanes = slice((k0 + k) * 128, (k0 + k + 1) * 128)
                    GM[:, lanes] = peaks[k]
                    GS[:, lanes] = masses[k]
            return 0

        GM[...] = jnp.full(GM.shape, -jnp.inf, jnp.float32)
        GS[...] = jnp.zeros(GS.shape, jnp.float32)
        lax.fori_loop(0, PARTS, part, 0)
        for k in range(KT):
            lanes = slice(k * 128, (k + 1) * 128)
            peak = GM[:, lanes]
            top = jnp.max(peak, axis=0, keepdims=True)
            mass = jnp.sum(GS[:, lanes] * jnp.exp2(peak - top), axis=0, keepdims=True)
            GX[t, zed, k : k + 1, :] = top + jnp.log2(mass)
        swap_columns(t)

    def fast_rows(t):
        def part(h, _):
            for q in range(4):
                sums = []
                for r in range(16):
                    at = pl.ds(pl.multiple_of(h * 512 + q * 128 + r * 8, 8), 8)
                    sums.append(
                        tree(
                            jnp.add,
                            [PB[at, k * 128 : (k + 1) * 128] * VB[:, k * 128 : (k + 1) * 128] for k in range(KT)],
                        )
                    )
                total = jnp.sum(jnp.concatenate(sums, axis=0).T, axis=0, keepdims=True)
                FX[t, h, xy, q : q + 1, :] = total * RHO[pl.ds(h * 4 + q, 1), :]
            send_rows(t, h)
            return 0

        lax.fori_loop(0, PARTS, part, 0)

    def fast_columns(t, first):
        def part(h, _):
            drain(FX.at[t, h, pl.ds(0, 15)], fr.at[t, h])
            rows = pl.ds(pl.multiple_of(h * 4, 4), 4)
            mass_a = jnp.exp2(LA[rows, :])
            if first:
                lam = lse(FX[t, h])
                LAM[rows, :] = lam - LBN[...]
                RHO[rows, :] = jnp.exp2(TOP[rows, :] - lam)
                zs = mass_a
            else:
                total = jnp.sum(FX[t, h], axis=0)
                zs = mass_a / total
                good = jnp.logical_and(total >= 2.0**-35, zs <= 2.0**20)
                BADR[...] = jnp.maximum(BADR[...], jnp.where(good, 0.0, 1.0))
            zs = zs * RHO[rows, :]
            for q in range(4):
                ZB[q * 128 : (q + 1) * 128, :] = jnp.broadcast_to(zs[q : q + 1, :], (128, 128)).T
            for k0 in range(0, KT, GROUP):
                sums = [GS[:, k * 128 : (k + 1) * 128] for k in range(k0, k0 + GROUP)]
                for q in range(4):
                    at = [q * 128 + r * 8 for r in range(16)]
                    z = [ZB[i : i + 8, :] for i in at]
                    for k in range(GROUP):
                        lanes = slice((k0 + k) * 128, (k0 + k + 1) * 128)
                        here = [pl.ds(pl.multiple_of(h * 512 + i, 8), 8) for i in at]
                        sums[k] = sums[k] + tree(jnp.add, [PB[here[r], lanes] * z[r] for r in range(16)])
                for k in range(GROUP):
                    GS[:, (k0 + k) * 128 : (k0 + k + 1) * 128] = sums[k]
            return 0

        GS[...] = jnp.zeros(GS.shape, jnp.float32)
        lax.fori_loop(0, PARTS, part, 0)
        for k in range(KT):
            GX[t, zed, k : k + 1, :] = jnp.sum(GS[:, k * 128 : (k + 1) * 128], axis=0, keepdims=True)
        swap_columns(t)
        total = jnp.sum(GX[t], axis=0)
        w = jnp.exp2(LB[...]) / total
        good = jnp.logical_and(total >= 2.0**-65, w <= 2.0**45)
        BADC[...] = jnp.maximum(BADC[...], jnp.where(good, 0.0, 1.0))
        return w

    def exponentials(h, _):
        tops = TOP[pl.ds(pl.multiple_of(h * 4, 4), 4), :]
        for q in range(4):
            UB[q * 128 : (q + 1) * 128, :] = jnp.broadcast_to(tops[q : q + 1, :], (128, 128)).T
        for q in range(4):
            for k in range(KT):
                lanes = slice(k * 128, (k + 1) * 128)
                at = [q * 128 + r * 8 for r in range(16)]
                here = [pl.ds(pl.multiple_of(h * 512 + i, 8), 8) for i in at]
                p = [S[here[r], lanes] + VB[:, lanes] for r in range(16)]
                p = [jnp.exp2(p[r] - UB[at[r] : at[r] + 8, :]) for r in range(16)]
                for r in range(16):
                    PB[here[r], lanes] = p[r]
        return 0

    if fast:
        lax.fori_loop(0, PARTS, exponentials, 0)
    for p in range(16):
        x = XT[p // 4 * 8 : p // 4 * 8 + 8, :, pl.ds((p % 4) * 128, 128)].reshape(F, 128).astype(jnp.float32)
        XSQ[p : p + 1, :] = jnp.sum(x * x, axis=0, keepdims=True)

    drain(NB.at[pl.ds(0, 15)], nsem.at[1])
    drain(NA.at[pl.ds(0, 7)], nsem.at[3])
    log_b_norm = lse(NB[...])
    log_a_norm = lse(NA[...])
    LB[...] = LB[...] - log_b_norm
    LA[...] = LA[...] - log_a_norm
    LBN[...] = log_b_norm
    BADR[...] = jnp.zeros(BADR.shape, jnp.float32)
    BADC[...] = jnp.zeros(BADC.shape, jnp.float32)
    last = ITERS - 1

    if fast:
        set_v(fast_columns(0, True), 0, KT)
        fast_rows(1)

        def iteration(t, _):
            w = fast_columns(t, False)

            @pl.when(t < last)
            def _():
                set_v(w, 0, KT)
                fast_rows(t + 1)

            return 0

        lax.fori_loop(1, ITERS, iteration, 0)
        g = (LB[...] - jnp.log2(jnp.sum(GX[last], axis=0))) * (EPS * LN2)
        lam = jnp.concatenate([jnp.sum(FX[last, h], axis=0) for h in range(PARTS)], axis=0)
        lam = LAM[...] + jnp.log2(lam)
    else:

        def iteration(t, _):
            g_pass(t)

            @pl.when(t < last)
            def _():
                set_v(LB[...] - lse(GX[t]), 0, KT)
                f_pass(t + 1)

            return 0

        lax.fori_loop(0, ITERS, iteration, 0)
        g = YSQ[...] * (1.0 / F) - lse(GX[last]) * (EPS * LN2)
        lam = jnp.concatenate([lse(FX[last, h]) for h in range(PARTS)], axis=0)
    f = XSQ[...] * (1.0 / F) - lam * (EPS * LN2)

    bad = jnp.maximum(jnp.max(BADR[...], axis=0, keepdims=True), jnp.max(BADC[...], axis=0, keepdims=True)) > 0.0
    GL[xy] = jnp.where(bad, jnp.nan, jnp.sum(jnp.exp2(LB[...]) * g, axis=0, keepdims=True))
    GH[co["xl"]] = g
    for t in xy_peers:
        send(GL.at[xy], GL.at[xy], ends.at[0], ends.at[1], t)
    send(GH.at[co["xl"]], GH.at[co["xl"]], ends.at[2], ends.at[3], across)
    FL[zed] = jnp.where(bad, jnp.nan, jnp.sum(jnp.exp2(LA[...]) * f, axis=0, keepdims=True))
    for t in z_peers:
        send(FL.at[zed], FL.at[zed], ends.at[10], ends.at[11], t)
    FO[...] = jnp.where(co["xl"] == 0, f[0:4], f[8:12])
    send(FO, FO, ends.at[4], ends.at[5], sibling)
    f_out[...] = jnp.where(co["xl"] == 0, f[4:8], f[12:16])
    drain(GH.at[0], ends.at[3])
    send(GH, GH, ends.at[6], ends.at[7], sibling)
    g_out[:KT] = GH[0]
    g_out[KT:] = GH[1]
    drain(FL.at[pl.ds(0, 7)], ends.at[11])
    drain(GL.at[pl.ds(0, 15)], ends.at[1])
    loss = jnp.sum(jnp.sum(FL[...], axis=0), axis=(0, 1), keepdims=True) + jnp.sum(
        jnp.sum(GL[...], axis=0), axis=(0, 1), keepdims=True
    )
    LO[...] = jnp.broadcast_to(loss, (1, 128))
    send(LO, LO, ends.at[8], ends.at[9], sibling)
    loss_out[...] = loss

    drain(GL.at[pl.ds(0, 15)], ends.at[0])
    drain(GH.at[0], ends.at[2])
    drain(FO, ends.at[4])
    drain(GH, ends.at[6])
    drain(LO, ends.at[8])
    drain(FL.at[pl.ds(0, 7)], ends.at[10])
    for t in range(ITERS):
        drain(FX.at[t, :, pl.ds(0, 15)], fs.at[t])
        drain(GX.at[t, pl.ds(0, 7)], gs.at[t])
    drain(NB.at[pl.ds(0, 15)], nsem.at[0])
    drain(NA.at[pl.ds(0, 7)], nsem.at[2])
    drain(Y8.at[0, pl.ds(0, CHUNKS)], hsem.at[0])
    drain(Y8.at[:, pl.ds(0, 21)], ysem.at[0])
    drain(XT.at[pl.ds(0, 15)], xsem.at[0])
    drain(AA.at[0], asem.at[0])


def whole(fast, x_feat, y_feat, a_logits, b_logits):
    f32, bf16 = jnp.float32, jnp.bfloat16
    vmem = pl.BlockSpec(memory_space=pltpu.VMEM)
    hbm = pl.BlockSpec(memory_space=pltpu.HBM)
    dma = pltpu.SemaphoreType.DMA
    f, g, loss = pl.pallas_call(
        functools.partial(kernel, fast),
        out_shape=(
            jax.ShapeDtypeStruct((4, 128), f32),
            jax.ShapeDtypeStruct((24, 128), f32),
            jax.ShapeDtypeStruct((1, 1), f32),
        ),
        in_specs=[hbm, hbm, hbm, hbm],
        out_specs=(vmem, vmem, vmem),
        scratch_shapes=[
            pltpu.VMEM((32, 32, 512), bf16),
            pltpu.VMEM((ROWS, F), bf16),
            pltpu.VMEM((CHUNKS, 32, 8, CHUNK), bf16),
            pltpu.VMEM((F, COLS), bf16),
            pltpu.VMEM((ROWS, COLS), f32),
            pltpu.VMEM((ROWS, COLS) if fast else (8, 128), f32),
            pltpu.VMEM((8, COLS), f32),
            pltpu.VMEM((512, 128), f32),
            pltpu.VMEM((512, 128), f32),
            pltpu.VMEM((4, 4, 128), f32),
            pltpu.VMEM((24, 128), f32),
            pltpu.VMEM((8, 1, 128), f32),
            pltpu.VMEM((16, 1, 128), f32),
            pltpu.VMEM((16, 128), f32),
            pltpu.VMEM((KT, 128), f32),
            pltpu.VMEM((1, 128), f32),
            pltpu.VMEM((16, 128), f32),
            pltpu.VMEM((KT, 128), f32),
            pltpu.VMEM((8, COLS), f32),
            pltpu.VMEM((8, COLS), f32),
            pltpu.VMEM((ITERS, PARTS, 16, 4, 128), f32),
            pltpu.VMEM((ITERS, 8, KT, 128), f32),
            pltpu.VMEM((8, 1, 128), f32),
            pltpu.VMEM((16, 1, 128), f32),
            pltpu.VMEM((2, KT, 128), f32),
            pltpu.VMEM((4, 128), f32),
            pltpu.VMEM((1, 128), f32),
            pltpu.VMEM((ROWS, 128), f32),
            pltpu.VMEM((ROWS, 128), f32),
            pltpu.VMEM((16, 128), f32),
            pltpu.VMEM((16, 128), f32),
            pltpu.VMEM((16, 128), f32),
            pltpu.VMEM((4, 128), f32),
            pltpu.VMEM((KT, 128), f32),
            dma((1 + CHUNKS,)),
            dma((1 + CHUNKS,)),
            dma((2,)),
            dma((2,)),
            dma((4,)),
            dma((3 + CHUNKS,)),
            dma((ITERS,)),
            dma((ITERS, PARTS)),
            dma((ITERS,)),
            dma((ITERS,)),
            dma((12,)),
        ],
        compiler_params=pltpu.CompilerParams(
            collective_id=0 if fast else 1, has_side_effects=True, vmem_limit_bytes=63 * 1024 * 1024
        ),
        name="sinkhorn" if fast else "sinkhorn_log",
    )(x_feat.T, y_feat.T, a_logits.reshape(4, 128), b_logits.reshape(24, 128))
    return f.reshape(512), g.reshape(3072), loss.reshape(())


def body(x_feat, y_feat, a_logits, b_logits):
    args = x_feat, y_feat, a_logits, b_logits
    f, g, loss = whole(True, *args)
    return lax.cond(jnp.isfinite(loss), lambda *_: (f, g, loss), functools.partial(whole, False), *args)


def solution(mesh):
    in_specs = (P("row", "col"), P("col", "row"), P("row"), P("col"))
    out_specs = (P("row"), P("col"), P())
    return jax.shard_map(body, mesh=mesh, in_specs=in_specs, out_specs=out_specs, check_vma=False)
```

```python
import functools
import math

import jax
import jax.numpy as jnp
from jax import lax
from jax.experimental import pallas as pl
from jax.experimental.pallas import tpu as pltpu
from jax.sharding import PartitionSpec as P

ITERS = 4
EPS = 0.05
LN2 = math.log(2.0)
LOG2E = 1.0 / LN2
F = 256
SIZE = {"z": 8, "xl": 2, "c": 2, "y": 4, "xh": 2}
MESH = pl.DeviceIdType.MESH
ROWS, COLS = 2048, 1536
PARTS = 4
KT = COLS // 128
CHUNKS = 2
CHUNK = COLS // CHUNKS
GROUP = 4


def coords():
    r = lax.axis_index("row")
    k = lax.axis_index("col")
    return {"z": r // 4, "xl": lax.rem(r // 2, 2), "c": lax.rem(r, 2), "y": k // 2, "xh": lax.rem(k, 2)}


def device(o):
    return ((o["z"] * 2 + o["xl"]) * 2 + o["c"], o["y"] * 2 + o["xh"])


def hops(o):
    z, y = o.get("z", 0), o.get("y", 0)
    return min(z, 8 - z) + min(y, 4 - y) + 2 * o.get("xh", 0) + o.get("xl", 0)


def offsets(names):
    out = [{}]
    for n in names:
        out = [{**o, n: d} for o in out for d in range(SIZE[n])]
    return sorted([o for o in out if any(o.values())], key=lambda o: -hops(o))


def at_offset(co, o, c):
    return {n: (lax.rem(co[n] + o[n], SIZE[n]) if o.get(n, 0) else co[n]) for n in co} | {"c": c}


def send(src, dst, ssem, rsem, target):
    pltpu.make_async_remote_copy(
        src_ref=src, dst_ref=dst, send_sem=ssem, recv_sem=rsem, device_id=device(target), device_id_type=MESH
    ).start()


def drain(ref, sem):
    pltpu.make_async_copy(ref, ref, sem).wait()


def lse(x):
    peak = jnp.max(x, axis=0)
    return peak + jnp.log2(jnp.sum(jnp.exp2(x - peak[None]), axis=0))


def tree(op, xs):
    while len(xs) > 1:
        xs = [op(xs[i], xs[i + 1]) if i + 1 < len(xs) else xs[i] for i in range(0, len(xs), 2)]
    return xs[0]


def full_lse(x):
    peak = jnp.max(x, axis=(0, 1), keepdims=True)
    return peak + jnp.log2(jnp.sum(jnp.exp2(x - peak), axis=(0, 1), keepdims=True))


def kernel(
    fast, xt, yt, a, b, f_out, g_out, loss_out,
    XT, XR, Y8, YM, S, PB, VB, UB, ZB, AA, OWN_B, NA, NB, LA, LB, LBN, XSQ, YSQ, GM, GS, FX, GX, FL, GL, GH, FO, LO, FP, FM, LAM, TOP, RHO, EA, EAR, EB, BADR, BADC,
    hsem, ysem, xsem, asem, nsem, local, fs, fr, gs, gr, ends,
):
    co = coords()
    row, col = device(co)
    c = co["c"]
    xy = (co["xh"] * 2 + co["xl"]) * 4 + co["y"]
    zed = co["z"]
    xy_offsets = offsets(["y", "xh", "xl"])
    z_offsets = offsets(["z"])
    xy_peers = [at_offset(co, o, 1) for o in xy_offsets]
    z_peers = [at_offset(co, o, 1) for o in z_offsets]
    across = at_offset(co, {"xl": 1}, 1)
    sibling = at_offset(co, {}, 1 - c)
    worker = c == 1
    helper = c == 0

    barrier = pltpu.get_barrier_semaphore()

    def greet(t):
        pl.semaphore_signal(barrier, inc=1, device_id=device(t), device_id_type=MESH)

    @pl.when(worker)
    def _():
        for o in sorted(xy_offsets + z_offsets, key=lambda o: -hops(o)):
            greet(at_offset(co, o, 0))
            greet(at_offset(co, o, 1))
        greet(sibling)

    @pl.when(helper)
    def _():
        greet(sibling)

    def cut(xl, n):
        return yt.at[:, pl.ds(pl.multiple_of(xl * COLS + n * CHUNK, 128), CHUNK)]

    own = [
        pltpu.make_async_copy(xt, XT.at[row % 4 * 8 + col], local.at[0]),
        pltpu.make_async_copy(a, AA.at[row % 4], local.at[1]),
        pltpu.make_async_copy(b, OWN_B, local.at[2]),
    ] + [pltpu.make_async_copy(cut(co["xl"], n), Y8.at[n, row], local.at[3 + n]) for n in range(CHUNKS)]

    @pl.when(worker)
    def _():
        for copy in own:
            copy.start()

    pl.semaphore_wait(barrier, len(xy_offsets) + len(z_offsets) + 1)

    send(a, AA.at[row % 4], asem.at[0], asem.at[1], across)

    @pl.when(helper)
    def _():
        send(a, AA.at[row % 4], asem.at[0], asem.at[1], sibling)

    for n in range(CHUNKS):
        send(cut(across["xl"], n), Y8.at[n, row], hsem.at[0], hsem.at[1 + n], across)
    for n in range(CHUNKS):
        for t in z_peers:
            send(cut(co["xl"], n), Y8.at[n, row], ysem.at[0], ysem.at[1 + n], t)
    for t in xy_peers:
        send(xt, XT.at[row % 4 * 8 + col], xsem.at[0], xsem.at[1], t)

    @pl.when(helper)
    def _():
        for n in range(CHUNKS):
            send(cut(co["xl"], n), Y8.at[n, row], ysem.at[0], ysem.at[1 + n], sibling)
        send(xt, XT.at[row % 4 * 8 + col], xsem.at[0], xsem.at[1], sibling)
        drain(Y8.at[0, pl.ds(0, CHUNKS)], hsem.at[0])
        drain(Y8.at[0, pl.ds(0, CHUNKS * 8)], ysem.at[0])
        drain(XT.at[pl.ds(0, 16)], xsem.at[0])
        drain(AA.at[pl.ds(0, 2)], asem.at[0])
        drain(FO, ends.at[5])
        drain(GH, ends.at[7])
        drain(LO, ends.at[9])
        f_out[...] = FO[...]
        g_out[:KT] = GH[0]
        g_out[KT:] = GH[1]
        loss_out[...] = LO[0:1, 0:1]

    @pl.when(worker)
    def _():
        work(
            fast, co, row, col, xy, zed, xy_peers, z_peers, across, sibling, own, f_out, g_out, loss_out,
            XT, XR, Y8, YM, S, PB, VB, UB, ZB, AA, OWN_B, NA, NB, LA, LB, LBN, XSQ, YSQ, GM, GS, FX, GX, FL, GL, GH, FO, LO, FP, FM, LAM, TOP, RHO, EA, EAR, EB, BADR, BADC,
            hsem, ysem, xsem, asem, nsem, fs, fr, gs, gr, ends,
        )


def work(
    fast, co, row, col, xy, zed, xy_peers, z_peers, across, sibling, own, f_out, g_out, loss_out,
    XT, XR, Y8, YM, S, PB, VB, UB, ZB, AA, OWN_B, NA, NB, LA, LB, LBN, XSQ, YSQ, GM, GS, FX, GX, FL, GL, GH, FO, LO, FP, FM, LAM, TOP, RHO, EA, EAR, EB, BADR, BADC,
    hsem, ysem, xsem, asem, nsem, fs, fr, gs, gr, ends,
):
    other = co["z"] * 4 + across["xl"] * 2
    for n in range(CHUNKS):
        landed = Y8.at[n, pl.ds(other, 2)]
        drain(landed, hsem.at[1 + n])
        for t in z_peers:
            send(landed, landed, ysem.at[0], ysem.at[1 + n], t)

    for copy in own:
        copy.wait()
    own_b = jnp.where(co["xl"] == 0, OWN_B[:KT], OWN_B[KT:]) * LOG2E
    LB[...] = own_b
    NB[xy] = jnp.broadcast_to(full_lse(own_b), (1, 128))
    for t in xy_peers:
        send(NB.at[xy], NB.at[xy], nsem.at[0], nsem.at[1], t)
    drain(AA.at[pl.ds(0, 3)], asem.at[1])
    whole_a = AA[...].reshape(16, 128) * LOG2E
    LA[...] = whole_a
    NA[zed] = jnp.broadcast_to(full_lse(whole_a), (1, 128))
    for t in z_peers:
        send(NA.at[zed], NA.at[zed], nsem.at[2], nsem.at[3], t)

    def set_v(v, first, count):
        for k in range(count):
            at = first + k
            VB[:, at * 128 : (at + 1) * 128] = jnp.broadcast_to(v[k : k + 1, :], (8, 128))

    def over_lanes(peaks, masses):
        peak = jnp.concatenate(peaks, axis=0).T
        mass = jnp.concatenate(masses, axis=0).T
        top = jnp.max(peak, axis=0, keepdims=True)
        return top, top + jnp.log2(jnp.sum(mass * jnp.exp2(peak - top), axis=0, keepdims=True))

    def send_rows(t, h):
        for peer in xy_peers:
            send(FX.at[t, h, xy], FX.at[t, h, xy], fs.at[t], fr.at[t, h], peer)

    scale = 2.0 / F / EPS * LOG2E
    tiles_in = CHUNK // 128
    for n in range(CHUNKS):
        drain(Y8.at[n, pl.ds(0, 29)], ysem.at[1 + n])
        span = slice(n * CHUNK, (n + 1) * CHUNK)
        total = jnp.zeros((16, CHUNK), jnp.float32)
        for q in range(16):
            y = jnp.concatenate(
                [Y8[n, 2 * q].astype(jnp.float32), Y8[n, 2 * q + 1].astype(jnp.float32)], axis=0
            )
            YM[q * 16 : (q + 1) * 16, span] = y.astype(jnp.bfloat16)
            total = total + y * y
        total = jnp.sum(total, axis=0, keepdims=True)
        for k in range(tiles_in):
            at = n * tiles_in + k
            YSQ[at : at + 1, :] = total[:, k * 128 : (k + 1) * 128]
        mine = slice(n * tiles_in, (n + 1) * tiles_in)
        set_v(LB[mine] - YSQ[mine] * (LOG2E / F / EPS), n * tiles_in, tiles_in)

        if n == 0:
            drain(XT.at[pl.ds(0, 31)], xsem.at[1])

        def first_rows(h, _):
            for q in range(4):
                block = pl.ds(pl.multiple_of(h * 512 + q * 128, 128), 128)
                if n:
                    x = XR[block, :]
                else:
                    x = XT[pl.ds(pl.multiple_of(h * 8, 8), 8), :, q * 128 : (q + 1) * 128].reshape(F, 128).T
                    XR[block, :] = x
                inner = jnp.dot(x, YM[:, span], preferred_element_type=jnp.float32) * scale
                S[block, span] = inner
                peaks, masses = [], []
                for r in range(16):
                    at = pl.ds(pl.multiple_of(h * 512 + q * 128 + r * 8, 8), 8)
                    tiles = [
                        inner[r * 8 : (r + 1) * 8, k * 128 : (k + 1) * 128]
                        + VB[:, (n * tiles_in + k) * 128 : (n * tiles_in + k + 1) * 128]
                        for k in range(tiles_in)
                    ]
                    if n:
                        before = FP[at, :]
                        peak = tree(jnp.maximum, tiles + [before])
                        mass = [jnp.exp2(s - peak) for s in tiles] + [FM[at, :] * jnp.exp2(before - peak)]
                    else:
                        peak = tree(jnp.maximum, tiles)
                        mass = [jnp.exp2(s - peak) for s in tiles]
                    mass = tree(jnp.add, mass)
                    if n < CHUNKS - 1:
                        FP[at, :] = peak
                        FM[at, :] = mass
                    peaks.append(peak)
                    masses.append(mass)
                if n == CHUNKS - 1:
                    top, FX[0, h, xy, q : q + 1, :] = over_lanes(peaks, masses)
                    TOP[pl.ds(h * 4 + q, 1), :] = top
            if n == CHUNKS - 1:
                send_rows(0, h)
            return 0

        lax.fori_loop(0, PARTS, first_rows, 0)

    def f_pass(t):
        def part(h, _):
            for q in range(4):
                peaks, masses = [], []
                for r in range(16):
                    at = pl.ds(pl.multiple_of(h * 512 + q * 128 + r * 8, 8), 8)
                    tiles = [S[at, k * 128 : (k + 1) * 128] + VB[:, k * 128 : (k + 1) * 128] for k in range(KT)]
                    peak = functools.reduce(jnp.maximum, tiles)
                    peaks.append(peak)
                    masses.append(functools.reduce(jnp.add, [jnp.exp2(s - peak) for s in tiles]))
                FX[t, h, xy, q : q + 1, :] = over_lanes(peaks, masses)[1]
            send_rows(t, h)
            return 0

        lax.fori_loop(0, PARTS, part, 0)

    def swap_columns(t):
        for peer in z_peers:
            send(GX.at[t, zed], GX.at[t, zed], gs.at[t], gr.at[t], peer)
        drain(GX.at[t, pl.ds(0, 7)], gr.at[t])

    def g_pass(t):
        def part(h, _):
            drain(FX.at[t, h, pl.ds(0, 15)], fr.at[t, h])
            rows = pl.ds(pl.multiple_of(h * 4, 4), 4)
            u = LA[rows, :] - (lse(FX[t, h]) - jnp.where(t == 0, LBN[...], 0.0))
            for q in range(4):
                UB[q * 128 : (q + 1) * 128, :] = jnp.broadcast_to(u[q : q + 1, :], (128, 128)).T
            for k0 in range(0, KT, GROUP):
                span = slice(k0 * 128, (k0 + GROUP) * 128)
                peaks = [GM[:, k * 128 : (k + 1) * 128] for k in range(k0, k0 + GROUP)]
                masses = [GS[:, k * 128 : (k + 1) * 128] for k in range(k0, k0 + GROUP)]
                for q in range(4):
                    us = [UB[q * 128 + r * 8 : q * 128 + r * 8 + 8, :] for r in range(16)]
                    for k in range(GROUP):
                        lanes = slice((k0 + k) * 128, (k0 + k + 1) * 128)
                        tiles = [
                            S[pl.ds(pl.multiple_of(h * 512 + q * 128 + r * 8, 8), 8), lanes] + us[r]
                            for r in range(16)
                        ]
                        peak = functools.reduce(jnp.maximum, tiles + [peaks[k]])
                        mass = functools.reduce(jnp.add, [jnp.exp2(s - peak) for s in tiles])
                        masses[k] = mass + masses[k] * jnp.exp2(peaks[k] - peak)
                        peaks[k] = peak
                for k in range(GROUP):
                    lanes = slice((k0 + k) * 128, (k0 + k + 1) * 128)
                    GM[:, lanes] = peaks[k]
                    GS[:, lanes] = masses[k]
            return 0

        GM[...] = jnp.full(GM.shape, -jnp.inf, jnp.float32)
        GS[...] = jnp.zeros(GS.shape, jnp.float32)
        lax.fori_loop(0, PARTS, part, 0)
        for k in range(KT):
            lanes = slice(k * 128, (k + 1) * 128)
            peak = GM[:, lanes]
            top = jnp.max(peak, axis=0, keepdims=True)
            mass = jnp.sum(GS[:, lanes] * jnp.exp2(peak - top), axis=0, keepdims=True)
            GX[t, zed, k : k + 1, :] = top + jnp.log2(mass)
        swap_columns(t)

    def fast_rows(t):
        def part(h, _):
            for q in range(4):
                sums = []
                for r in range(16):
                    at = pl.ds(pl.multiple_of(h * 512 + q * 128 + r * 8, 8), 8)
                    sums.append(
                        tree(
                            jnp.add,
                            [PB[at, k * 128 : (k + 1) * 128] * VB[:, k * 128 : (k + 1) * 128] for k in range(KT)],
                        )
                    )
                total = jnp.sum(jnp.concatenate(sums, axis=0).T, axis=0, keepdims=True)
                FX[t, h, xy, q : q + 1, :] = total * RHO[pl.ds(h * 4 + q, 1), :]
            send_rows(t, h)
            return 0

        lax.fori_loop(0, PARTS, part, 0)

    def fast_columns(t, first):
        def part(h, _):
            drain(FX.at[t, h, pl.ds(0, 15)], fr.at[t, h])
            rows = pl.ds(pl.multiple_of(h * 4, 4), 4)
            if first:
                lam = lse(FX[t, h])
                LAM[rows, :] = lam - LBN[...]
                rho = jnp.exp2(TOP[rows, :] - lam)
                RHO[rows, :] = rho
                zs = EA[rows, :] * rho
                EAR[rows, :] = zs
            else:
                total = jnp.sum(FX[t, h], axis=0)
                zs = EAR[rows, :] / total
                good = jnp.logical_and(total >= 2.0**-35, EA[rows, :] <= 2.0**20 * total)
                BADR[...] = jnp.maximum(BADR[...], jnp.where(good, 0.0, 1.0))
            for q in range(4):
                ZB[q * 128 : (q + 1) * 128, :] = jnp.broadcast_to(zs[q : q + 1, :], (128, 128)).T
            for k0 in range(0, KT, GROUP):
                sums = [GS[:, k * 128 : (k + 1) * 128] for k in range(k0, k0 + GROUP)]
                for q in range(4):
                    at = [q * 128 + r * 8 for r in range(16)]
                    z = [ZB[i : i + 8, :] for i in at]
                    for k in range(GROUP):
                        lanes = slice((k0 + k) * 128, (k0 + k + 1) * 128)
                        here = [pl.ds(pl.multiple_of(h * 512 + i, 8), 8) for i in at]
                        sums[k] = sums[k] + tree(jnp.add, [PB[here[r], lanes] * z[r] for r in range(16)])
                for k in range(GROUP):
                    GS[:, (k0 + k) * 128 : (k0 + k + 1) * 128] = sums[k]
            return 0

        GS[...] = jnp.zeros(GS.shape, jnp.float32)
        lax.fori_loop(0, PARTS, part, 0)
        for k in range(KT):
            GX[t, zed, k : k + 1, :] = jnp.sum(GS[:, k * 128 : (k + 1) * 128], axis=0, keepdims=True)
        swap_columns(t)
        total = jnp.sum(GX[t], axis=0)
        w = EB[...] / total
        good = jnp.logical_and(total >= 2.0**-65, w <= 2.0**45)
        BADC[...] = jnp.maximum(BADC[...], jnp.where(good, 0.0, 1.0))
        return w

    def exponentials(h, _):
        tops = TOP[pl.ds(pl.multiple_of(h * 4, 4), 4), :]
        for q in range(4):
            UB[q * 128 : (q + 1) * 128, :] = jnp.broadcast_to(tops[q : q + 1, :], (128, 128)).T
        for q in range(4):
            for k in range(KT):
                lanes = slice(k * 128, (k + 1) * 128)
                at = [q * 128 + r * 8 for r in range(16)]
                here = [pl.ds(pl.multiple_of(h * 512 + i, 8), 8) for i in at]
                p = [S[here[r], lanes] + VB[:, lanes] for r in range(16)]
                p = [jnp.exp2(p[r] - UB[at[r] : at[r] + 8, :]) for r in range(16)]
                for r in range(16):
                    PB[here[r], lanes] = p[r]
        return 0

    if fast:
        lax.fori_loop(0, PARTS, exponentials, 0)
    for p in range(16):
        x = XT[p // 4 * 8 : p // 4 * 8 + 8, :, pl.ds((p % 4) * 128, 128)].reshape(F, 128).astype(jnp.float32)
        XSQ[p : p + 1, :] = jnp.sum(x * x, axis=0, keepdims=True)

    drain(NB.at[pl.ds(0, 15)], nsem.at[1])
    drain(NA.at[pl.ds(0, 7)], nsem.at[3])
    log_b_norm = lse(NB[...])
    log_a_norm = lse(NA[...])
    LB[...] = LB[...] - log_b_norm
    LA[...] = LA[...] - log_a_norm
    LBN[...] = log_b_norm
    EA[...] = jnp.exp2(LA[...])
    EB[...] = jnp.exp2(LB[...])
    BADR[...] = jnp.zeros(BADR.shape, jnp.float32)
    BADC[...] = jnp.zeros(BADC.shape, jnp.float32)
    last = ITERS - 1

    if fast:
        set_v(fast_columns(0, True), 0, KT)
        fast_rows(1)

        def iteration(t, _):
            w = fast_columns(t, False)

            @pl.when(t < last)
            def _():
                set_v(w, 0, KT)
                fast_rows(t + 1)

            return 0

        lax.fori_loop(1, ITERS, iteration, 0)
        g = (LB[...] - jnp.log2(jnp.sum(GX[last], axis=0))) * (EPS * LN2)
        lam = jnp.concatenate([jnp.sum(FX[last, h], axis=0) for h in range(PARTS)], axis=0)
        lam = LAM[...] + jnp.log2(lam)
    else:

        def iteration(t, _):
            g_pass(t)

            @pl.when(t < last)
            def _():
                set_v(LB[...] - lse(GX[t]), 0, KT)
                f_pass(t + 1)

            return 0

        lax.fori_loop(0, ITERS, iteration, 0)
        g = YSQ[...] * (1.0 / F) - lse(GX[last]) * (EPS * LN2)
        lam = jnp.concatenate([lse(FX[last, h]) for h in range(PARTS)], axis=0)
    f = XSQ[...] * (1.0 / F) - lam * (EPS * LN2)

    bad = jnp.maximum(jnp.max(BADR[...], axis=0, keepdims=True), jnp.max(BADC[...], axis=0, keepdims=True)) > 0.0
    GL[xy] = jnp.where(bad, jnp.nan, jnp.sum(jnp.exp2(LB[...]) * g, axis=0, keepdims=True))
    GH[co["xl"]] = g
    for t in xy_peers:
        send(GL.at[xy], GL.at[xy], ends.at[0], ends.at[1], t)
    send(GH.at[co["xl"]], GH.at[co["xl"]], ends.at[2], ends.at[3], across)
    FL[zed] = jnp.where(bad, jnp.nan, jnp.sum(jnp.exp2(LA[...]) * f, axis=0, keepdims=True))
    for t in z_peers:
        send(FL.at[zed], FL.at[zed], ends.at[10], ends.at[11], t)
    FO[...] = jnp.where(co["xl"] == 0, f[0:4], f[8:12])
    send(FO, FO, ends.at[4], ends.at[5], sibling)
    f_out[...] = jnp.where(co["xl"] == 0, f[4:8], f[12:16])
    drain(GH.at[0], ends.at[3])
    send(GH, GH, ends.at[6], ends.at[7], sibling)
    g_out[:KT] = GH[0]
    g_out[KT:] = GH[1]
    drain(FL.at[pl.ds(0, 7)], ends.at[11])
    drain(GL.at[pl.ds(0, 15)], ends.at[1])
    loss = jnp.sum(jnp.sum(FL[...], axis=0), axis=(0, 1), keepdims=True) + jnp.sum(
        jnp.sum(GL[...], axis=0), axis=(0, 1), keepdims=True
    )
    LO[...] = jnp.broadcast_to(loss, (1, 128))
    send(LO, LO, ends.at[8], ends.at[9], sibling)
    loss_out[...] = loss

    drain(GL.at[pl.ds(0, 15)], ends.at[0])
    drain(GH.at[0], ends.at[2])
    drain(FO, ends.at[4])
    drain(GH, ends.at[6])
    drain(LO, ends.at[8])
    drain(FL.at[pl.ds(0, 7)], ends.at[10])
    for t in range(ITERS):
        drain(FX.at[t, :, pl.ds(0, 15)], fs.at[t])
        drain(GX.at[t, pl.ds(0, 7)], gs.at[t])
    drain(NB.at[pl.ds(0, 15)], nsem.at[0])
    drain(NA.at[pl.ds(0, 7)], nsem.at[2])
    drain(Y8.at[0, pl.ds(0, CHUNKS)], hsem.at[0])
    drain(Y8.at[:, pl.ds(0, 21)], ysem.at[0])
    drain(XT.at[pl.ds(0, 15)], xsem.at[0])
    drain(AA.at[0], asem.at[0])


def whole(fast, x_feat, y_feat, a_logits, b_logits):
    f32, bf16 = jnp.float32, jnp.bfloat16
    vmem = pl.BlockSpec(memory_space=pltpu.VMEM)
    hbm = pl.BlockSpec(memory_space=pltpu.HBM)
    dma = pltpu.SemaphoreType.DMA
    f, g, loss = pl.pallas_call(
        functools.partial(kernel, fast),
        out_shape=(
            jax.ShapeDtypeStruct((4, 128), f32),
            jax.ShapeDtypeStruct((24, 128), f32),
            jax.ShapeDtypeStruct((1, 1), f32),
        ),
        in_specs=[hbm, hbm, hbm, hbm],
        out_specs=(vmem, vmem, vmem),
        scratch_shapes=[
            pltpu.VMEM((32, 32, 512), bf16),
            pltpu.VMEM((ROWS, F), bf16),
            pltpu.VMEM((CHUNKS, 32, 8, CHUNK), bf16),
            pltpu.VMEM((F, COLS), bf16),
            pltpu.VMEM((ROWS, COLS), f32),
            pltpu.VMEM((ROWS, COLS) if fast else (8, 128), f32),
            pltpu.VMEM((8, COLS), f32),
            pltpu.VMEM((512, 128), f32),
            pltpu.VMEM((512, 128), f32),
            pltpu.VMEM((4, 4, 128), f32),
            pltpu.VMEM((24, 128), f32),
            pltpu.VMEM((8, 1, 128), f32),
            pltpu.VMEM((16, 1, 128), f32),
            pltpu.VMEM((16, 128), f32),
            pltpu.VMEM((KT, 128), f32),
            pltpu.VMEM((1, 128), f32),
            pltpu.VMEM((16, 128), f32),
            pltpu.VMEM((KT, 128), f32),
            pltpu.VMEM((8, COLS), f32),
            pltpu.VMEM((8, COLS), f32),
            pltpu.VMEM((ITERS, PARTS, 16, 4, 128), f32),
            pltpu.VMEM((ITERS, 8, KT, 128), f32),
            pltpu.VMEM((8, 1, 128), f32),
            pltpu.VMEM((16, 1, 128), f32),
            pltpu.VMEM((2, KT, 128), f32),
            pltpu.VMEM((4, 128), f32),
            pltpu.VMEM((1, 128), f32),
            pltpu.VMEM((ROWS, 128), f32),
            pltpu.VMEM((ROWS, 128), f32),
            pltpu.VMEM((16, 128), f32),
            pltpu.VMEM((16, 128), f32),
            pltpu.VMEM((16, 128), f32),
            pltpu.VMEM((16, 128), f32),
            pltpu.VMEM((16, 128), f32),
            pltpu.VMEM((KT, 128), f32),
            pltpu.VMEM((4, 128), f32),
            pltpu.VMEM((KT, 128), f32),
            dma((1 + CHUNKS,)),
            dma((1 + CHUNKS,)),
            dma((2,)),
            dma((2,)),
            dma((4,)),
            dma((3 + CHUNKS,)),
            dma((ITERS,)),
            dma((ITERS, PARTS)),
            dma((ITERS,)),
            dma((ITERS,)),
            dma((12,)),
        ],
        compiler_params=pltpu.CompilerParams(
            collective_id=0 if fast else 1, has_side_effects=True, vmem_limit_bytes=64 * 1024 * 1024 - 24 * 1024
        ),
        name="sinkhorn" if fast else "sinkhorn_log",
    )(x_feat.T, y_feat.T, a_logits.reshape(4, 128), b_logits.reshape(24, 128))
    return f.reshape(512), g.reshape(3072), loss.reshape(())


def body(x_feat, y_feat, a_logits, b_logits):
    args = x_feat, y_feat, a_logits, b_logits
    f, g, loss = whole(True, *args)
    return lax.cond(jnp.isfinite(loss), lambda *_: (f, g, loss), functools.partial(whole, False), *args)


def solution(mesh):
    in_specs = (P("row", "col"), P("col", "row"), P("row"), P("col"))
    out_specs = (P("row"), P("col"), P())
    return jax.shard_map(body, mesh=mesh, in_specs=in_specs, out_specs=out_specs, check_vma=False)
```

```python
import functools
import math

import jax
import jax.numpy as jnp
from jax import lax
from jax.experimental import pallas as pl
from jax.experimental.pallas import tpu as pltpu
from jax.sharding import PartitionSpec as P

ITERS = 4
EPS = 0.05
LN2 = math.log(2.0)
LOG2E = 1.0 / LN2
F = 256
SIZE = {"z": 8, "xl": 2, "c": 2, "y": 4, "xh": 2}
MESH = pl.DeviceIdType.MESH
ROWS, COLS = 2048, 1536
PARTS = 4
KT = COLS // 128
CHUNKS = 2
CHUNK = COLS // CHUNKS
GROUP = 4


def coords():
    r = lax.axis_index("row")
    k = lax.axis_index("col")
    return {"z": r // 4, "xl": lax.rem(r // 2, 2), "c": lax.rem(r, 2), "y": k // 2, "xh": lax.rem(k, 2)}


def device(o):
    return ((o["z"] * 2 + o["xl"]) * 2 + o["c"], o["y"] * 2 + o["xh"])


def hops(o):
    z, y = o.get("z", 0), o.get("y", 0)
    return min(z, 8 - z) + min(y, 4 - y) + 2 * o.get("xh", 0) + o.get("xl", 0)


def offsets(names):
    out = [{}]
    for n in names:
        out = [{**o, n: d} for o in out for d in range(SIZE[n])]
    return sorted([o for o in out if any(o.values())], key=lambda o: -hops(o))


def at_offset(co, o, c):
    return {n: (lax.rem(co[n] + o[n], SIZE[n]) if o.get(n, 0) else co[n]) for n in co} | {"c": c}


def send(src, dst, ssem, rsem, target):
    pltpu.make_async_remote_copy(
        src_ref=src, dst_ref=dst, send_sem=ssem, recv_sem=rsem, device_id=device(target), device_id_type=MESH
    ).start()


def drain(ref, sem):
    pltpu.make_async_copy(ref, ref, sem).wait()


def lse(x):
    peak = jnp.max(x, axis=0)
    return peak + jnp.log2(jnp.sum(jnp.exp2(x - peak[None]), axis=0))


def tree(op, xs):
    while len(xs) > 1:
        xs = [op(xs[i], xs[i + 1]) if i + 1 < len(xs) else xs[i] for i in range(0, len(xs), 2)]
    return xs[0]


def full_lse(x):
    peak = jnp.max(x, axis=(0, 1), keepdims=True)
    return peak + jnp.log2(jnp.sum(jnp.exp2(x - peak), axis=(0, 1), keepdims=True))


def kernel(
    fast, xt, yt, a, b, f_out, g_out, loss_out,
    XT, XR, Y8, YM, S, PB, VB, UB, ZB, AA, OWN_B, NA, NB, LA, LB, LBN, XSQ, YSQ, GM, GS, FX, GX, FL, GL, GH, FO, FP, FM, LAM, TOP, RHO, EA, EAR, EB, BADR, BADC,
    hsem, ysem, xsem, asem, nsem, local, fs, fr, gs, gr, ends,
):
    co = coords()
    row, col = device(co)
    c = co["c"]
    xy = (co["xh"] * 2 + co["xl"]) * 4 + co["y"]
    zed = co["z"]
    xy_offsets = offsets(["y", "xh", "xl"])
    z_offsets = offsets(["z"])
    xy_peers = [at_offset(co, o, 1) for o in xy_offsets]
    z_peers = [at_offset(co, o, 1) for o in z_offsets]
    across = at_offset(co, {"xl": 1}, 1)
    sibling = at_offset(co, {}, 1 - c)
    worker = c == 1
    helper = c == 0

    barrier = pltpu.get_barrier_semaphore()

    def greet(t):
        pl.semaphore_signal(barrier, inc=1, device_id=device(t), device_id_type=MESH)

    @pl.when(worker)
    def _():
        for o in sorted(xy_offsets + z_offsets, key=lambda o: -hops(o)):
            greet(at_offset(co, o, 0))
            greet(at_offset(co, o, 1))
        greet(sibling)

    @pl.when(helper)
    def _():
        greet(sibling)

    def cut(xl, n):
        return yt.at[:, pl.ds(pl.multiple_of(xl * COLS + n * CHUNK, 128), CHUNK)]

    own = [
        pltpu.make_async_copy(xt, XT.at[row % 4 * 8 + col], local.at[0]),
        pltpu.make_async_copy(a, AA.at[row % 4], local.at[1]),
        pltpu.make_async_copy(b, OWN_B, local.at[2]),
    ] + [pltpu.make_async_copy(cut(co["xl"], n), Y8.at[n, row], local.at[3 + n]) for n in range(CHUNKS)]

    @pl.when(worker)
    def _():
        for copy in own:
            copy.start()

    pl.semaphore_wait(barrier, len(xy_offsets) + len(z_offsets) + 1)

    send(a, AA.at[row % 4], asem.at[0], asem.at[1], across)

    @pl.when(helper)
    def _():
        send(a, AA.at[row % 4], asem.at[0], asem.at[1], sibling)

    for n in range(CHUNKS):
        send(cut(across["xl"], n), Y8.at[n, row], hsem.at[0], hsem.at[1 + n], across)
    for n in range(CHUNKS):
        for t in z_peers:
            send(cut(co["xl"], n), Y8.at[n, row], ysem.at[0], ysem.at[1 + n], t)
    for t in xy_peers:
        send(xt, XT.at[row % 4 * 8 + col], xsem.at[0], xsem.at[1], t)

    @pl.when(helper)
    def _():
        for n in range(CHUNKS):
            send(cut(co["xl"], n), Y8.at[n, row], ysem.at[0], ysem.at[1 + n], sibling)
        send(xt, XT.at[row % 4 * 8 + col], xsem.at[0], xsem.at[1], sibling)
        drain(Y8.at[0, pl.ds(0, CHUNKS)], hsem.at[0])
        drain(Y8.at[0, pl.ds(0, CHUNKS * 8)], ysem.at[0])
        drain(XT.at[pl.ds(0, 16)], xsem.at[0])
        drain(AA.at[pl.ds(0, 2)], asem.at[0])
        drain(FO, ends.at[5])
        drain(GH, ends.at[7])
        drain(GL, ends.at[1])
        drain(FL, ends.at[11])
        f_out[...] = FO[...]
        g_out[:KT] = GH[0]
        g_out[KT:] = GH[1]
        loss_out[...] = objective(FL, GL)

    @pl.when(worker)
    def _():
        work(
            fast, co, row, col, xy, zed, xy_peers, z_peers, across, sibling, own, f_out, g_out, loss_out,
            XT, XR, Y8, YM, S, PB, VB, UB, ZB, AA, OWN_B, NA, NB, LA, LB, LBN, XSQ, YSQ, GM, GS, FX, GX, FL, GL, GH, FO, FP, FM, LAM, TOP, RHO, EA, EAR, EB, BADR, BADC,
            hsem, ysem, xsem, asem, nsem, fs, fr, gs, gr, ends,
        )


def objective(FL, GL):
    return jnp.sum(jnp.sum(FL[...], axis=0), axis=(0, 1), keepdims=True) + jnp.sum(
        jnp.sum(GL[...], axis=0), axis=(0, 1), keepdims=True
    )


def work(
    fast, co, row, col, xy, zed, xy_peers, z_peers, across, sibling, own, f_out, g_out, loss_out,
    XT, XR, Y8, YM, S, PB, VB, UB, ZB, AA, OWN_B, NA, NB, LA, LB, LBN, XSQ, YSQ, GM, GS, FX, GX, FL, GL, GH, FO, FP, FM, LAM, TOP, RHO, EA, EAR, EB, BADR, BADC,
    hsem, ysem, xsem, asem, nsem, fs, fr, gs, gr, ends,
):
    other = co["z"] * 4 + across["xl"] * 2
    for n in range(CHUNKS):
        landed = Y8.at[n, pl.ds(other, 2)]
        drain(landed, hsem.at[1 + n])
        for t in z_peers:
            send(landed, landed, ysem.at[0], ysem.at[1 + n], t)

    for copy in own:
        copy.wait()
    own_b = jnp.where(co["xl"] == 0, OWN_B[:KT], OWN_B[KT:]) * LOG2E
    LB[...] = own_b
    NB[xy] = jnp.broadcast_to(full_lse(own_b), (1, 128))
    for t in xy_peers:
        send(NB.at[xy], NB.at[xy], nsem.at[0], nsem.at[1], t)
    drain(AA.at[pl.ds(0, 3)], asem.at[1])
    whole_a = AA[...].reshape(16, 128) * LOG2E
    LA[...] = whole_a
    NA[zed] = jnp.broadcast_to(full_lse(whole_a), (1, 128))
    for t in z_peers:
        send(NA.at[zed], NA.at[zed], nsem.at[2], nsem.at[3], t)

    def set_v(v, first, count):
        for k in range(count):
            at = first + k
            VB[:, at * 128 : (at + 1) * 128] = jnp.broadcast_to(v[k : k + 1, :], (8, 128))

    def over_lanes(peaks, masses):
        peak = jnp.concatenate(peaks, axis=0).T
        mass = jnp.concatenate(masses, axis=0).T
        top = jnp.max(peak, axis=0, keepdims=True)
        return top, top + jnp.log2(jnp.sum(mass * jnp.exp2(peak - top), axis=0, keepdims=True))

    def send_rows(t, h):
        for peer in xy_peers:
            send(FX.at[t, h, xy], FX.at[t, h, xy], fs.at[t], fr.at[t, h], peer)

    scale = 2.0 / F / EPS * LOG2E
    tiles_in = CHUNK // 128
    for n in range(CHUNKS):
        drain(Y8.at[n, pl.ds(0, 29)], ysem.at[1 + n])
        span = slice(n * CHUNK, (n + 1) * CHUNK)
        total = jnp.zeros((16, CHUNK), jnp.float32)
        for q in range(16):
            y = jnp.concatenate(
                [Y8[n, 2 * q].astype(jnp.float32), Y8[n, 2 * q + 1].astype(jnp.float32)], axis=0
            )
            YM[q * 16 : (q + 1) * 16, span] = y.astype(jnp.bfloat16)
            total = total + y * y
        total = jnp.sum(total, axis=0, keepdims=True)
        for k in range(tiles_in):
            at = n * tiles_in + k
            YSQ[at : at + 1, :] = total[:, k * 128 : (k + 1) * 128]
        mine = slice(n * tiles_in, (n + 1) * tiles_in)
        set_v(LB[mine] - YSQ[mine] * (LOG2E / F / EPS), n * tiles_in, tiles_in)

        if n == 0:
            drain(XT.at[pl.ds(0, 31)], xsem.at[1])

        def first_rows(h, _):
            for q in range(4):
                block = pl.ds(pl.multiple_of(h * 512 + q * 128, 128), 128)
                if n:
                    x = XR[block, :]
                else:
                    x = XT[pl.ds(pl.multiple_of(h * 8, 8), 8), :, q * 128 : (q + 1) * 128].reshape(F, 128).T
                    XR[block, :] = x
                inner = jnp.dot(x, YM[:, span], preferred_element_type=jnp.float32) * scale
                S[block, span] = inner
                peaks, masses = [], []
                for r in range(16):
                    at = pl.ds(pl.multiple_of(h * 512 + q * 128 + r * 8, 8), 8)
                    tiles = [
                        inner[r * 8 : (r + 1) * 8, k * 128 : (k + 1) * 128]
                        + VB[:, (n * tiles_in + k) * 128 : (n * tiles_in + k + 1) * 128]
                        for k in range(tiles_in)
                    ]
                    if n:
                        before = FP[at, :]
                        peak = tree(jnp.maximum, tiles + [before])
                        mass = [jnp.exp2(s - peak) for s in tiles] + [FM[at, :] * jnp.exp2(before - peak)]
                    else:
                        peak = tree(jnp.maximum, tiles)
                        mass = [jnp.exp2(s - peak) for s in tiles]
                    mass = tree(jnp.add, mass)
                    if n < CHUNKS - 1:
                        FP[at, :] = peak
                        FM[at, :] = mass
                    peaks.append(peak)
                    masses.append(mass)
                if n == CHUNKS - 1:
                    top, FX[0, h, xy, q : q + 1, :] = over_lanes(peaks, masses)
                    TOP[pl.ds(h * 4 + q, 1), :] = top
            if n == CHUNKS - 1:
                send_rows(0, h)
            return 0

        lax.fori_loop(0, PARTS, first_rows, 0)

    def f_pass(t):
        def part(h, _):
            for q in range(4):
                peaks, masses = [], []
                for r in range(16):
                    at = pl.ds(pl.multiple_of(h * 512 + q * 128 + r * 8, 8), 8)
                    tiles = [S[at, k * 128 : (k + 1) * 128] + VB[:, k * 128 : (k + 1) * 128] for k in range(KT)]
                    peak = functools.reduce(jnp.maximum, tiles)
                    peaks.append(peak)
                    masses.append(functools.reduce(jnp.add, [jnp.exp2(s - peak) for s in tiles]))
                FX[t, h, xy, q : q + 1, :] = over_lanes(peaks, masses)[1]
            send_rows(t, h)
            return 0

        lax.fori_loop(0, PARTS, part, 0)

    def swap_columns(t):
        for peer in z_peers:
            send(GX.at[t, zed], GX.at[t, zed], gs.at[t], gr.at[t], peer)
        drain(GX.at[t, pl.ds(0, 7)], gr.at[t])

    def g_pass(t):
        def part(h, _):
            drain(FX.at[t, h, pl.ds(0, 15)], fr.at[t, h])
            rows = pl.ds(pl.multiple_of(h * 4, 4), 4)
            u = LA[rows, :] - (lse(FX[t, h]) - jnp.where(t == 0, LBN[...], 0.0))
            for q in range(4):
                UB[q * 128 : (q + 1) * 128, :] = jnp.broadcast_to(u[q : q + 1, :], (128, 128)).T
            for k0 in range(0, KT, GROUP):
                span = slice(k0 * 128, (k0 + GROUP) * 128)
                peaks = [GM[:, k * 128 : (k + 1) * 128] for k in range(k0, k0 + GROUP)]
                masses = [GS[:, k * 128 : (k + 1) * 128] for k in range(k0, k0 + GROUP)]
                for q in range(4):
                    us = [UB[q * 128 + r * 8 : q * 128 + r * 8 + 8, :] for r in range(16)]
                    for k in range(GROUP):
                        lanes = slice((k0 + k) * 128, (k0 + k + 1) * 128)
                        tiles = [
                            S[pl.ds(pl.multiple_of(h * 512 + q * 128 + r * 8, 8), 8), lanes] + us[r]
                            for r in range(16)
                        ]
                        peak = functools.reduce(jnp.maximum, tiles + [peaks[k]])
                        mass = functools.reduce(jnp.add, [jnp.exp2(s - peak) for s in tiles])
                        masses[k] = mass + masses[k] * jnp.exp2(peaks[k] - peak)
                        peaks[k] = peak
                for k in range(GROUP):
                    lanes = slice((k0 + k) * 128, (k0 + k + 1) * 128)
                    GM[:, lanes] = peaks[k]
                    GS[:, lanes] = masses[k]
            return 0

        GM[...] = jnp.full(GM.shape, -jnp.inf, jnp.float32)
        GS[...] = jnp.zeros(GS.shape, jnp.float32)
        lax.fori_loop(0, PARTS, part, 0)
        for k in range(KT):
            lanes = slice(k * 128, (k + 1) * 128)
            peak = GM[:, lanes]
            top = jnp.max(peak, axis=0, keepdims=True)
            mass = jnp.sum(GS[:, lanes] * jnp.exp2(peak - top), axis=0, keepdims=True)
            GX[t, zed, k : k + 1, :] = top + jnp.log2(mass)
        swap_columns(t)

    def fast_rows(t):
        def part(h, _):
            for q in range(4):
                sums = []
                for r in range(16):
                    at = pl.ds(pl.multiple_of(h * 512 + q * 128 + r * 8, 8), 8)
                    sums.append(
                        tree(
                            jnp.add,
                            [PB[at, k * 128 : (k + 1) * 128] * VB[:, k * 128 : (k + 1) * 128] for k in range(KT)],
                        )
                    )
                total = jnp.sum(jnp.concatenate(sums, axis=0).T, axis=0, keepdims=True)
                FX[t, h, xy, q : q + 1, :] = total * RHO[pl.ds(h * 4 + q, 1), :]
            send_rows(t, h)
            return 0

        lax.fori_loop(0, PARTS, part, 0)

    def fast_columns(t, first):
        def part(h, _):
            drain(FX.at[t, h, pl.ds(0, 15)], fr.at[t, h])
            rows = pl.ds(pl.multiple_of(h * 4, 4), 4)
            if first:
                lam = lse(FX[t, h])
                LAM[rows, :] = lam - LBN[...]
                rho = jnp.exp2(TOP[rows, :] - lam)
                RHO[rows, :] = rho
                zs = EA[rows, :] * rho
                EAR[rows, :] = zs
            else:
                total = jnp.sum(FX[t, h], axis=0)
                zs = EAR[rows, :] / total
                good = jnp.logical_and(total >= 2.0**-35, EA[rows, :] <= 2.0**20 * total)
                BADR[...] = jnp.maximum(BADR[...], jnp.where(good, 0.0, 1.0))
            for q in range(4):
                ZB[q * 128 : (q + 1) * 128, :] = jnp.broadcast_to(zs[q : q + 1, :], (128, 128)).T
            for k0 in range(0, KT, GROUP):
                sums = [GS[:, k * 128 : (k + 1) * 128] for k in range(k0, k0 + GROUP)]
                for q in range(4):
                    at = [q * 128 + r * 8 for r in range(16)]
                    z = [ZB[i : i + 8, :] for i in at]
                    for k in range(GROUP):
                        lanes = slice((k0 + k) * 128, (k0 + k + 1) * 128)
                        here = [pl.ds(pl.multiple_of(h * 512 + i, 8), 8) for i in at]
                        sums[k] = sums[k] + tree(jnp.add, [PB[here[r], lanes] * z[r] for r in range(16)])
                for k in range(GROUP):
                    GS[:, (k0 + k) * 128 : (k0 + k + 1) * 128] = sums[k]
            return 0

        GS[...] = jnp.zeros(GS.shape, jnp.float32)
        lax.fori_loop(0, PARTS, part, 0)
        for k in range(KT):
            GX[t, zed, k : k + 1, :] = jnp.sum(GS[:, k * 128 : (k + 1) * 128], axis=0, keepdims=True)
        swap_columns(t)
        total = jnp.sum(GX[t], axis=0)
        w = EB[...] / total
        good = jnp.logical_and(total >= 2.0**-65, w <= 2.0**45)
        BADC[...] = jnp.maximum(BADC[...], jnp.where(good, 0.0, 1.0))
        return w

    def exponentials(h, _):
        tops = TOP[pl.ds(pl.multiple_of(h * 4, 4), 4), :]
        for q in range(4):
            UB[q * 128 : (q + 1) * 128, :] = jnp.broadcast_to(tops[q : q + 1, :], (128, 128)).T
        for q in range(4):
            for k in range(KT):
                lanes = slice(k * 128, (k + 1) * 128)
                at = [q * 128 + r * 8 for r in range(16)]
                here = [pl.ds(pl.multiple_of(h * 512 + i, 8), 8) for i in at]
                p = [S[here[r], lanes] + VB[:, lanes] for r in range(16)]
                p = [jnp.exp2(p[r] - UB[at[r] : at[r] + 8, :]) for r in range(16)]
                for r in range(16):
                    PB[here[r], lanes] = p[r]
        return 0

    if fast:
        lax.fori_loop(0, PARTS, exponentials, 0)
    for p in range(16):
        x = XT[p // 4 * 8 : p // 4 * 8 + 8, :, pl.ds((p % 4) * 128, 128)].reshape(F, 128).astype(jnp.float32)
        XSQ[p : p + 1, :] = jnp.sum(x * x, axis=0, keepdims=True)

    drain(NB.at[pl.ds(0, 15)], nsem.at[1])
    drain(NA.at[pl.ds(0, 7)], nsem.at[3])
    log_b_norm = lse(NB[...])
    log_a_norm = lse(NA[...])
    LB[...] = LB[...] - log_b_norm
    LA[...] = LA[...] - log_a_norm
    LBN[...] = log_b_norm
    EA[...] = jnp.exp2(LA[...])
    EB[...] = jnp.exp2(LB[...])
    BADR[...] = jnp.zeros(BADR.shape, jnp.float32)
    BADC[...] = jnp.zeros(BADC.shape, jnp.float32)
    last = ITERS - 1

    if fast:
        set_v(fast_columns(0, True), 0, KT)
        fast_rows(1)

        def iteration(t, _):
            w = fast_columns(t, False)

            @pl.when(t < last)
            def _():
                set_v(w, 0, KT)
                fast_rows(t + 1)

            return 0

        lax.fori_loop(1, ITERS, iteration, 0)
        g = (LB[...] - jnp.log2(jnp.sum(GX[last], axis=0))) * (EPS * LN2)
        lam = jnp.concatenate([jnp.sum(FX[last, h], axis=0) for h in range(PARTS)], axis=0)
        lam = LAM[...] + jnp.log2(lam)
    else:

        def iteration(t, _):
            g_pass(t)

            @pl.when(t < last)
            def _():
                set_v(LB[...] - lse(GX[t]), 0, KT)
                f_pass(t + 1)

            return 0

        lax.fori_loop(0, ITERS, iteration, 0)
        g = YSQ[...] * (1.0 / F) - lse(GX[last]) * (EPS * LN2)
        lam = jnp.concatenate([lse(FX[last, h]) for h in range(PARTS)], axis=0)
    f = XSQ[...] * (1.0 / F) - lam * (EPS * LN2)

    bad = jnp.maximum(jnp.max(BADR[...], axis=0, keepdims=True), jnp.max(BADC[...], axis=0, keepdims=True)) > 0.0
    GL[xy] = jnp.where(bad, jnp.nan, jnp.sum(jnp.exp2(LB[...]) * g, axis=0, keepdims=True))
    GH[co["xl"]] = g
    for t in xy_peers:
        send(GL.at[xy], GL.at[xy], ends.at[0], ends.at[1], t)
        send(GL.at[xy], GL.at[xy], ends.at[8], ends.at[1], t | {"c": 0})
    send(GL.at[xy], GL.at[xy], ends.at[8], ends.at[1], sibling)
    send(GH.at[co["xl"]], GH.at[co["xl"]], ends.at[2], ends.at[3], across)
    FL[zed] = jnp.where(bad, jnp.nan, jnp.sum(jnp.exp2(LA[...]) * f, axis=0, keepdims=True))
    for t in z_peers:
        send(FL.at[zed], FL.at[zed], ends.at[10], ends.at[11], t)
        send(FL.at[zed], FL.at[zed], ends.at[9], ends.at[11], t | {"c": 0})
    send(FL.at[zed], FL.at[zed], ends.at[9], ends.at[11], sibling)
    FO[...] = jnp.where(co["xl"] == 0, f[0:4], f[8:12])
    send(FO, FO, ends.at[4], ends.at[5], sibling)
    f_out[...] = jnp.where(co["xl"] == 0, f[4:8], f[12:16])
    drain(GH.at[0], ends.at[3])
    send(GH, GH, ends.at[6], ends.at[7], sibling)
    g_out[:KT] = GH[0]
    g_out[KT:] = GH[1]
    drain(FL.at[pl.ds(0, 7)], ends.at[11])
    drain(GL.at[pl.ds(0, 15)], ends.at[1])
    loss_out[...] = objective(FL, GL)

    drain(GL.at[pl.ds(0, 15)], ends.at[0])
    drain(GH.at[0], ends.at[2])
    drain(FO, ends.at[4])
    drain(GH, ends.at[6])
    drain(GL, ends.at[8])
    drain(FL, ends.at[9])
    drain(FL.at[pl.ds(0, 7)], ends.at[10])
    for t in range(ITERS):
        drain(FX.at[t, :, pl.ds(0, 15)], fs.at[t])
        drain(GX.at[t, pl.ds(0, 7)], gs.at[t])
    drain(NB.at[pl.ds(0, 15)], nsem.at[0])
    drain(NA.at[pl.ds(0, 7)], nsem.at[2])
    drain(Y8.at[0, pl.ds(0, CHUNKS)], hsem.at[0])
    drain(Y8.at[:, pl.ds(0, 21)], ysem.at[0])
    drain(XT.at[pl.ds(0, 15)], xsem.at[0])
    drain(AA.at[0], asem.at[0])


def whole(fast, x_feat, y_feat, a_logits, b_logits):
    f32, bf16 = jnp.float32, jnp.bfloat16
    vmem = pl.BlockSpec(memory_space=pltpu.VMEM)
    hbm = pl.BlockSpec(memory_space=pltpu.HBM)
    dma = pltpu.SemaphoreType.DMA
    f, g, loss = pl.pallas_call(
        functools.partial(kernel, fast),
        out_shape=(
            jax.ShapeDtypeStruct((4, 128), f32),
            jax.ShapeDtypeStruct((24, 128), f32),
            jax.ShapeDtypeStruct((1, 1), f32),
        ),
        in_specs=[hbm, hbm, hbm, hbm],
        out_specs=(vmem, vmem, vmem),
        scratch_shapes=[
            pltpu.VMEM((32, 32, 512), bf16),
            pltpu.VMEM((ROWS, F), bf16),
            pltpu.VMEM((CHUNKS, 32, 8, CHUNK), bf16),
            pltpu.VMEM((F, COLS), bf16),
            pltpu.VMEM((ROWS, COLS), f32),
            pltpu.VMEM((ROWS, COLS) if fast else (8, 128), f32),
            pltpu.VMEM((8, COLS), f32),
            pltpu.VMEM((512, 128), f32),
            pltpu.VMEM((512, 128), f32),
            pltpu.VMEM((4, 4, 128), f32),
            pltpu.VMEM((24, 128), f32),
            pltpu.VMEM((8, 1, 128), f32),
            pltpu.VMEM((16, 1, 128), f32),
            pltpu.VMEM((16, 128), f32),
            pltpu.VMEM((KT, 128), f32),
            pltpu.VMEM((1, 128), f32),
            pltpu.VMEM((16, 128), f32),
            pltpu.VMEM((KT, 128), f32),
            pltpu.VMEM((8, COLS), f32),
            pltpu.VMEM((8, COLS), f32),
            pltpu.VMEM((ITERS, PARTS, 16, 4, 128), f32),
            pltpu.VMEM((ITERS, 8, KT, 128), f32),
            pltpu.VMEM((8, 1, 128), f32),
            pltpu.VMEM((16, 1, 128), f32),
            pltpu.VMEM((2, KT, 128), f32),
            pltpu.VMEM((4, 128), f32),
            pltpu.VMEM((ROWS, 128), f32),
            pltpu.VMEM((ROWS, 128), f32),
            pltpu.VMEM((16, 128), f32),
            pltpu.VMEM((16, 128), f32),
            pltpu.VMEM((16, 128), f32),
            pltpu.VMEM((16, 128), f32),
            pltpu.VMEM((16, 128), f32),
            pltpu.VMEM((KT, 128), f32),
            pltpu.VMEM((4, 128), f32),
            pltpu.VMEM((KT, 128), f32),
            dma((1 + CHUNKS,)),
            dma((1 + CHUNKS,)),
            dma((2,)),
            dma((2,)),
            dma((4,)),
            dma((3 + CHUNKS,)),
            dma((ITERS,)),
            dma((ITERS, PARTS)),
            dma((ITERS,)),
            dma((ITERS,)),
            dma((12,)),
        ],
        compiler_params=pltpu.CompilerParams(
            collective_id=0 if fast else 1, has_side_effects=True, vmem_limit_bytes=64 * 1024 * 1024 - 24 * 1024
        ),
        name="sinkhorn" if fast else "sinkhorn_log",
    )(x_feat.T, y_feat.T, a_logits.reshape(4, 128), b_logits.reshape(24, 128))
    return f.reshape(512), g.reshape(3072), loss.reshape(())


def body(x_feat, y_feat, a_logits, b_logits):
    args = x_feat, y_feat, a_logits, b_logits
    f, g, loss = whole(True, *args)
    return lax.cond(jnp.isfinite(loss), lambda *_: (f, g, loss), functools.partial(whole, False), *args)


def solution(mesh):
    in_specs = (P("row", "col"), P("col", "row"), P("row"), P("col"))
    out_specs = (P("row"), P("col"), P())
    return jax.shard_map(body, mesh=mesh, in_specs=in_specs, out_specs=out_specs, check_vma=False)
```
